256 devices in a mesh: lon: 64 (over x, z, y_hi), chan: 4 (over y_lo, core).
Axes of the slice: x: 4, y: 4 (y_hi: 2, y_lo: 2; y = y_hi * 2 + y_lo), z: 8, core: 2. Of those that a mesh axis runs over, the one named last changes fastest.
Arguments:
- coarse: bfloat16 [384, 8, 4096], P('chan', None, 'lon'), may hold values from -6 to 6
- up_weight: bfloat16 [4, 4, 384, 192], replicated, may hold values from -0.15625 to 0.15625
- up_bias: float32 [192], replicated, may hold values from -3 to 3
- conv_weight: bfloat16 [3, 3, 192, 192], replicated, may hold values from -0.15625 to 0.15625
- conv_bias: float32 [192], replicated, may hold values from -3 to 3
- cotangent: bfloat16 [192, 16, 8192], P('chan', None, 'lon'), may hold values from -6 to 6
Outputs:
- refined: bfloat16 [192, 16, 8192], P('chan', None, 'lon')
- coarse_grad: bfloat16 [384, 8, 4096], P('chan', None, 'lon')
- up_grad: float32 [4, 4, 384, 192], P(None, None, 'chan')
- conv_grad: float32 [3, 3, 192, 192], P(None, None, None, 'chan')
The draws below stay inside these ranges and needn't reach their ends.
All inputs are finite; a program needn't handle non-finite values.
Results may differ from the reference program's by a relative error of at most 0.0049.
Values may be sent and summed in bfloat16 or wider, within the bound.
A program may use at most 64 MiB of HBM per device.

```python
import jax
import jax.numpy as jnp
from jax import lax

CIN = 384
COUT = 192
H = 8
W = 4096


def level_of(key, dims, cuts, least, high):
    def one(dim, shards_of):
        heights = jax.random.uniform(jax.random.fold_in(jax.random.fold_in(key, 6), dim), (shards_of,), jnp.float32, least / len(cuts), high / len(cuts))
        return jnp.repeat(jnp.exp(heights), dims[dim] // shards_of).reshape((-1,) + (1,) * (len(dims) - dim - 1))

    gain = one(*cuts[0])
    for cut in cuts[1:]:
        gain = gain * one(*cut)
    return gain


def scatter_about(stream_key, shape, spread, bound, pieces=(), dtype=jnp.bfloat16):
    values = jax.random.normal(stream_key, shape, jnp.float32) * spread
    if len(pieces) > 0:
        values = level_of(stream_key, shape, pieces, -0.22, 0.18) * values
    return jnp.clip(values, min=-bound, max=bound).astype(dtype)


def setup_inputs(seed: int = 0) -> dict:
    streams_of = jax.random.split(jax.random.key(seed), 7)
    coarse = scatter_about(streams_of[0], (CIN, H, W), 1.0, 6.0, ((0, 4), (2, 64)))
    up_weight = scatter_about(streams_of[1], (4, 4, CIN, COUT), (4 * CIN) ** -0.5, 0.15625)
    up_bias = scatter_about(streams_of[2], (COUT,), 0.5, 3.0, (), jnp.float32)
    conv_weight = scatter_about(streams_of[3], (3, 3, COUT, COUT), (9 * COUT) ** -0.5, 0.15625)
    conv_bias = scatter_about(streams_of[4], (COUT,), 0.5, 3.0, (), jnp.float32)
    cotangent = scatter_about(streams_of[5], (COUT, 2 * H, 2 * W), 1.0, 6.0, ((0, 4), (2, 64)))
    return dict(coarse=coarse, up_weight=up_weight, up_bias=up_bias, conv_weight=conv_weight, conv_bias=conv_bias, cotangent=cotangent)


TAPS = (((1, 0), (3, -1)), ((0, 1), (2, 0)))

def wrap_pad(field):
    beside_all = jnp.concatenate([field[:, :, -1:], field, field[:, :, :1]], 2)
    return jnp.pad(beside_all, ((0, 0), (1, 1), (0, 0)))

def transposed_taps(padded, weight):
    rows = padded.shape[1] - 2
    cols = padded.shape[2] - 2
    parities = []
    for row_par in range(2):
        pair = []
        for col_par in range(2):
            total = None
            for tap_y, row_off in TAPS[row_par]:
                for tap_x, col_off in TAPS[col_par]:
                    window = padded[:, 1 + row_off:1 + row_off + rows, 1 + col_off:1 + col_off + cols]
                    term = jnp.einsum('chw,co->ohw', window, weight[tap_y, tap_x], preferred_element_type=jnp.float32)
                    total = term if total is None else total + term
            pair.append(total)
        parities.append(jnp.stack(pair, -1))
    stacked = jnp.stack(parities, 2)
    return stacked.reshape(stacked.shape[0], 2 * rows, 2 * cols)

def cross_taps(padded, weight):
    rows = padded.shape[1] - 2
    cols = padded.shape[2] - 2
    total = None
    for tap_y in range(3):
        for tap_x in range(3):
            window = padded[:, tap_y:tap_y + rows, tap_x:tap_x + cols]
            term = jnp.einsum('chw,co->ohw', window, weight[tap_y, tap_x], preferred_element_type=jnp.float32)
            total = term if total is None else total + term
    return total

def cross_adjoint(padded, weight):
    rows = padded.shape[1] - 2
    cols = padded.shape[2] - 2
    total = None
    for tap_y in range(3):
        for tap_x in range(3):
            window = padded[:, 2 - tap_y:2 - tap_y + rows, 2 - tap_x:2 - tap_x + cols]
            term = jnp.einsum('ohw,co->chw', window, weight[tap_y, tap_x], preferred_element_type=jnp.float32)
            total = term if total is None else total + term
    return total

def cross_weight_grad(padded, grad):
    rows = padded.shape[1] - 2
    cols = padded.shape[2] - 2
    outer = []
    for tap_y in range(3):
        inner = []
        for tap_x in range(3):
            window = padded[:, tap_y:tap_y + rows, tap_x:tap_x + cols]
            inner.append(jnp.einsum('chw,ohw->co', window, grad, preferred_element_type=jnp.float32))
        outer.append(jnp.stack(inner, 0))
    return jnp.stack(outer, 0)

def parity_view(padded, tap_y, tap_x):
    rows = (padded.shape[1] - 2) // 2
    cols = (padded.shape[2] - 2) // 2
    split = padded.reshape(padded.shape[0], rows + 1, 2, cols + 1, 2)
    return split[:, tap_y // 2:tap_y // 2 + rows, tap_y % 2, tap_x // 2:tap_x // 2 + cols, tap_x % 2]

def transposed_weight_grad(coarse, padded_delta):
    outer = []
    for tap_y in range(4):
        inner = []
        for tap_x in range(4):
            view = parity_view(padded_delta, tap_y, tap_x)
            inner.append(jnp.einsum('chw,ohw->co', coarse, view, preferred_element_type=jnp.float32))
        outer.append(jnp.stack(inner, 0))
    return jnp.stack(outer, 0)

def transposed_adjoint(padded_delta, weight):
    total = None
    for tap_y in range(4):
        for tap_x in range(4):
            view = parity_view(padded_delta, tap_y, tap_x)
            term = jnp.einsum('ohw,co->chw', view, weight[tap_y, tap_x], preferred_element_type=jnp.float32)
            total = term if total is None else total + term
    return total

def reference(coarse, up_weight, up_bias, conv_weight, conv_bias, cotangent):
    coarse_wide = coarse.astype(jnp.float32)
    up_wide = up_weight.astype(jnp.float32)
    conv_wide = conv_weight.astype(jnp.float32)
    grad_wide = cotangent.astype(jnp.float32)
    pre_act = transposed_taps(wrap_pad(coarse_wide), up_wide) + up_bias.astype(jnp.float32)[:, None, None]
    sigma = jax.nn.sigmoid(pre_act)
    hidden = lax.optimization_barrier((pre_act * sigma).astype(jnp.bfloat16)).astype(jnp.float32)
    hidden_pad = wrap_pad(hidden)
    refined = (cross_taps(hidden_pad, conv_wide) + conv_bias.astype(jnp.float32)[:, None, None]).astype(jnp.bfloat16)
    hidden_grad = cross_adjoint(wrap_pad(grad_wide), conv_wide)
    conv_grad = cross_weight_grad(hidden_pad, grad_wide)
    delta = lax.optimization_barrier((hidden_grad * sigma * (1.0 + pre_act * (1.0 - sigma))).astype(jnp.bfloat16)).astype(jnp.float32)
    delta_pad = wrap_pad(delta)
    up_grad = transposed_weight_grad(coarse_wide, delta_pad)
    coarse_grad = transposed_adjoint(delta_pad, up_wide).astype(jnp.bfloat16)
    return (refined, coarse_grad, up_grad, conv_grad)
```

```python
import functools

import jax
import jax.numpy as jnp
from jax import lax
from jax.experimental import pallas as pl
from jax.experimental.pallas import tpu as pltpu
from jax.sharding import PartitionSpec as P

MESH = pl.DeviceIdType.MESH
F32, BF16 = jnp.float32, jnp.bfloat16
VM = pl.BlockSpec(memory_space=pltpu.VMEM)
CIN, COUT, H, WC = 384, 192, 8, 64
OWN_IN, OWN_OUT = CIN // 4, COUT // 4
POS, FINE = H * WC, 4 * H * WC
ROWS = 3072
LIMIT = 60 << 20


def nn(a, b):
    return jnp.dot(a, b, preferred_element_type=F32)


def nt(a, b):
    return lax.dot_general(a, b, (((1,), (1,)), ((), ())), preferred_element_type=F32)


def down(v):
    row = lax.broadcasted_iota(jnp.int32, v.shape, v.ndim - 2)
    return jnp.where(row == 0, 0.0, pltpu.roll(v, 1, v.ndim - 2))


def up(v):
    row = lax.broadcasted_iota(jnp.int32, v.shape, v.ndim - 2)
    return jnp.where(row == H - 1, 0.0, pltpu.roll(v, H - 1, v.ndim - 2))


PIECES = 4


def gather_kernel(coarse, cot, edge, c_all, g_all, e_all, cs, cr, gs, gr, es, er):
    lon, rank = lax.axis_index("lon"), lax.axis_index("chan")
    n_lon = lax.axis_size("lon")
    far, core = rank // 2, lax.rem(rank, 2)
    sib, cross = far * 2 + 1 - core, (1 - far) * 2 + core
    diag = (1 - far) * 2 + 1 - core
    sides = (lax.rem(lon + 1, n_lon), lax.rem(lon + n_lon - 1, n_lon))

    barrier = pltpu.get_barrier_semaphore()
    for d in range(1, 4):
        pl.semaphore_signal(barrier, inc=1, device_id=(lon, lax.rem(rank + d, 4)), device_id_type=MESH)
    for side in sides:
        for d in range(4):
            pl.semaphore_signal(barrier, inc=1, device_id=(side, lax.rem(rank + d, 4)), device_id_type=MESH)
    pl.semaphore_wait(barrier, 11)

    def c_block(r):
        return c_all.at[pl.ds(pl.multiple_of(r * OWN_IN, 16), OWN_IN), :]

    width = FINE // PIECES

    def g_block(r, k):
        return g_all.at[pl.ds(pl.multiple_of(r * OWN_OUT, 16), OWN_OUT), pl.ds(k * width, width)]

    def send(src, dst, s, r, to):
        copy = pltpu.make_async_remote_copy(
            src_ref=src, dst_ref=dst, send_sem=s, recv_sem=r, device_id=to, device_id_type=MESH
        )
        copy.start()
        return copy

    out = []
    c_cross = send(coarse, c_block(rank), cs.at[0], cr.at[0], (lon, cross))
    c_sib = send(coarse, c_block(rank), cs.at[1], cr.at[1], (lon, sib))
    e_copies = []
    for n, side in enumerate(sides):
        for d in range(4):
            to = lax.rem(rank + d, 4)
            dst = e_all.at[n, pl.ds(pl.multiple_of(rank * OWN_OUT, 16), OWN_OUT), :]
            e_copies.append(send(edge, dst, es.at[n, d], er.at[n, d], (side, to)))
    g_cross, g_sib = [], []
    for k in range(PIECES):
        src = cot.at[:, pl.ds(k * width, width)]
        g_cross.append(send(src, g_block(rank, k), gs.at[0, k], gr.at[0, k], (lon, cross)))
        g_sib.append(send(src, g_block(rank, k), gs.at[1, k], gr.at[1, k], (lon, sib)))
    c_all[pl.ds(pl.multiple_of(rank * OWN_IN, 16), OWN_IN), :] = coarse[...]
    g_all[pl.ds(pl.multiple_of(rank * OWN_OUT, 16), OWN_OUT), :] = cot[...]

    def arrival(dst, r):
        return pltpu.make_async_remote_copy(
            src_ref=dst, dst_ref=dst, send_sem=r, recv_sem=r, device_id=(lon, sib), device_id_type=MESH
        )

    arrival(c_block(cross), cr.at[0]).wait_recv()
    out.append(send(c_block(cross), c_block(cross), cs.at[2], cr.at[2], (lon, sib)))
    for k in range(PIECES):
        arrival(g_block(cross, k), gr.at[0, k]).wait_recv()
        out.append(send(g_block(cross, k), g_block(cross, k), gs.at[2, k], gr.at[2, k], (lon, sib)))
    arrival(c_block(sib), cr.at[1]).wait_recv()
    arrival(c_block(diag), cr.at[2]).wait_recv()
    for k in range(PIECES):
        arrival(g_block(sib, k), gr.at[1, k]).wait_recv()
        arrival(g_block(diag, k), gr.at[2, k]).wait_recv()
    for n in range(2):
        for d in range(4):
            origin = lax.rem(rank + 4 - d, 4)
            dst = e_all.at[n, pl.ds(pl.multiple_of(origin * OWN_OUT, 16), OWN_OUT), :]
            arrival(dst, er.at[n, d]).wait_recv()
    for copy in [c_cross, c_sib] + e_copies + g_cross + g_sib + out:
        copy.wait_send()


def gather(coarse, cot, edge):
    dma = pltpu.SemaphoreType.DMA
    return pl.pallas_call(
        gather_kernel,
        out_shape=(
            jax.ShapeDtypeStruct((CIN, POS), BF16),
            jax.ShapeDtypeStruct((COUT, FINE), BF16),
            jax.ShapeDtypeStruct((2, COUT, 128), BF16),
        ),
        in_specs=[VM] * 3,
        out_specs=[VM] * 3,
        scratch_shapes=[
            dma((3,)), dma((3,)), dma((3, PIECES)), dma((3, PIECES)), dma((2, 4)), dma((2, 4)),
        ],
        compiler_params=pltpu.CompilerParams(collective_id=0, has_side_effects=True),
        name="gather",
    )(coarse, cot, edge)


def compute_kernel(rank_ref, c_all, g_all, e_all, coarse, cot, up_w, up_b, conv_w, conv_b,
                   refined, c_grad, packed, xf, xl, pre, fs, hid, cots, df):
    rank = rank_ref[0]

    for b in range(4):
        xf[pl.ds(1 + 16 * b, 16)] = c_all[:, pl.ds(128 * b, 128)].astype(F32).T.reshape(16, H, CIN)
    left, right = e_all[0].astype(F32).T, e_all[1].astype(F32).T
    src = lax.broadcasted_iota(jnp.int32, (COUT, CIN), 0)
    dst = lax.broadcasted_iota(jnp.int32, (COUT, CIN), 1)
    place = src // OWN_OUT * OWN_IN + lax.rem(src, OWN_OUT)
    spread = [(dst == place + OWN_OUT * h).astype(F32).astype(BF16) for h in range(2)]

    def widen(pair):
        return nn(pair[:16].astype(BF16), spread[0]) + nn(pair[16:].astype(BF16), spread[1])

    xf[0] = widen(left[96:128])[8:]
    xf[65] = widen(right[32:64])[:8]
    xf[66:68] = jnp.zeros((2, H, CIN), F32)

    @pl.loop(0, 3)
    def _(n):
        t0 = n * 22
        rows = pl.ds(pl.multiple_of(t0 * H, 16), 22 * H)
        for d in range(2):
            v = xf[pl.ds(t0 + 1 - d, 22)]
            for s, w in enumerate((down(v), v, up(v))):
                xl[rows, pl.ds((2 * s + d) * CIN, CIN)] = w.reshape(22 * H, CIN).astype(BF16)

    for rp in range(2):
        for cp in range(2):
            taps = ((3, 1), (2, 0))[rp]
            w = jnp.concatenate([up_w[ky, cp + 2 * d] for ky in taps for d in range(2)], 0)
            val = nn(xl[:, pl.ds(rp * 2 * CIN, 4 * CIN)], w)
            pre[:, cp, rp] = val.reshape(66, H, COUT)

    bias = up_b[...].reshape(1, 1, 1, 1, COUT)

    @pl.loop(0, 22)
    def _(n):
        ts = pl.ds(n * 3, 3)
        z = pre[ts] + bias
        s = jax.nn.sigmoid(z)
        fs[ts] = s * (1.0 + z * (1.0 - s))
        h = (z * s).astype(BF16).astype(F32)
        even, odd = h[:, :, 0], h[:, :, 1]
        for m, (a, b) in enumerate(((down(odd), even), (even, odd), (odd, up(even)))):
            both = jnp.concatenate([a, b], 2).astype(BF16)
            hid[m, pl.ds(n * 6, 6)] = both.reshape(6, 16, COUT)

    def put(at, v, n):
        v = v.reshape(n, 2, H, COUT)
        even, odd = v[:, 0], v[:, 1]
        for m, (a, b) in enumerate(((down(odd), even), (even, odd), (odd, up(even)))):
            cots[m, pl.ds(at, n)] = jnp.concatenate([a, b], 1).astype(BF16)

    put(0, left[64:96], 2)
    put(130, right[0:32], 2)
    for b in range(16):
        put(2 + 8 * b, g_all[:, pl.ds(128 * b, 128)].astype(F32).T, 8)

    @pl.loop(0, 5)
    def _(n):
        acc = None
        for ky in range(3):
            for kx in range(3):
                g = cots[2 - ky, pl.ds(n * 26 + 2 - kx, 26)].reshape(416, COUT)
                term = nt(g, conv_w[ky, kx])
                acc = term if acc is None else acc + term
        ts = pl.ds(n * 13, 13)
        d = (acc.reshape(13, 2, 2, H, COUT) * fs[ts]).astype(BF16).astype(F32)
        for cp in range(2):
            even, odd = d[:, cp, 0], d[:, cp, 1]
            for ky, v in enumerate((down(odd), even, odd, up(even))):
                df[cp, ky, ts] = v

    own = pl.ds(pl.multiple_of(rank * OWN_IN, 16), OWN_IN)
    total = None
    for ky in range(4):
        for pair in range(2):
            ab = []
            for kx in (2 * pair, 2 * pair + 1):
                w = df[kx % 2, ky, pl.ds(kx // 2, 64)].reshape(POS, COUT).astype(BF16)
                ab.append(nn(coarse[...], w))
                term = nt(up_w[ky, kx, own, :], w)
                total = term if total is None else total + term
            a, b = ab
            base = ky * 768 + pair * 288
            packed[pl.ds(base, 96), :] = a[:, :128].astype(BF16)
            packed[pl.ds(base + 96, 96), :] = jnp.concatenate([a[:, 128:], b[:, :64]], 1).astype(BF16)
            packed[pl.ds(base + 192, 96), :] = b[:, 64:].astype(BF16)
    c_grad[...] = total.astype(BF16)

    k_of = lax.broadcasted_iota(jnp.int32, (OWN_OUT, COUT), 0)
    o_of = lax.broadcasted_iota(jnp.int32, (OWN_OUT, COUT), 1)
    pick = (o_of == k_of + OWN_OUT * rank).astype(F32).astype(BF16)
    mine = [nt(pick, conv_w[t // 3, t % 3]).astype(BF16) for t in range(9)]

    for n in range(8):
        acc = None
        for t in range(9):
            term = nt(mine[t], hid[t // 3, pl.ds(16 * n + t % 3, 16)].reshape(256, COUT))
            acc = term if acc is None else acc + term
        refined[:, pl.ds(256 * n, 256)] = (acc + conv_b[...]).astype(BF16)

    def spot(b):
        return pl.ds(b // 4 * 768 + 576 + b % 4 * OWN_OUT, OWN_OUT)

    tails = []
    for t in range(9):
        g = nn(cot[...], hid[t // 3, pl.ds(t % 3, 128)].reshape(FINE, COUT))
        packed[spot(t), :] = g[:, :128].astype(BF16)
        tails.append(g[:, 128:])
    tails.append(jnp.zeros((OWN_OUT, 64), F32))
    for u in range(5):
        packed[spot(9 + u), :] = jnp.concatenate(tails[2 * u:2 * u + 2], 1).astype(BF16)
    for b in (14, 15):
        packed[spot(b), :] = jnp.zeros((OWN_OUT, 128), BF16)


def compute(rank, *args):
    return pl.pallas_call(
        compute_kernel,
        out_shape=(
            jax.ShapeDtypeStruct((OWN_OUT, FINE), BF16),
            jax.ShapeDtypeStruct((OWN_IN, POS), BF16),
            jax.ShapeDtypeStruct((ROWS, 128), BF16),
        ),
        in_specs=[pl.BlockSpec(memory_space=pltpu.SMEM)] + [VM] * 9,
        out_specs=[VM] * 3,
        scratch_shapes=[
            pltpu.VMEM((68, H, CIN), F32),
            pltpu.VMEM((528, 6 * CIN), BF16),
            pltpu.VMEM((66, 2, 2, H, COUT), F32),
            pltpu.VMEM((66, 2, 2, H, COUT), F32),
            pltpu.VMEM((3, 132, 16, COUT), BF16),
            pltpu.VMEM((3, 132, 16, COUT), BF16),
            pltpu.VMEM((2, 4, 66, H, COUT), F32),
        ],
        compiler_params=pltpu.CompilerParams(vmem_limit_bytes=LIMIT),
        name="strip",
    )(rank, *args)


def sum_kernel(dims, src, res, rx, sb, rz, ys, yr,
               x_s, x_r, z_s, z_r, y_sem, az_s, az_r, ax_s, ax_r):
    nx, nz, ny = dims
    size = ROWS // (nx * nz)
    lon, rank = lax.axis_index("lon"), lax.axis_index("chan")
    x, z, y = lon // (nz * ny), lax.rem(lon // ny, nz), lax.rem(lon, ny)

    def dev(px, pz, py):
        return ((px * nz + pz) * ny + py, rank)

    xs = [dev(lax.rem(x + d, nx), z, y) for d in range(1, nx)]
    zs = [dev(x, lax.rem(z + d, nz), y) for d in range(1, nz)]
    ypeer = [dev(x, z, 1 - y)] if ny == 2 else []
    barrier = pltpu.get_barrier_semaphore()
    for peer in xs + zs + ypeer:
        pl.semaphore_signal(barrier, inc=1, device_id=peer, device_id_type=MESH)
    pl.semaphore_wait(barrier, len(xs + zs + ypeer))

    def piece(px, pz):
        return pl.ds(pl.multiple_of((px * nz + pz) * size, 16), size)

    started = []

    def copy_of(a, b, s, r, to):
        return pltpu.make_async_remote_copy(
            src_ref=a, dst_ref=b, send_sem=s, recv_sem=r, device_id=to, device_id_type=MESH
        )

    def send(a, b, s, r, to):
        copy = copy_of(a, b, s, r, to)
        copy.start()
        started.append(copy)

    for k in range(nz):
        zz = lax.rem(z + 1 + k, nz)
        for d in range(1, nx):
            px = lax.rem(x + d, nx)
            send(src.at[piece(px, zz), :], rx.at[d - 1, k], x_s.at[d - 1, k], x_r.at[d - 1, k], xs[d - 1])
    acc = None
    for k in range(nz):
        zz = lax.rem(z + 1 + k, nz)
        acc = src[piece(x, zz), :].astype(F32)
        for d in range(1, nx):
            copy_of(rx.at[d - 1, k], rx.at[d - 1, k], x_s.at[d - 1, k], x_r.at[d - 1, k], xs[0]).wait_recv()
            acc = acc + rx[d - 1, k].astype(F32)
        if k < nz - 1:
            sb[k] = acc.astype(BF16)
            send(sb.at[k], rz.at[k], z_s.at[k], z_r.at[k], zs[k])
    for k in range(nz - 1):
        copy_of(rz.at[k], rz.at[k], z_s.at[k], z_r.at[k], zs[0]).wait_recv()
        acc = acc + rz[k].astype(F32)
    if ny == 2:
        ys[...] = acc
        send(ys, yr, y_sem.at[0], y_sem.at[1], ypeer[0])
        copy_of(yr, yr, y_sem.at[0], y_sem.at[1], ypeer[0]).wait_recv()
        acc = acc + yr[...]
    res[piece(x, z), :] = acc.astype(BF16)
    here = res.at[piece(x, z), :]
    for k in range(1, nz):
        send(here, here, az_s.at[k - 1], az_r.at[k - 1], zs[k - 1])
    for k in range(nz):
        part = res.at[piece(x, lax.rem(z + nz - k, nz)), :]
        if k > 0:
            copy_of(part, part, az_s.at[k - 1], az_r.at[k - 1], zs[0]).wait_recv()
        for d in range(1, nx):
            send(part, part, ax_s.at[d - 1, k], ax_r.at[d - 1, k], xs[d - 1])
    for k in range(nz):
        for d in range(1, nx):
            part = res.at[piece(lax.rem(x + nx - d, nx), lax.rem(z + nz - k, nz)), :]
            copy_of(part, part, ax_s.at[d - 1, k], ax_r.at[d - 1, k], xs[0]).wait_recv()
    for copy in started:
        copy.wait_send()


def sum_lon(dims, packed):
    nx, nz, ny = dims
    size = ROWS // (nx * nz)
    dma = pltpu.SemaphoreType.DMA
    return pl.pallas_call(
        functools.partial(sum_kernel, dims),
        out_shape=jax.ShapeDtypeStruct((ROWS, 128), BF16),
        in_specs=[VM],
        out_specs=VM,
        scratch_shapes=[
            pltpu.VMEM((nx - 1, nz, size, 128), BF16),
            pltpu.VMEM((nz - 1, size, 128), BF16),
            pltpu.VMEM((nz - 1, size, 128), BF16),
            pltpu.VMEM((size, 128), F32),
            pltpu.VMEM((size, 128), F32),
            dma((nx - 1, nz)), dma((nx - 1, nz)), dma((nz - 1,)), dma((nz - 1,)), dma((2,)),
            dma((nz - 1,)), dma((nz - 1,)), dma((nx - 1, nz)), dma((nx - 1, nz)),
        ],
        compiler_params=pltpu.CompilerParams(collective_id=1, has_side_effects=True),
        name="sum_lon",
    )(packed)


def unpack_kernel(src, up_grad, conv_grad):
    for ky in range(4):
        for pair in range(2):
            base = ky * 768 + pair * 288
            a, m, b = [src[pl.ds(base + 96 * n, 96), :].astype(F32) for n in range(3)]
            up_grad[ky, 2 * pair] = jnp.concatenate([a, m[:, :64]], 1)
            up_grad[ky, 2 * pair + 1] = jnp.concatenate([m[:, 64:], b], 1)

    def block(b):
        return src[pl.ds(b // 4 * 768 + 576 + b % 4 * OWN_OUT, OWN_OUT), :].astype(F32)

    for t in range(9):
        tail = block(9 + t // 2)[:, 64 * (t % 2):64 * (t % 2) + 64]
        conv_grad[t // 3, t % 3] = jnp.concatenate([block(t), tail], 1).T


def unpack(sums):
    return pl.pallas_call(
        unpack_kernel,
        out_shape=(
            jax.ShapeDtypeStruct((4, 4, OWN_IN, COUT), F32),
            jax.ShapeDtypeStruct((3, 3, COUT, OWN_OUT), F32),
        ),
        in_specs=[VM],
        out_specs=[VM] * 2,
        compiler_params=pltpu.CompilerParams(vmem_limit_bytes=LIMIT),
        name="unpack",
    )(sums)


def local(dims, coarse, up_weight, up_bias, conv_weight, conv_bias, cotangent):
    rank = lax.axis_index("chan")
    conv_b = lax.dynamic_slice_in_dim(conv_bias, rank * OWN_OUT, OWN_OUT).reshape(OWN_OUT, 1)
    c = coarse.transpose(0, 2, 1).reshape(OWN_IN, POS)
    g = cotangent.reshape(OWN_OUT, H, 2, 2 * WC).transpose(0, 3, 2, 1).reshape(OWN_OUT, FINE)
    edge = jnp.concatenate(
        [g[:, :32], c[:48, :16], c[48:, :16], g[:, -32:], c[:48, -16:], c[48:, -16:]], 1
    )
    c_all, g_all, e_all = gather(c, g, edge)
    ref, cg, packed = compute(
        rank.astype(jnp.int32).reshape(1), c_all, g_all, e_all, c, g,
        up_weight, up_bias.reshape(1, COUT), conv_weight, conv_b,
    )
    up_grad, conv_grad = unpack(sum_lon(dims, packed))
    refined = ref.reshape(OWN_OUT, 2 * WC, 2, H).transpose(0, 3, 2, 1).reshape(OWN_OUT, 2 * H, 2 * WC)
    coarse_grad = cg.reshape(OWN_IN, WC, H).transpose(0, 2, 1)
    return refined, coarse_grad, up_grad, conv_grad


def solution(mesh):
    dims = {64: (4, 8, 2), 8: (2, 2, 2), 4: (2, 2, 1)}[mesh.shape["lon"]]
    placed = (P("chan", None, "lon"), P(), P(), P(), P(), P("chan", None, "lon"))
    return jax.shard_map(
        functools.partial(local, dims),
        mesh=mesh,
        in_specs=placed,
        out_specs=(
            P("chan", None, "lon"),
            P("chan", None, "lon"),
            P(None, None, "chan", None),
            P(None, None, None, "chan"),
        ),
        check_vma=False,
    )
```

```python
import functools

import jax
import jax.numpy as jnp
from jax import lax
from jax.experimental import pallas as pl
from jax.experimental.pallas import tpu as pltpu
from jax.sharding import PartitionSpec as P

MESH = pl.DeviceIdType.MESH
F32, BF16 = jnp.float32, jnp.bfloat16
VM = pl.BlockSpec(memory_space=pltpu.VMEM)
CIN, COUT, H, WC = 384, 192, 8, 64
OWN_IN, OWN_OUT = CIN // 4, COUT // 4
POS, FINE = H * WC, 4 * H * WC
PIECE = 96
LIMIT = 60 << 20


def nn(a, b):
    return jnp.dot(a, b, preferred_element_type=F32)


def nt(a, b):
    return lax.dot_general(a, b, (((1,), (1,)), ((), ())), preferred_element_type=F32)


def down(v):
    row = lax.broadcasted_iota(jnp.int32, v.shape, v.ndim - 2)
    return jnp.where(row == 0, 0.0, pltpu.roll(v, 1, v.ndim - 2))


def up(v):
    row = lax.broadcasted_iota(jnp.int32, v.shape, v.ndim - 2)
    return jnp.where(row == H - 1, 0.0, pltpu.roll(v, H - 1, v.ndim - 2))


PIECES = 4


def shifted(v):
    even, odd = v[:, 0], v[:, 1]
    pairs = ((down(odd), even), (even, odd), (odd, up(even)))
    return [jnp.concatenate(pair, 1).astype(BF16) for pair in pairs]


def kernel(dims, coarse, cot, edge, up_hbm, conv_hbm, up_b, conv_b,
           refined, c_grad, res,
           c_all, g_all, e_all, up_w, conv_w, conv_t, mine, own_up,
           xf, xl, pre, fs, hid, cots, df, part, r_pos, c_pos,
           rx1, kept, sb1, rx2, sb2, rz, ys, yr,
           w_sem, cs, cr, gs, gr, es, er, x1s, x1r, x2s, x2r, zs_s, zs_r, y_sem,
           azs, azr, axs, axr):
    nx, nz, ny = dims
    lon, rank = lax.axis_index("lon"), lax.axis_index("chan")
    n_lon = nx * nz * ny
    x, z, y = lon // (nz * ny), lax.rem(lon // ny, nz), lax.rem(lon, ny)
    far, core = rank // 2, lax.rem(rank, 2)
    sib, cross = far * 2 + 1 - core, (1 - far) * 2 + core
    diag = (1 - far) * 2 + 1 - core
    sides = (lax.rem(lon + 1, n_lon), lax.rem(lon + n_lon - 1, n_lon))
    xa, xb = x + 1 - 2 * lax.rem(x, 2), 3 - x
    xo = lax.rem(x + 2, 4)

    def dev(px, pz, py):
        return ((px * nz + pz) * ny + py, rank)

    def first(zz):
        return xa + lax.rem(zz, 2) * (xb - xa)

    def second(zz):
        return xb + lax.rem(zz, 2) * (xa - xb)

    zpeers = [dev(x, lax.rem(z + d, nz), y) for d in range(1, nz)]
    ypeers = [dev(x, z, 1 - y)] if ny == 2 else []

    loads = [
        pltpu.make_async_copy(up_hbm, up_w, w_sem.at[0]),
        pltpu.make_async_copy(conv_hbm, conv_w, w_sem.at[1]),
    ]
    for load in loads:
        load.start()

    barrier = pltpu.get_barrier_semaphore()
    greet = [(lon, lax.rem(rank + d, 4)) for d in range(1, 4)]
    greet += [(side, lax.rem(rank + d, 4)) for side in sides for d in range(4)]
    greet += [dev(xa, z, y), dev(xb, z, y)] + zpeers + ypeers
    for peer in greet:
        pl.semaphore_signal(barrier, inc=1, device_id=peer, device_id_type=MESH)
    pl.semaphore_wait(barrier, len(greet))

    started = []

    def copy_of(a, b, s, r, to):
        return pltpu.make_async_remote_copy(
            src_ref=a, dst_ref=b, send_sem=s, recv_sem=r, device_id=to, device_id_type=MESH
        )

    def send(a, b, s, r, to):
        copy = copy_of(a, b, s, r, to)
        copy.start()
        started.append(copy)

    def arrived(b, r):
        copy_of(b, b, r, r, (lon, sib)).wait_recv()

    def c_block(r):
        return c_all.at[pl.ds(pl.multiple_of(r * OWN_IN, 16), OWN_IN), :]

    width = FINE // PIECES

    def g_block(r, k):
        return g_all.at[pl.ds(pl.multiple_of(r * OWN_OUT, 16), OWN_OUT), pl.ds(k * width, width)]

    def e_block(n, r):
        return e_all.at[n, pl.ds(pl.multiple_of(r * OWN_OUT, 16), OWN_OUT), :]

    send(coarse, c_block(rank), cs.at[0], cr.at[0], (lon, cross))
    send(coarse, c_block(rank), cs.at[1], cr.at[1], (lon, sib))
    for n, side in enumerate(sides):
        for d in range(4):
            send(edge, e_block(n, rank), es.at[n, d], er.at[n, d], (side, lax.rem(rank + d, 4)))
    for k in range(PIECES):
        own_part = cot.at[:, pl.ds(k * width, width)]
        send(own_part, g_block(rank, k), gs.at[0, k], gr.at[0, k], (lon, cross))
        send(own_part, g_block(rank, k), gs.at[1, k], gr.at[1, k], (lon, sib))
    c_all[pl.ds(pl.multiple_of(rank * OWN_IN, 16), OWN_IN), :] = coarse[...]
    g_all[pl.ds(pl.multiple_of(rank * OWN_OUT, 16), OWN_OUT), :] = cot[...]

    def pass_on(k):
        arrived(g_block(cross, k), gr.at[0, k])
        send(g_block(cross, k), g_block(cross, k), gs.at[2, k], gr.at[2, k], (lon, sib))

    for load in loads:
        load.wait()
    a_of = lax.broadcasted_iota(jnp.int32, (COUT, OWN_OUT), 0)
    b_of = lax.broadcasted_iota(jnp.int32, (COUT, OWN_OUT), 1)
    pick = (a_of == b_of + OWN_OUT * rank).astype(F32).astype(BF16)
    for t in range(9):
        w = conv_w[t // 3, t % 3]
        mine[t] = nn(w, pick).astype(BF16)
        conv_t[t] = w.astype(F32).T.astype(BF16)
    src = lax.broadcasted_iota(jnp.int32, (COUT, CIN), 0)
    dst = lax.broadcasted_iota(jnp.int32, (COUT, CIN), 1)
    place = src // OWN_OUT * OWN_IN + lax.rem(src, OWN_OUT)
    spread = [(dst == place + OWN_OUT * h).astype(F32).astype(BF16) for h in range(2)]

    arrived(c_block(cross), cr.at[0])
    send(c_block(cross), c_block(cross), cs.at[2], cr.at[2], (lon, sib))
    a_of = lax.broadcasted_iota(jnp.int32, (CIN, OWN_IN), 0)
    b_of = lax.broadcasted_iota(jnp.int32, (CIN, OWN_IN), 1)
    pick = (a_of == b_of + OWN_IN * rank).astype(F32).astype(BF16)
    for t in range(16):
        own_up[t] = nn(up_w[t // 4, t % 4], pick).astype(BF16)
    for n in range(2):
        for d in range(4):
            arrived(e_block(n, lax.rem(rank + 4 - d, 4)), er.at[n, d])
    arrived(c_block(sib), cr.at[1])
    arrived(c_block(diag), cr.at[2])
    for b in range(4):
        xf[pl.ds(1 + 16 * b, 16)] = c_all[:, pl.ds(128 * b, 128)].astype(F32).T.reshape(16, H, CIN)
    left, right = e_all[0].astype(F32).T, e_all[1].astype(F32).T

    def widen(pair):
        return nn(pair[:16].astype(BF16), spread[0]) + nn(pair[16:].astype(BF16), spread[1])

    xf[0] = widen(left[96:128])[8:]
    xf[65] = widen(right[32:64])[:8]
    xf[66:68] = jnp.zeros((2, H, CIN), F32)

    @pl.loop(0, 3)
    def _(n):
        t0 = n * 22
        rows = pl.ds(pl.multiple_of(t0 * H, 16), 22 * H)
        for d in range(2):
            v = xf[pl.ds(t0 + 1 - d, 22)]
            for s, w in enumerate((down(v), v, up(v))):
                xl[rows, pl.ds((2 * s + d) * CIN, CIN)] = w.reshape(22 * H, CIN).astype(BF16)

    pass_on(0)
    for rp in range(2):
        for cp in range(2):
            taps = ((3, 1), (2, 0))[rp]
            w = jnp.concatenate([up_w[ky, cp + 2 * d] for ky in taps for d in range(2)], 1)
            val = nt(xl[:, pl.ds(rp * 2 * CIN, 4 * CIN)], w)
            pre[:, cp, rp] = val.reshape(66, H, COUT)
        pass_on(1 + rp)

    bias = up_b[...].reshape(1, 1, 1, 1, COUT)

    @pl.loop(0, 22)
    def _(n):
        ts = pl.ds(n * 3, 3)
        v = pre[ts] + bias
        s = jax.nn.sigmoid(v)
        fs[ts] = s * (1.0 + v * (1.0 - s))
        h = (v * s).astype(BF16).astype(F32).reshape(6, 2, H, COUT)
        for m, w in enumerate(shifted(h)):
            hid[m, pl.ds(n * 6, 6)] = w

    pass_on(3)

    def along_x(chunk, p, which):
        send(part.at[chunk, p], rx1.at[p, which], x1s.at[p, which], x1r.at[p, which],
             dev(first(p), z, y))

    def spot(b):
        return b // 4, 6 + b % 4 // 2, pl.ds(b % 2 * OWN_OUT, OWN_OUT)

    def put(b, v):
        c, p, rows = spot(b)
        part[c, p, rows, :] = v.astype(BF16)

    tails = []
    for t in range(9):
        g = nn(cot[...], hid[t // 3, pl.ds(t % 3, 128)].reshape(FINE, COUT))
        put(t, g[:, :128])
        tails.append(g[:, 128:])
    tails.append(jnp.zeros((OWN_OUT, 64), F32))
    for u in range(5):
        put(9 + u, jnp.concatenate(tails[2 * u:2 * u + 2], 1))
    for b in (14, 15):
        put(b, jnp.zeros((OWN_OUT, 128), F32))
    for p in (6, 7):
        along_x(xo, p, 1)
        along_x(first(p), p, 0)

    for k in range(PIECES):
        arrived(g_block(sib, k), gr.at[1, k])
        arrived(g_block(diag, k), gr.at[2, k])

    def place_cot(at, v, n):
        for m, w in enumerate(shifted(v.reshape(n, 2, H, COUT))):
            cots[m, pl.ds(at, n)] = w

    place_cot(0, left[64:96], 2)
    place_cot(130, right[0:32], 2)
    for b in range(16):
        place_cot(2 + 8 * b, g_all[:, pl.ds(128 * b, 128)].astype(F32).T, 8)

    @pl.loop(0, 5)
    def _(n):
        acc = None
        for ky in range(3):
            for kx in range(3):
                g = cots[2 - ky, pl.ds(n * 26 + 2 - kx, 26)].reshape(416, COUT)
                term = nn(g, conv_t[ky * 3 + kx])
                acc = term if acc is None else acc + term
        ts = pl.ds(n * 13, 13)
        d = (acc.reshape(13, 2, 2, H, COUT) * fs[ts]).astype(BF16).astype(F32)
        for cp in range(2):
            even, odd = d[:, cp, 0], d[:, cp, 1]
            for ky, v in enumerate((down(odd), even, odd, up(even))):
                df[cp, ky, ts] = v

    def window(ky, kx):
        return df[kx % 2, ky, pl.ds(kx // 2, 64)].reshape(POS, COUT).astype(BF16)

    for ky in (xo, xa, xb, x):
        for pair in range(2):
            a, b = [nn(coarse[...], window(ky, kx)) for kx in (2 * pair, 2 * pair + 1)]
            slabs = (a[:, :128], jnp.concatenate([a[:, 128:], b[:, :64]], 1), b[:, 64:])
            for n, slab in enumerate(slabs):
                p = 3 * pair + n
                part[ky, p] = slab.astype(BF16)
                if ky is xo:
                    along_x(xo, p, 1)
                elif ky is (xa, xb)[p % 2]:
                    along_x(ky, p, 0)

    total = None
    for t in range(16):
        term = nn(window(t // 4, t % 4), own_up[t])
        total = term if total is None else total + term
    c_pos[...] = total

    for k in range(nz):
        zz = lax.rem(z + 1 + k, nz)
        q = second(zz)
        for which in range(2):
            arrived(rx1.at[zz, which], x1r.at[zz, which])
        kept[k] = part[x, zz].astype(F32) + rx1[zz, 0].astype(F32)
        sb1[k] = (part[q, zz].astype(F32) + rx1[zz, 1].astype(F32)).astype(BF16)
        send(sb1.at[k], rx2.at[k], x2s.at[k], x2r.at[k], dev(q, z, y))

    def refine(n):
        acc = None
        for t in range(9):
            term = nn(hid[t // 3, pl.ds(16 * n + t % 3, 16)].reshape(256, COUT), mine[t])
            acc = term if acc is None else acc + term
        r_pos[pl.ds(256 * n, 256), :] = acc + conv_b[...]

    for n in range(4):
        refine(n)

    acc = None
    for k in range(nz):
        arrived(rx2.at[k], x2r.at[k])
        acc = kept[k] + rx2[k].astype(F32)
        if k < nz - 1:
            sb2[k] = acc.astype(BF16)
            send(sb2.at[k], rz.at[k], zs_s.at[k], zs_r.at[k], zpeers[k])
    for n in range(4, 8):
        refine(n)
    for k in range(nz - 1):
        arrived(rz.at[k], zs_r.at[k])
        acc = acc + rz[k].astype(F32)
    if ny == 2:
        ys[...] = acc
        send(ys, yr, y_sem.at[0], y_sem.at[1], ypeers[0])
    for r in range(2):
        for i in range(H):
            refined[2 * i + r] = r_pos[pl.ds(8 * r + i, 128, stride=16), :].T.astype(BF16)
    for i in range(H):
        c_grad[i] = c_pos[pl.ds(i, WC, stride=H), :].astype(BF16)
    if ny == 2:
        arrived(yr, y_sem.at[1])
        acc = acc + yr[...]
    res[x, z] = acc.astype(BF16)
    here = res.at[x, z]
    order = [d for k in range(1, nz // 2 + 1) for d in sorted({k, nz - k})]
    for d in order:
        send(here, here, azs.at[d - 1], azr.at[d - 1], zpeers[d - 1])
    for d in [0] + order:
        zz = lax.rem(z + nz - d, nz)
        got = res.at[x, zz]
        if d > 0:
            arrived(got, azr.at[d - 1])
        send(got, got, axs.at[0, zz], axr.at[0, zz], dev(second(zz), z, y))
        send(got, got, axs.at[1, zz], axr.at[1, zz], dev(first(zz), z, y))
    for d in [0] + order:
        zz = lax.rem(z + nz - d, nz)
        got = res.at[second(zz), zz]
        arrived(got, axr.at[0, zz])
        send(got, got, axs.at[2, zz], axr.at[2, zz], dev(first(zz), z, y))
    for d in [0] + order:
        zz = lax.rem(z + nz - d, nz)
        arrived(res.at[first(zz), zz], axr.at[1, zz])
        arrived(res.at[xo, zz], axr.at[2, zz])
    for copy in started:
        copy.wait_send()


def strip(dims, *args):
    nx, nz, ny = dims
    dma = pltpu.SemaphoreType.DMA
    vm = pltpu.VMEM
    any_ = pl.BlockSpec(memory_space=pl.ANY)
    return pl.pallas_call(
        functools.partial(kernel, dims),
        out_shape=(
            jax.ShapeDtypeStruct((2 * H, OWN_OUT, 2 * WC), BF16),
            jax.ShapeDtypeStruct((H, WC, OWN_IN), BF16),
            jax.ShapeDtypeStruct((nx, nz, PIECE, 128), BF16),
        ),
        in_specs=[VM, VM, VM, any_, any_, VM, VM],
        out_specs=[VM] * 3,
        scratch_shapes=[
            vm((CIN, POS), BF16),
            vm((COUT, FINE), BF16),
            vm((2, COUT, 128), BF16),
            vm((4, 4, COUT, CIN), BF16),
            vm((3, 3, COUT, COUT), BF16),
            vm((9, COUT, COUT), BF16),
            vm((9, COUT, OWN_OUT), BF16),
            vm((16, COUT, OWN_IN), BF16),
            vm((68, H, CIN), F32),
            vm((528, 6 * CIN), BF16),
            vm((66, 2, 2, H, COUT), F32),
            vm((66, 2, 2, H, COUT), F32),
            vm((3, 132, 16, COUT), BF16),
            vm((3, 132, 16, COUT), BF16),
            vm((2, 4, 66, H, COUT), F32),
            vm((nx, nz, PIECE, 128), BF16),
            vm((FINE, OWN_OUT), F32),
            vm((POS, OWN_IN), F32),
            vm((nz, 2, PIECE, 128), BF16),
            vm((nz, PIECE, 128), F32),
            vm((nz, PIECE, 128), BF16),
            vm((nz, PIECE, 128), BF16),
            vm((nz - 1, PIECE, 128), BF16),
            vm((nz - 1, PIECE, 128), BF16),
            vm((PIECE, 128), F32),
            vm((PIECE, 128), F32),
            dma((2,)), dma((3,)), dma((3,)), dma((3, PIECES)), dma((3, PIECES)), dma((2, 4)), dma((2, 4)),
            dma((nz, 2)), dma((nz, 2)), dma((nz,)), dma((nz,)), dma((nz - 1,)), dma((nz - 1,)), dma((2,)),
            dma((nz - 1,)), dma((nz - 1,)), dma((3, nz)), dma((3, nz)),
        ],
        compiler_params=pltpu.CompilerParams(
            collective_id=0, has_side_effects=True, vmem_limit_bytes=LIMIT
        ),
        name="strip",
    )(*args)


def unpack_kernel(src, up_grad, conv_grad):
    for ky in range(4):
        for pair in range(2):
            a, m, b = [src[ky, 3 * pair + n].astype(F32) for n in range(3)]
            up_grad[ky, 2 * pair] = jnp.concatenate([a, m[:, :64]], 1)
            up_grad[ky, 2 * pair + 1] = jnp.concatenate([m[:, 64:], b], 1)

    def block(b):
        return src[b // 4, 6 + b % 4 // 2, pl.ds(b % 2 * OWN_OUT, OWN_OUT), :].astype(F32)

    for t in range(9):
        tail = block(9 + t // 2)[:, 64 * (t % 2):64 * (t % 2) + 64]
        conv_grad[t // 3, t % 3] = jnp.concatenate([block(t), tail], 1)


def unpack(sums):
    return pl.pallas_call(
        unpack_kernel,
        out_shape=(
            jax.ShapeDtypeStruct((4, 4, OWN_IN, COUT), F32),
            jax.ShapeDtypeStruct((3, 3, OWN_OUT, COUT), F32),
        ),
        in_specs=[VM],
        out_specs=[VM] * 2,
        compiler_params=pltpu.CompilerParams(vmem_limit_bytes=LIMIT),
        name="unpack",
    )(sums)


def local(dims, coarse, up_weight, up_bias, conv_weight, conv_bias, cotangent):
    rank = lax.axis_index("chan")
    conv_b = lax.dynamic_slice_in_dim(conv_bias, rank * OWN_OUT, OWN_OUT).reshape(1, OWN_OUT)
    c = coarse.transpose(0, 2, 1).reshape(OWN_IN, POS)
    g = cotangent.reshape(OWN_OUT, H, 2, 2 * WC).transpose(0, 3, 2, 1).reshape(OWN_OUT, FINE)
    edge = jnp.concatenate(
        [g[:, :32], c[:48, :16], c[48:, :16], g[:, -32:], c[:48, -16:], c[48:, -16:]], 1
    )
    refined, c_grad, sums = strip(
        dims, c, g, edge, up_weight.transpose(0, 1, 3, 2), conv_weight, up_bias.reshape(1, COUT), conv_b
    )
    up_grad, conv_grad = unpack(sums)
    return refined.transpose(1, 0, 2), c_grad.transpose(2, 0, 1), up_grad, conv_grad.transpose(0, 1, 3, 2)


def solution(mesh):
    dims = {64: (4, 8, 2), 8: (4, 2, 1)}[mesh.shape["lon"]]
    placed = (P("chan", None, "lon"), P(), P(), P(), P(), P("chan", None, "lon"))
    return jax.shard_map(
        functools.partial(local, dims),
        mesh=mesh,
        in_specs=placed,
        out_specs=(
            P("chan", None, "lon"),
            P("chan", None, "lon"),
            P(None, None, "chan", None),
            P(None, None, None, "chan"),
        ),
        check_vma=False,
    )
```

```python
import functools

import jax
import jax.numpy as jnp
from jax import lax
from jax.experimental import pallas as pl
from jax.experimental.pallas import tpu as pltpu
from jax.sharding import PartitionSpec as P

MESH = pl.DeviceIdType.MESH
F32, BF16 = jnp.float32, jnp.bfloat16
VM = pl.BlockSpec(memory_space=pltpu.VMEM)
CIN, COUT, H, WC = 384, 192, 8, 64
OWN_IN, OWN_OUT = CIN // 4, COUT // 4
POS, FINE = H * WC, 4 * H * WC
PIECE = 96
LIMIT = 60 << 20


def nn(a, b):
    return jnp.dot(a, b, preferred_element_type=F32)


def nt(a, b):
    return lax.dot_general(a, b, (((1,), (1,)), ((), ())), preferred_element_type=F32)


def down(v):
    row = lax.broadcasted_iota(jnp.int32, v.shape, v.ndim - 2)
    return jnp.where(row == 0, 0.0, pltpu.roll(v, 1, v.ndim - 2))


def up(v):
    row = lax.broadcasted_iota(jnp.int32, v.shape, v.ndim - 2)
    return jnp.where(row == H - 1, 0.0, pltpu.roll(v, H - 1, v.ndim - 2))


PIECES = 4


def shifted(v):
    even, odd = v[:, 0], v[:, 1]
    pairs = ((down(odd), even), (even, odd), (odd, up(even)))
    return [jnp.concatenate(pair, 1).astype(BF16) for pair in pairs]


def kernel(dims, coarse_hbm, cot_hbm, up_hbm, conv_hbm, up_b, conv_b,
           refined, c_grad, res,
           coarse_in, cot_in, coarse, cot, edge, g32, c_all, g_all, e_all, up_w, conv_w, conv_t, mine, own_up,
           xf, xl, pre, fs, hid, cots, df, part, r_pos, c_pos,
           rx1, kept, sb1, rx2, sb2, rz,
           w_sem, cs, cr, gs, gr, es, er, x1s, x1r, x2s, x2r, zs_s, zs_r,
           azs, azr, axs, axr):
    nx, nz, ny = dims
    lon, rank = lax.axis_index("lon"), lax.axis_index("chan")
    n_lon = nx * nz * ny
    x, z, y = lon // (nz * ny), lax.rem(lon // ny, nz), lax.rem(lon, ny)
    far, core = rank // 2, lax.rem(rank, 2)
    sib, cross = far * 2 + 1 - core, (1 - far) * 2 + core
    diag = (1 - far) * 2 + 1 - core
    sides = (lax.rem(lon + 1, n_lon), lax.rem(lon + n_lon - 1, n_lon))
    xa, xb = x + 1 - 2 * lax.rem(x, 2), 3 - x
    xo = lax.rem(x + 2, 4)

    def dev(px, pz, py):
        return ((px * nz + pz) * ny + py, rank)

    def first(zz):
        return xa + lax.rem(zz, 2) * (xb - xa)

    def second(zz):
        return xb + lax.rem(zz, 2) * (xa - xb)

    links = sorted(
        [(d, f) for d in range(nz) for f in range(ny)], key=lambda v: min(v[0], nz - v[0]) + 2 * v[1]
    )
    zy = {(d, f): dev(x, lax.rem(z + d, nz), lax.rem(y + f, ny)) for d, f in links}

    def slot(d, f):
        return ny * d + f

    loads = [
        pltpu.make_async_copy(coarse_hbm, coarse_in, w_sem.at[0]),
        pltpu.make_async_copy(cot_hbm, cot_in, w_sem.at[1]),
        pltpu.make_async_copy(up_hbm, up_w, w_sem.at[2]),
        pltpu.make_async_copy(conv_hbm, conv_w, w_sem.at[3]),
    ]
    for load in loads:
        load.start()

    barrier = pltpu.get_barrier_semaphore()
    greet = [(lon, lax.rem(rank + d, 4)) for d in range(1, 4)]
    greet += [(side, lax.rem(rank + d, 4)) for side in sides for d in range(4)]
    greet += [dev(xa, z, y), dev(xb, z, y), dev(xo, z, y)] + [zy[v] for v in links[1:]]
    for peer in greet:
        pl.semaphore_signal(barrier, inc=1, device_id=peer, device_id_type=MESH)

    loads[0].wait()
    for i in range(H):
        c_pos[pl.ds(i, WC, stride=H), :] = coarse_in[i].astype(F32)
    for n in range(4):
        coarse[:, pl.ds(128 * n, 128)] = c_pos[pl.ds(128 * n, 128), :].T.astype(BF16)
    loads[1].wait()
    g32[...] = cot_in[...].astype(F32).reshape(OWN_OUT * 16, 128)
    for r in range(2):
        for i in range(H):
            r_pos[pl.ds(8 * r + i, 128, stride=16), :] = g32[pl.ds(2 * i + r, OWN_OUT, stride=16), :].T
    for n in range(16):
        cot[:, pl.ds(128 * n, 128)] = r_pos[pl.ds(128 * n, 128), :].T.astype(BF16)
    ends = []
    for c0, g0 in ((0, 0), (POS - 16, FINE - 32)):
        c_end = coarse[:, pl.ds(c0, 16)].astype(F32)
        ends += [cot[:, pl.ds(g0, 32)].astype(F32), c_end[:OWN_OUT], c_end[OWN_OUT:]]
    edge[...] = jnp.concatenate(ends, 1).astype(BF16)
    pad = jnp.zeros((132, 16, 64), BF16)
    for m in range(3):
        cots[:, :, pl.ds(256 * m + COUT, 64)] = pad
    conv_t[...] = jnp.zeros(conv_t.shape, BF16)
    pl.semaphore_wait(barrier, len(greet))

    started = []

    def copy_of(a, b, s, r, to):
        return pltpu.make_async_remote_copy(
            src_ref=a, dst_ref=b, send_sem=s, recv_sem=r, device_id=to, device_id_type=MESH
        )

    def send(a, b, s, r, to):
        copy = copy_of(a, b, s, r, to)
        copy.start()
        started.append(copy)

    def arrived(b, r):
        copy_of(b, b, r, r, (lon, sib)).wait_recv()

    def c_block(r):
        return c_all.at[pl.ds(pl.multiple_of(r * OWN_IN, 16), OWN_IN), :]

    width = FINE // PIECES

    def g_block(r, k):
        return g_all.at[pl.ds(pl.multiple_of(r * OWN_OUT, 16), OWN_OUT), pl.ds(k * width, width)]

    def e_block(n, r):
        return e_all.at[n, pl.ds(pl.multiple_of(r * OWN_OUT, 16), OWN_OUT), :]

    send(coarse, c_block(rank), cs.at[0], cr.at[0], (lon, cross))
    send(coarse, c_block(rank), cs.at[1], cr.at[1], (lon, sib))
    for n, side in enumerate(sides):
        for d in range(4):
            send(edge, e_block(n, rank), es.at[n, d], er.at[n, d], (side, lax.rem(rank + d, 4)))
    for k in range(PIECES):
        own_part = cot.at[:, pl.ds(k * width, width)]
        send(own_part, g_block(rank, k), gs.at[0, k], gr.at[0, k], (lon, cross))
        send(own_part, g_block(rank, k), gs.at[1, k], gr.at[1, k], (lon, sib))
    c_all[pl.ds(pl.multiple_of(rank * OWN_IN, 16), OWN_IN), :] = coarse[...]
    g_all[pl.ds(pl.multiple_of(rank * OWN_OUT, 16), OWN_OUT), :] = cot[...]

    def pass_on(k):
        arrived(g_block(cross, k), gr.at[0, k])
        send(g_block(cross, k), g_block(cross, k), gs.at[2, k], gr.at[2, k], (lon, sib))

    for load in loads[2:]:
        load.wait()
    own_bias = jnp.zeros((1, OWN_OUT), F32)
    for r in range(4):
        own_bias += jnp.where(rank == r, conv_b[:, pl.ds(OWN_OUT * r, OWN_OUT)], 0.0)
    a_of = lax.broadcasted_iota(jnp.int32, (COUT, OWN_OUT), 0)
    b_of = lax.broadcasted_iota(jnp.int32, (COUT, OWN_OUT), 1)
    pick = (a_of == b_of + OWN_OUT * rank).astype(F32).astype(BF16)
    for t in range(9):
        w = conv_w[t // 3, t % 3]
        mine[t] = nn(w, pick).astype(BF16)
        conv_t[pl.ds(768 * (t % 3) + 256 * (2 - t // 3), COUT), :] = w.astype(F32).T.astype(BF16)
    src = lax.broadcasted_iota(jnp.int32, (COUT, CIN), 0)
    dst = lax.broadcasted_iota(jnp.int32, (COUT, CIN), 1)
    place = src // OWN_OUT * OWN_IN + lax.rem(src, OWN_OUT)
    spread = [(dst == place + OWN_OUT * h).astype(F32).astype(BF16) for h in range(2)]

    arrived(c_block(cross), cr.at[0])
    send(c_block(cross), c_block(cross), cs.at[2], cr.at[2], (lon, sib))
    a_of = lax.broadcasted_iota(jnp.int32, (CIN, OWN_IN), 0)
    b_of = lax.broadcasted_iota(jnp.int32, (CIN, OWN_IN), 1)
    pick = (a_of == b_of + OWN_IN * rank).astype(F32).astype(BF16)
    for t in range(16):
        own_up[t] = nn(up_w[t // 4, t % 4], pick).astype(BF16)
    for n in range(2):
        for d in range(4):
            arrived(e_block(n, lax.rem(rank + 4 - d, 4)), er.at[n, d])
    arrived(c_block(sib), cr.at[1])
    arrived(c_block(diag), cr.at[2])
    for b in range(4):
        xf[pl.ds(1 + 16 * b, 16)] = c_all[:, pl.ds(128 * b, 128)].astype(F32).T.reshape(16, H, CIN)
    left, right = e_all[0].astype(F32).T, e_all[1].astype(F32).T

    def widen(pair):
        return nn(pair[:16].astype(BF16), spread[0]) + nn(pair[16:].astype(BF16), spread[1])

    xf[0] = widen(left[96:128])[8:]
    xf[65] = widen(right[32:64])[:8]
    xf[66:68] = jnp.zeros((2, H, CIN), F32)

    @pl.loop(0, 3)
    def _(n):
        t0 = n * 22
        rows = pl.ds(pl.multiple_of(t0 * H, 16), 22 * H)
        for d in range(2):
            v = xf[pl.ds(t0 + 1 - d, 22)]
            for s, w in enumerate((down(v), v, up(v))):
                xl[rows, pl.ds((2 * s + d) * CIN, CIN)] = w.reshape(22 * H, CIN).astype(BF16)

    pass_on(0)
    for rp in range(2):
        for cp in range(2):
            taps = ((3, 1), (2, 0))[rp]
            w = jnp.concatenate([up_w[ky, cp + 2 * d] for ky in taps for d in range(2)], 1)
            val = nt(xl[:, pl.ds(rp * 2 * CIN, 4 * CIN)], w)
            pre[:, cp, rp] = val.reshape(66, H, COUT)
        pass_on(1 + rp)

    bias = up_b[...].reshape(1, 1, 1, 1, COUT)

    @pl.loop(0, 22)
    def _(n):
        ts = pl.ds(n * 3, 3)
        v = pre[ts] + bias
        s = jax.nn.sigmoid(v)
        fs[ts] = s * (1.0 + v * (1.0 - s))
        h = (v * s).astype(BF16).astype(F32).reshape(6, 2, H, COUT)
        for m, w in enumerate(shifted(h)):
            hid[m, pl.ds(n * 6, 6)] = w

    pass_on(3)

    def along_x(chunk, p, which):
        send(part.at[chunk, p], rx1.at[p, which], x1s.at[p, which], x1r.at[p, which],
             dev(first(p), z, y))

    def spot(b):
        return b // 4, 6 + b % 4 // 2, pl.ds(b % 2 * OWN_OUT, OWN_OUT)

    def put(b, v):
        c, p, rows = spot(b)
        part[c, p, rows, :] = v.astype(BF16)

    tails = []
    for t in range(9):
        g = nn(cot[...], hid[t // 3, pl.ds(t % 3, 128)].reshape(FINE, COUT))
        put(t, g[:, :128])
        tails.append(g[:, 128:])
    tails.append(jnp.zeros((OWN_OUT, 64), F32))
    for u in range(5):
        put(9 + u, jnp.concatenate(tails[2 * u:2 * u + 2], 1))
    for b in (14, 15):
        put(b, jnp.zeros((OWN_OUT, 128), F32))
    for p in (6, 7):
        along_x(xo, p, 1)
        along_x(first(p), p, 0)

    for k in range(PIECES):
        arrived(g_block(sib, k), gr.at[1, k])
        arrived(g_block(diag, k), gr.at[2, k])

    def place_cot(at, v, n):
        for m, w in enumerate(shifted(v.reshape(n, 2, H, COUT))):
            cots[pl.ds(at, n), :, pl.ds(256 * m, COUT)] = w

    place_cot(0, left[64:96], 2)
    place_cot(130, right[0:32], 2)
    for b in range(16):
        place_cot(2 + 8 * b, g_all[:, pl.ds(128 * b, 128)].astype(F32).T, 8)

    @pl.loop(0, 5)
    def _(n):
        g = [cots[pl.ds(n * 26 + 2 - kx, 26)].reshape(416, 768) for kx in range(3)]
        acc = nn(jnp.concatenate(g, 1), conv_t[...])
        ts = pl.ds(n * 13, 13)
        d = (acc.reshape(13, 2, 2, H, COUT) * fs[ts]).astype(BF16).astype(F32)
        for cp in range(2):
            even, odd = d[:, cp, 0], d[:, cp, 1]
            for ky, v in enumerate((down(odd), even, odd, up(even))):
                df[cp, ky, ts] = v

    def window(ky, kx):
        return df[kx % 2, ky, pl.ds(kx // 2, 64)].reshape(POS, COUT).astype(BF16)

    for ky in (xo, xa, xb, x):
        for pair in range(2):
            a, b = [nn(coarse[...], window(ky, kx)) for kx in (2 * pair, 2 * pair + 1)]
            slabs = (a[:, :128], jnp.concatenate([a[:, 128:], b[:, :64]], 1), b[:, 64:])
            for n, slab in enumerate(slabs):
                p = 3 * pair + n
                part[ky, p] = slab.astype(BF16)
                if ky is xo:
                    along_x(xo, p, 1)
                elif ky is (xa, xb)[p % 2]:
                    along_x(ky, p, 0)

    total = None
    for t in range(16):
        term = nn(window(t // 4, t % 4), own_up[t])
        total = term if total is None else total + term
    c_pos[...] = total

    far_first = sorted(range(nz), key=lambda d: -min(d, nz - d))
    for d in far_first:
        zz = lax.rem(z + d, nz)
        q = second(zz)
        for which in range(2):
            arrived(rx1.at[zz, which], x1r.at[zz, which])
        kept[d] = part[x, zz].astype(F32) + rx1[zz, 0].astype(F32)
        sb1[d] = (part[q, zz].astype(F32) + rx1[zz, 1].astype(F32)).astype(BF16)
        send(sb1.at[d], rx2.at[d], x2s.at[d], x2r.at[d], dev(q, z, y))

    def refine(n):
        acc = None
        for t in range(9):
            term = nn(hid[t // 3, pl.ds(16 * n + t % 3, 16)].reshape(256, COUT), mine[t])
            acc = term if acc is None else acc + term
        r_pos[pl.ds(256 * n, 256), :] = acc + own_bias

    for n in range(4):
        refine(n)

    half = PIECE // ny

    def part_of(h):
        return pl.ds(pl.multiple_of(h * half, 16), half)

    for d in far_first:
        arrived(rx2.at[d], x2r.at[d])
        total = kept[d] + rx2[d].astype(F32)
        kept[d] = total
        sb2[d] = total.astype(BF16)
        for f in range(ny - 1, -1, -1):
            if (d, f) != (0, 0):
                h = part_of(lax.rem(y + f, ny))
                send(sb2.at[d, h, :], rz.at[slot(d, f)], zs_s.at[slot(d, f)], zs_r.at[slot(d, f)], zy[d, f])
    for n in range(4, 8):
        refine(n)
    for i in range(H):
        c_grad[i] = c_pos[pl.ds(i, WC, stride=H), :].astype(BF16)
    mine_rows = part_of(y)
    acc = kept[0, mine_rows, :]
    for d, f in links[1:]:
        arrived(rz.at[slot(d, f)], zs_r.at[slot(d, f)])
        acc = acc + rz[slot(d, f)].astype(F32)
    res[x, z, mine_rows, :] = acc.astype(BF16)
    here = res.at[x, z, mine_rows, :]
    for d, f in links[:0:-1]:
        send(here, here, azs.at[slot(d, f)], azr.at[slot(d, f)], zy[d, f])

    for r in range(2):
        for i in range(H):
            g32[pl.ds(2 * i + r, OWN_OUT, stride=16), :] = r_pos[pl.ds(8 * r + i, 128, stride=16), :].T
    refined[...] = g32[...].reshape(OWN_OUT, 16, 128).astype(BF16)

    def origin(d, f):
        return lax.rem(z + nz - d, nz), part_of(lax.rem(y + f, ny))

    def direct(d):
        return d == nz // 2

    def spread_x(d, f):
        zz, rows = origin(d, f)
        n = slot(d, f)
        got = res.at[x, zz, rows, :]
        if (d, f) != (0, 0):
            arrived(got, azr.at[n])
        if direct(d):
            send(got, got, axs.at[2, n], axr.at[2, n], dev(xo, z, y))
        send(got, got, axs.at[0, n], axr.at[0, n], dev(second(zz), z, y))
        send(got, got, axs.at[1, n], axr.at[1, n], dev(first(zz), z, y))

    def forward_x(d, f):
        zz, rows = origin(d, f)
        n = slot(d, f)
        got = res.at[second(zz), zz, rows, :]
        arrived(got, axr.at[0, n])
        if not direct(d):
            send(got, got, axs.at[2, n], axr.at[2, n], dev(first(zz), z, y))

    lag = 4
    for n in range(len(links) + lag):
        if n < len(links):
            spread_x(*links[n])
        if n >= lag:
            forward_x(*links[n - lag])
    for d, f in links:
        zz, rows = origin(d, f)
        n = slot(d, f)
        arrived(res.at[first(zz), zz, rows, :], axr.at[1, n])
        arrived(res.at[xo, zz, rows, :], axr.at[2, n])
    for copy in started:
        copy.wait_send()


def strip(dims, *args):
    nx, nz, ny = dims
    dma = pltpu.SemaphoreType.DMA
    vm = pltpu.VMEM
    any_ = pl.BlockSpec(memory_space=pl.ANY)
    return pl.pallas_call(
        functools.partial(kernel, dims),
        out_shape=(
            jax.ShapeDtypeStruct((OWN_OUT, 2 * H, 2 * WC), BF16),
            jax.ShapeDtypeStruct((H, WC, OWN_IN), BF16),
            jax.ShapeDtypeStruct((nx, nz, PIECE, 128), BF16),
        ),
        in_specs=[any_] * 4 + [VM] * 2,
        out_specs=[VM] * 3,
        scratch_shapes=[
            vm((H, WC, OWN_IN), BF16),
            vm((OWN_OUT, 2 * H, 2 * WC), BF16),
            vm((OWN_IN, POS), BF16),
            vm((OWN_OUT, FINE), BF16),
            vm((OWN_OUT, 128), BF16),
            vm((OWN_OUT * 2 * H, 2 * WC), F32),
            vm((CIN, POS), BF16),
            vm((COUT, FINE), BF16),
            vm((2, COUT, 128), BF16),
            vm((4, 4, COUT, CIN), BF16),
            vm((3, 3, COUT, COUT), BF16),
            vm((9 * 256, COUT), BF16),
            vm((9, COUT, OWN_OUT), BF16),
            vm((16, COUT, OWN_IN), BF16),
            vm((68, H, CIN), F32),
            vm((528, 6 * CIN), BF16),
            vm((66, 2, 2, H, COUT), F32),
            vm((66, 2, 2, H, COUT), F32),
            vm((3, 132, 16, COUT), BF16),
            vm((132, 16, 3 * 256), BF16),
            vm((2, 4, 66, H, COUT), F32),
            vm((nx, nz, PIECE, 128), BF16),
            vm((FINE, OWN_OUT), F32),
            vm((POS, OWN_IN), F32),
            vm((nz, 2, PIECE, 128), BF16),
            vm((nz, PIECE, 128), F32),
            vm((nz, PIECE, 128), BF16),
            vm((nz, PIECE, 128), BF16),
            vm((nz, PIECE, 128), BF16),
            vm((nz * ny, PIECE // ny, 128), BF16),
            dma((4,)), dma((3,)), dma((3,)), dma((3, PIECES)), dma((3, PIECES)), dma((2, 4)), dma((2, 4)),
            dma((nz, 2)), dma((nz, 2)), dma((nz,)), dma((nz,)), dma((nz * ny,)), dma((nz * ny,)),
            dma((nz * ny,)), dma((nz * ny,)), dma((3, nz * ny)), dma((3, nz * ny)),
        ],
        compiler_params=pltpu.CompilerParams(
            collective_id=0, has_side_effects=True, vmem_limit_bytes=LIMIT
        ),
        name="strip",
    )(*args)


def unpack_kernel(refined, c_grad, sums, refined_out, c_out, up_grad, conv_grad, src, up, conv, sems, out_sems):
    nx = sums.shape[0]
    passes = [
        pltpu.make_async_copy(refined, refined_out, out_sems.at[nx]),
        pltpu.make_async_copy(c_grad, c_out, out_sems.at[nx + 1]),
    ]
    loads = [pltpu.make_async_copy(sums.at[k], src.at[k], sems.at[k]) for k in range(nx)]
    for copy in loads + passes:
        copy.start()
    for ky in range(4):
        loads[ky].wait()
        for pair in range(2):
            a, m, b = [src[ky, 3 * pair + n].astype(F32) for n in range(3)]
            up[ky, 2 * pair] = jnp.concatenate([a, m[:, :64]], 1)
            up[ky, 2 * pair + 1] = jnp.concatenate([m[:, 64:], b], 1)
        copy = pltpu.make_async_copy(up.at[ky], up_grad.at[ky], out_sems.at[ky])
        copy.start()
        passes.append(copy)

    def block(b):
        return src[b // 4, 6 + b % 4 // 2, pl.ds(b % 2 * OWN_OUT, OWN_OUT), :].astype(F32)

    for t in range(9):
        tail = block(9 + t // 2)[:, 64 * (t % 2):64 * (t % 2) + 64]
        conv[t // 3, t % 3] = jnp.concatenate([block(t), tail], 1)
    copy = pltpu.make_async_copy(conv, conv_grad, out_sems.at[nx + 2])
    copy.start()
    for copy in passes + [copy]:
        copy.wait()


def unpack(refined, c_grad, sums):
    any_ = pl.BlockSpec(memory_space=pl.ANY)
    up = (4, 4, OWN_IN, COUT)
    conv = (3, 3, OWN_OUT, COUT)
    return pl.pallas_call(
        unpack_kernel,
        out_shape=(
            jax.ShapeDtypeStruct(refined.shape, BF16),
            jax.ShapeDtypeStruct(c_grad.shape, BF16),
            jax.ShapeDtypeStruct(up, F32),
            jax.ShapeDtypeStruct(conv, F32),
        ),
        in_specs=[any_] * 3,
        out_specs=[any_] * 4,
        scratch_shapes=[
            pltpu.VMEM(sums.shape, BF16),
            pltpu.VMEM(up, F32),
            pltpu.VMEM(conv, F32),
            pltpu.SemaphoreType.DMA((4,)),
            pltpu.SemaphoreType.DMA((7,)),
        ],
        compiler_params=pltpu.CompilerParams(vmem_limit_bytes=LIMIT),
        name="unpack",
    )(refined, c_grad, sums)


def local(dims, coarse, up_weight, up_bias, conv_weight, conv_bias, cotangent):
    refined, c_grad, sums = strip(
        dims, coarse.transpose(1, 2, 0), cotangent, up_weight.transpose(0, 1, 3, 2), conv_weight,
        up_bias.reshape(1, COUT), conv_bias.reshape(1, COUT),
    )
    refined, c_grad, up_grad, conv_grad = unpack(refined, c_grad, sums)
    return refined, c_grad.transpose(2, 0, 1), up_grad, conv_grad.transpose(0, 1, 3, 2)


def solution(mesh):
    dims = (4, 8, 2)
    placed = (P("chan", None, "lon"), P(), P(), P(), P(), P("chan", None, "lon"))
    return jax.shard_map(
        functools.partial(local, dims),
        mesh=mesh,
        in_specs=placed,
        out_specs=(
            P("chan", None, "lon"),
            P("chan", None, "lon"),
            P(None, None, "chan", None),
            P(None, None, None, "chan"),
        ),
        check_vma=False,
    )
```

```python
import functools

import jax
import jax.numpy as jnp
from jax import lax
from jax.experimental import pallas as pl
from jax.experimental.pallas import tpu as pltpu
from jax.sharding import PartitionSpec as P

MESH = pl.DeviceIdType.MESH
F32, BF16 = jnp.float32, jnp.bfloat16
VM = pl.BlockSpec(memory_space=pltpu.VMEM)
CIN, COUT, H, WC = 384, 192, 8, 64
OWN_IN, OWN_OUT = CIN // 4, COUT // 4
POS, FINE = H * WC, 4 * H * WC
PIECE = 96
LIMIT = 60 << 20


def nn(a, b):
    return jnp.dot(a, b, preferred_element_type=F32)


def nt(a, b):
    return lax.dot_general(a, b, (((1,), (1,)), ((), ())), preferred_element_type=F32)


def down(v):
    row = lax.broadcasted_iota(jnp.int32, v.shape, v.ndim - 2)
    return jnp.where(row == 0, 0.0, pltpu.roll(v, 1, v.ndim - 2))


def up(v):
    row = lax.broadcasted_iota(jnp.int32, v.shape, v.ndim - 2)
    return jnp.where(row == H - 1, 0.0, pltpu.roll(v, H - 1, v.ndim - 2))


PIECES = 4


def shifted(v):
    even, odd = v[:, 0], v[:, 1]
    pairs = ((down(odd), even), (even, odd), (odd, up(even)))
    return [jnp.concatenate(pair, 1).astype(BF16) for pair in pairs]


def kernel(dims, coarse_hbm, cot_hbm, up_hbm, conv_hbm, up_b, conv_b,
           refined, c_grad, res,
           coarse_in, cot_in, coarse, cot, edge, g32, c_all, g_all, e_all, up_w, conv_w, conv_t, mine, own_up,
           xf, xl, pre, fs, hid, cots, df, part, r_pos, c_pos,
           rx1, kept, sb1, rx2, sb2, rz, ys, yr,
           w_sem, cs, cr, gs, gr, es, er, x1s, x1r, x2s, x2r, zs_s, zs_r, y_sem,
           azs, azr, axs, axr):
    nx, nz, ny = dims
    lon, rank = lax.axis_index("lon"), lax.axis_index("chan")
    n_lon = nx * nz * ny
    x, z, y = lon // (nz * ny), lax.rem(lon // ny, nz), lax.rem(lon, ny)
    far, core = rank // 2, lax.rem(rank, 2)
    sib, cross = far * 2 + 1 - core, (1 - far) * 2 + core
    diag = (1 - far) * 2 + 1 - core
    sides = (lax.rem(lon + 1, n_lon), lax.rem(lon + n_lon - 1, n_lon))
    xa, xb = x + 1 - 2 * lax.rem(x, 2), 3 - x
    xo = lax.rem(x + 2, 4)

    def dev(px, pz, py):
        return ((px * nz + pz) * ny + py, rank)

    def first(zz):
        return xa + lax.rem(zz, 2) * (xb - xa)

    def second(zz):
        return xb + lax.rem(zz, 2) * (xa - xb)

    near_first = sorted(range(nz), key=lambda d: min(d, nz - d))
    far_first = near_first[::-1]
    zdev = [dev(x, lax.rem(z + d, nz), y) for d in range(nz)]
    ydev = dev(x, z, 1 - y)

    loads = [
        pltpu.make_async_copy(coarse_hbm, coarse_in, w_sem.at[0]),
        pltpu.make_async_copy(cot_hbm, cot_in, w_sem.at[1]),
        pltpu.make_async_copy(up_hbm, up_w, w_sem.at[2]),
        pltpu.make_async_copy(conv_hbm, conv_w, w_sem.at[3]),
    ]
    for load in loads:
        load.start()

    barrier = pltpu.get_barrier_semaphore()
    greet = [zdev[d] for d in far_first[:-1]]
    greet += [(side, lax.rem(rank + d, 4)) for side in sides for d in range(4)]
    greet += [dev(xo, z, y), dev(xa, z, y), dev(xb, z, y)]
    greet += [(lon, lax.rem(rank + d, 4)) for d in range(1, 4)]
    for peer in greet:
        pl.semaphore_signal(barrier, inc=1, device_id=peer, device_id_type=MESH)

    loads[0].wait()
    for i in range(H):
        c_pos[pl.ds(i, WC, stride=H), :] = coarse_in[i].astype(F32)
    for n in range(4):
        coarse[:, pl.ds(128 * n, 128)] = c_pos[pl.ds(128 * n, 128), :].T.astype(BF16)
    pl.semaphore_wait(barrier, len(greet))

    started = []

    def copy_of(a, b, s, r, to):
        return pltpu.make_async_remote_copy(
            src_ref=a, dst_ref=b, send_sem=s, recv_sem=r, device_id=to, device_id_type=MESH
        )

    def send(a, b, s, r, to):
        copy = copy_of(a, b, s, r, to)
        copy.start()
        started.append(copy)

    def arrived(b, r):
        copy_of(b, b, r, r, (lon, sib)).wait_recv()

    def c_block(r):
        return c_all.at[pl.ds(pl.multiple_of(r * OWN_IN, 16), OWN_IN), :]

    width = FINE // PIECES

    def g_block(r, k):
        return g_all.at[pl.ds(pl.multiple_of(r * OWN_OUT, 16), OWN_OUT), pl.ds(k * width, width)]

    def e_block(n, r):
        return e_all.at[n, pl.ds(pl.multiple_of(r * OWN_OUT, 16), OWN_OUT), :]

    send(coarse, c_block(rank), cs.at[0], cr.at[0], (lon, cross))
    send(coarse, c_block(rank), cs.at[1], cr.at[1], (lon, sib))
    loads[1].wait()
    g32[...] = cot_in[...].astype(F32).reshape(OWN_OUT * 16, 128)
    for r in range(2):
        for i in range(H):
            r_pos[pl.ds(8 * r + i, 128, stride=16), :] = g32[pl.ds(2 * i + r, OWN_OUT, stride=16), :].T
    for n in range(16):
        cot[:, pl.ds(128 * n, 128)] = r_pos[pl.ds(128 * n, 128), :].T.astype(BF16)
    ends = []
    for c0, g0 in ((0, 0), (POS - 16, FINE - 32)):
        c_end = coarse[:, pl.ds(c0, 16)].astype(F32)
        ends += [cot[:, pl.ds(g0, 32)].astype(F32), c_end[:OWN_OUT], c_end[OWN_OUT:]]
    edge[...] = jnp.concatenate(ends, 1).astype(BF16)
    for n, side in enumerate(sides):
        for d in range(4):
            send(edge, e_block(n, rank), es.at[n, d], er.at[n, d], (side, lax.rem(rank + d, 4)))
    for k in range(PIECES):
        own_part = cot.at[:, pl.ds(k * width, width)]
        send(own_part, g_block(rank, k), gs.at[0, k], gr.at[0, k], (lon, cross))
        send(own_part, g_block(rank, k), gs.at[1, k], gr.at[1, k], (lon, sib))
    c_all[pl.ds(pl.multiple_of(rank * OWN_IN, 16), OWN_IN), :] = coarse[...]
    g_all[pl.ds(pl.multiple_of(rank * OWN_OUT, 16), OWN_OUT), :] = cot[...]

    def pass_on(k):
        arrived(g_block(cross, k), gr.at[0, k])
        send(g_block(cross, k), g_block(cross, k), gs.at[2, k], gr.at[2, k], (lon, sib))

    pad = jnp.zeros((132, 16, 64), BF16)
    for m in range(3):
        cots[:, :, pl.ds(256 * m + COUT, 64)] = pad
    conv_t[...] = jnp.zeros(conv_t.shape, BF16)
    for load in loads[2:]:
        load.wait()
    own_bias = jnp.zeros((1, OWN_OUT), F32)
    for r in range(4):
        own_bias += jnp.where(rank == r, conv_b[:, pl.ds(OWN_OUT * r, OWN_OUT)], 0.0)
    a_of = lax.broadcasted_iota(jnp.int32, (COUT, OWN_OUT), 0)
    b_of = lax.broadcasted_iota(jnp.int32, (COUT, OWN_OUT), 1)
    pick = (a_of == b_of + OWN_OUT * rank).astype(F32).astype(BF16)
    for t in range(9):
        w = conv_w[t // 3, t % 3]
        mine[t] = nn(w, pick).astype(BF16)
        conv_t[pl.ds(768 * (t % 3) + 256 * (2 - t // 3), COUT), :] = w.astype(F32).T.astype(BF16)
    src = lax.broadcasted_iota(jnp.int32, (COUT, CIN), 0)
    dst = lax.broadcasted_iota(jnp.int32, (COUT, CIN), 1)
    place = src // OWN_OUT * OWN_IN + lax.rem(src, OWN_OUT)
    spread = [(dst == place + OWN_OUT * h).astype(F32).astype(BF16) for h in range(2)]

    arrived(c_block(cross), cr.at[0])
    send(c_block(cross), c_block(cross), cs.at[2], cr.at[2], (lon, sib))
    a_of = lax.broadcasted_iota(jnp.int32, (CIN, OWN_IN), 0)
    b_of = lax.broadcasted_iota(jnp.int32, (CIN, OWN_IN), 1)
    pick = (a_of == b_of + OWN_IN * rank).astype(F32).astype(BF16)
    for t in range(16):
        own_up[t] = nn(up_w[t // 4, t % 4], pick).astype(BF16)
    for n in range(2):
        for d in range(4):
            arrived(e_block(n, lax.rem(rank + 4 - d, 4)), er.at[n, d])
    arrived(c_block(sib), cr.at[1])
    arrived(c_block(diag), cr.at[2])
    for b in range(4):
        xf[pl.ds(1 + 16 * b, 16)] = c_all[:, pl.ds(128 * b, 128)].astype(F32).T.reshape(16, H, CIN)
    left, right = e_all[0].astype(F32).T, e_all[1].astype(F32).T

    def widen(pair):
        return nn(pair[:16].astype(BF16), spread[0]) + nn(pair[16:].astype(BF16), spread[1])

    xf[0] = widen(left[96:128])[8:]
    xf[65] = widen(right[32:64])[:8]
    xf[66:68] = jnp.zeros((2, H, CIN), F32)

    @pl.loop(0, 3)
    def _(n):
        t0 = n * 22
        rows = pl.ds(pl.multiple_of(t0 * H, 16), 22 * H)
        for d in range(2):
            v = xf[pl.ds(t0 + 1 - d, 22)]
            for s, w in enumerate((down(v), v, up(v))):
                xl[rows, pl.ds((2 * s + d) * CIN, CIN)] = w.reshape(22 * H, CIN).astype(BF16)

    pass_on(0)
    for rp in range(2):
        for cp in range(2):
            taps = ((3, 1), (2, 0))[rp]
            w = jnp.concatenate([up_w[ky, cp + 2 * d] for ky in taps for d in range(2)], 1)
            val = nt(xl[:, pl.ds(rp * 2 * CIN, 4 * CIN)], w)
            pre[:, cp, rp] = val.reshape(66, H, COUT)
            if (rp, cp) != (1, 1):
                pass_on(1 + 2 * rp + cp)

    bias = up_b[...].reshape(1, 1, 1, 1, COUT)

    @pl.loop(0, 22)
    def _(n):
        ts = pl.ds(n * 3, 3)
        v = pre[ts] + bias
        s = jax.nn.sigmoid(v)
        fs[ts] = s * (1.0 + v * (1.0 - s))
        h = (v * s).astype(BF16).astype(F32).reshape(6, 2, H, COUT)
        for m, w in enumerate(shifted(h)):
            hid[m, pl.ds(n * 6, 6)] = w

    def along_x(chunk, p, which):
        send(part.at[chunk, p], rx1.at[p, which], x1s.at[p, which], x1r.at[p, which],
             dev(first(p), z, y))

    def place_cot(at, v, n):
        for m, w in enumerate(shifted(v.reshape(n, 2, H, COUT))):
            cots[pl.ds(at, n), :, pl.ds(256 * m, COUT)] = w

    place_cot(0, left[64:96], 2)
    place_cot(130, right[0:32], 2)
    cols = 2 * WC // PIECES
    for k in range(PIECES):
        arrived(g_block(sib, k), gr.at[1, k])
        arrived(g_block(diag, k), gr.at[2, k])
        for b in range(k * cols // 8, (k + 1) * cols // 8):
            place_cot(2 + 8 * b, g_all[:, pl.ds(128 * b, 128)].astype(F32).T, 8)
        count = cols + 2 * (k == PIECES - 1)
        g = [cots[pl.ds(k * cols + 2 - kx, count)].reshape(16 * count, 768) for kx in range(3)]
        acc = nn(jnp.concatenate(g, 1), conv_t[...])
        ts = pl.ds(k * cols // 2, count // 2)
        d = (acc.reshape(count // 2, 2, 2, H, COUT) * fs[ts]).astype(BF16).astype(F32)
        for cp in range(2):
            even, odd = d[:, cp, 0], d[:, cp, 1]
            for ky, v in enumerate((down(odd), even, odd, up(even))):
                df[cp, ky, ts] = v

    def window(ky, kx):
        return df[kx % 2, ky, pl.ds(kx // 2, 64)].reshape(POS, COUT).astype(BF16)

    for ky in (xo, xa, xb, x):
        for pair in range(2):
            a, b = [nn(coarse[...], window(ky, kx)) for kx in (2 * pair, 2 * pair + 1)]
            slabs = (a[:, :128], jnp.concatenate([a[:, 128:], b[:, :64]], 1), b[:, 64:])
            for n, slab in enumerate(slabs):
                p = 3 * pair + n
                part[ky, p] = slab.astype(BF16)
                if ky is xo:
                    along_x(xo, p, 1)
                elif ky is (xa, xb)[p % 2]:
                    along_x(ky, p, 0)

    def spot(b):
        return b // 4, 6 + b % 4 // 2, pl.ds(b % 2 * OWN_OUT, OWN_OUT)

    def put(b, v):
        c, p, rows = spot(b)
        part[c, p, rows, :] = v.astype(BF16)

    tails = []
    for t in range(9):
        g = nn(cot[...], hid[t // 3, pl.ds(t % 3, 128)].reshape(FINE, COUT))
        put(t, g[:, :128])
        tails.append(g[:, 128:])
    tails.append(jnp.zeros((OWN_OUT, 64), F32))
    for u in range(5):
        put(9 + u, jnp.concatenate(tails[2 * u:2 * u + 2], 1))
    for b in (14, 15):
        put(b, jnp.zeros((OWN_OUT, 128), F32))
    for p in (6, 7):
        along_x(xo, p, 1)
        along_x(first(p), p, 0)

    total = None
    for t in range(16):
        term = nn(window(t // 4, t % 4), own_up[t])
        total = term if total is None else total + term
    c_pos[...] = total

    for d in far_first:
        zz = lax.rem(z + d, nz)
        q = second(zz)
        for which in range(2):
            arrived(rx1.at[zz, which], x1r.at[zz, which])
        kept[d] = part[x, zz].astype(F32) + rx1[zz, 0].astype(F32)
        sb1[d] = (part[q, zz].astype(F32) + rx1[zz, 1].astype(F32)).astype(BF16)
        send(sb1.at[d], rx2.at[d], x2s.at[d], x2r.at[d], dev(q, z, y))

    def refine(n):
        acc = None
        for t in range(9):
            term = nn(hid[t // 3, pl.ds(16 * n + t % 3, 16)].reshape(256, COUT), mine[t])
            acc = term if acc is None else acc + term
        r_pos[pl.ds(256 * n, 256), :] = acc + own_bias

    for n in range(5):
        refine(n)

    for d in far_first:
        arrived(rx2.at[d], x2r.at[d])
        acc = kept[d] + rx2[d].astype(F32)
        if d > 0:
            sb2[d] = acc.astype(BF16)
            send(sb2.at[d], rz.at[d], zs_s.at[d], zs_r.at[d], zdev[d])
        else:
            kept[0] = acc
    for n in range(5, 8):
        refine(n)
    for r in range(2):
        for i in range(H):
            g32[pl.ds(2 * i + r, OWN_OUT, stride=16), :] = r_pos[pl.ds(8 * r + i, 128, stride=16), :].T
    refined[...] = g32[...].reshape(OWN_OUT, 16, 128).astype(BF16)
    acc = kept[0]
    for d in near_first[1:]:
        arrived(rz.at[d], zs_r.at[d])
        acc = acc + rz[d].astype(F32)
    ys[...] = acc
    send(ys, yr, y_sem.at[0], y_sem.at[1], ydev)
    for i in range(H):
        c_grad[i] = c_pos[pl.ds(i, WC, stride=H), :].astype(BF16)
    arrived(yr, y_sem.at[1])
    res[x, z] = (acc + yr[...]).astype(BF16)
    here = res.at[x, z]
    for d in near_first[1:]:
        send(here, here, azs.at[d], azr.at[d], zdev[d])

    def direct(d):
        return d == nz // 2

    def spread_x(d):
        zz = lax.rem(z + nz - d, nz)
        got = res.at[x, zz]
        if d > 0:
            arrived(got, azr.at[d])
        if direct(d):
            send(got, got, axs.at[2, d], axr.at[2, d], dev(xo, z, y))
        send(got, got, axs.at[0, d], axr.at[0, d], dev(second(zz), z, y))
        send(got, got, axs.at[1, d], axr.at[1, d], dev(first(zz), z, y))

    def forward_x(d):
        zz = lax.rem(z + nz - d, nz)
        got = res.at[second(zz), zz]
        arrived(got, axr.at[0, d])
        if not direct(d):
            send(got, got, axs.at[2, d], axr.at[2, d], dev(first(zz), z, y))

    lag = 3
    for n in range(nz + lag):
        if n < nz:
            spread_x(near_first[n])
        if n >= lag:
            forward_x(near_first[n - lag])
    for d in near_first:
        zz = lax.rem(z + nz - d, nz)
        arrived(res.at[first(zz), zz], axr.at[1, d])
        arrived(res.at[xo, zz], axr.at[2, d])
    for copy in started:
        copy.wait_send()


def strip(dims, *args):
    nx, nz, ny = dims
    dma = pltpu.SemaphoreType.DMA
    vm = pltpu.VMEM
    any_ = pl.BlockSpec(memory_space=pl.ANY)
    return pl.pallas_call(
        functools.partial(kernel, dims),
        out_shape=(
            jax.ShapeDtypeStruct((OWN_OUT, 2 * H, 2 * WC), BF16),
            jax.ShapeDtypeStruct((H, WC, OWN_IN), BF16),
            jax.ShapeDtypeStruct((nx, nz, PIECE, 128), BF16),
        ),
        in_specs=[any_] * 4 + [VM] * 2,
        out_specs=[VM] * 3,
        scratch_shapes=[
            vm((H, WC, OWN_IN), BF16),
            vm((OWN_OUT, 2 * H, 2 * WC), BF16),
            vm((OWN_IN, POS), BF16),
            vm((OWN_OUT, FINE), BF16),
            vm((OWN_OUT, 128), BF16),
            vm((OWN_OUT * 2 * H, 2 * WC), F32),
            vm((CIN, POS), BF16),
            vm((COUT, FINE), BF16),
            vm((2, COUT, 128), BF16),
            vm((4, 4, COUT, CIN), BF16),
            vm((3, 3, COUT, COUT), BF16),
            vm((9 * 256, COUT), BF16),
            vm((9, COUT, OWN_OUT), BF16),
            vm((16, COUT, OWN_IN), BF16),
            vm((68, H, CIN), F32),
            vm((528, 6 * CIN), BF16),
            vm((66, 2, 2, H, COUT), F32),
            vm((66, 2, 2, H, COUT), F32),
            vm((3, 132, 16, COUT), BF16),
            vm((132, 16, 3 * 256), BF16),
            vm((2, 4, 66, H, COUT), F32),
            vm((nx, nz, PIECE, 128), BF16),
            vm((FINE, OWN_OUT), F32),
            vm((POS, OWN_IN), F32),
            vm((nz, 2, PIECE, 128), BF16),
            vm((nz, PIECE, 128), F32),
            vm((nz, PIECE, 128), BF16),
            vm((nz, PIECE, 128), BF16),
            vm((nz, PIECE, 128), BF16),
            vm((nz, PIECE, 128), BF16),
            vm((PIECE, 128), F32),
            vm((PIECE, 128), F32),
            dma((4,)), dma((3,)), dma((3,)), dma((3, PIECES)), dma((3, PIECES)), dma((2, 4)), dma((2, 4)),
            dma((nz, 2)), dma((nz, 2)), dma((nz,)), dma((nz,)), dma((nz,)), dma((nz,)), dma((2,)),
            dma((nz,)), dma((nz,)), dma((3, nz)), dma((3, nz)),
        ],
        compiler_params=pltpu.CompilerParams(
            collective_id=0, has_side_effects=True, vmem_limit_bytes=LIMIT
        ),
        name="strip",
    )(*args)


def unpack_kernel(refined, c_grad, sums, refined_out, c_out, up_grad, conv_grad, ref, cg, src, up, conv, sems, out_sems):
    nx = sums.shape[0]
    loads = [pltpu.make_async_copy(sums.at[k], src.at[k], sems.at[k]) for k in range(nx)]
    loads += [
        pltpu.make_async_copy(refined, ref, sems.at[nx]),
        pltpu.make_async_copy(c_grad, cg, sems.at[nx + 1]),
    ]
    for copy in loads:
        copy.start()
    passes = [
        pltpu.make_async_copy(ref, refined_out, out_sems.at[nx]),
        pltpu.make_async_copy(cg, c_out, out_sems.at[nx + 1]),
    ]
    for ky in range(4):
        loads[ky].wait()
        for pair in range(2):
            a, m, b = [src[ky, 3 * pair + n].astype(F32) for n in range(3)]
            up[ky, 2 * pair] = jnp.concatenate([a, m[:, :64]], 1)
            up[ky, 2 * pair + 1] = jnp.concatenate([m[:, 64:], b], 1)
        copy = pltpu.make_async_copy(up.at[ky], up_grad.at[ky], out_sems.at[ky])
        copy.start()
        passes.append(copy)

    for load, copy in zip(loads[nx:], passes):
        load.wait()
        copy.start()

    def block(b):
        return src[b // 4, 6 + b % 4 // 2, pl.ds(b % 2 * OWN_OUT, OWN_OUT), :].astype(F32)

    for t in range(9):
        tail = block(9 + t // 2)[:, 64 * (t % 2):64 * (t % 2) + 64]
        conv[t // 3, t % 3] = jnp.concatenate([block(t), tail], 1)
    copy = pltpu.make_async_copy(conv, conv_grad, out_sems.at[nx + 2])
    copy.start()
    for copy in passes + [copy]:
        copy.wait()


def unpack(refined, c_grad, sums):
    any_ = pl.BlockSpec(memory_space=pl.ANY)
    up = (4, 4, OWN_IN, COUT)
    conv = (3, 3, OWN_OUT, COUT)
    return pl.pallas_call(
        unpack_kernel,
        out_shape=(
            jax.ShapeDtypeStruct(refined.shape, BF16),
            jax.ShapeDtypeStruct(c_grad.shape, BF16),
            jax.ShapeDtypeStruct(up, F32),
            jax.ShapeDtypeStruct(conv, F32),
        ),
        in_specs=[any_] * 3,
        out_specs=[any_] * 4,
        scratch_shapes=[
            pltpu.VMEM(refined.shape, BF16),
            pltpu.VMEM(c_grad.shape, BF16),
            pltpu.VMEM(sums.shape, BF16),
            pltpu.VMEM(up, F32),
            pltpu.VMEM(conv, F32),
            pltpu.SemaphoreType.DMA((6,)),
            pltpu.SemaphoreType.DMA((7,)),
        ],
        compiler_params=pltpu.CompilerParams(vmem_limit_bytes=LIMIT),
        name="unpack",
    )(refined, c_grad, sums)


def local(dims, coarse, up_weight, up_bias, conv_weight, conv_bias, cotangent):
    refined, c_grad, sums = strip(
        dims, coarse.transpose(1, 2, 0), cotangent, up_weight.transpose(0, 1, 3, 2), conv_weight,
        up_bias.reshape(1, COUT), conv_bias.reshape(1, COUT),
    )
    refined, c_grad, up_grad, conv_grad = unpack(refined, c_grad, sums)
    return refined, c_grad.transpose(2, 0, 1), up_grad, conv_grad.transpose(0, 1, 3, 2)


def solution(mesh):
    dims = (4, 8, 2)
    placed = (P("chan", None, "lon"), P(), P(), P(), P(), P("chan", None, "lon"))
    return jax.shard_map(
        functools.partial(local, dims),
        mesh=mesh,
        in_specs=placed,
        out_specs=(
            P("chan", None, "lon"),
            P("chan", None, "lon"),
            P(None, None, "chan", None),
            P(None, None, None, "chan"),
        ),
        check_vma=False,
    )
```

```python
import functools

import jax
import jax.numpy as jnp
from jax import lax
from jax.experimental import pallas as pl
from jax.experimental.pallas import tpu as pltpu
from jax.sharding import PartitionSpec as P

MESH = pl.DeviceIdType.MESH
F32, BF16 = jnp.float32, jnp.bfloat16
VM = pl.BlockSpec(memory_space=pltpu.VMEM)
CIN, COUT, H, WC = 384, 192, 8, 64
OWN_IN, OWN_OUT = CIN // 4, COUT // 4
POS, FINE = H * WC, 4 * H * WC
PIECE = 96
LIMIT = 60 << 20


def nn(a, b):
    return jnp.dot(a, b, preferred_element_type=F32)


def nt(a, b):
    return lax.dot_general(a, b, (((1,), (1,)), ((), ())), preferred_element_type=F32)


def down(v):
    row = lax.broadcasted_iota(jnp.int32, v.shape, v.ndim - 2)
    return jnp.where(row == 0, 0.0, pltpu.roll(v, 1, v.ndim - 2))


def up(v):
    row = lax.broadcasted_iota(jnp.int32, v.shape, v.ndim - 2)
    return jnp.where(row == H - 1, 0.0, pltpu.roll(v, H - 1, v.ndim - 2))


PIECES = 4


def shifted(v):
    even, odd = v[:, 0], v[:, 1]
    pairs = ((down(odd), even), (even, odd), (odd, up(even)))
    return [jnp.concatenate(pair, 1).astype(BF16) for pair in pairs]


def kernel(dims, coarse_hbm, cot_hbm, up_hbm, conv_hbm, up_b, conv_b,
           refined, c_grad, res,
           coarse_in, cot_in, coarse, cot, c_end, g_end, g32, c_all, g_all, ce_all, ge_all, up_w, conv_w, conv_t, mine, own_up,
           xf, xl, pre, fs, hid, cots, df, part, r_pos, c_pos,
           rx1, kept, sb1, rx2, sb2, rz, ys, yr,
           w_sem, cs, cr, gs, gr, es, er, x1s, x1r, x2s, x2r, zs_s, zs_r, y_sem,
           azs, azr, axs, axr):
    nx, nz, ny = dims
    lon, rank = lax.axis_index("lon"), lax.axis_index("chan")
    n_lon = nx * nz * ny
    x, z, y = lon // (nz * ny), lax.rem(lon // ny, nz), lax.rem(lon, ny)
    far, core = rank // 2, lax.rem(rank, 2)
    sib, cross = far * 2 + 1 - core, (1 - far) * 2 + core
    diag = (1 - far) * 2 + 1 - core
    sides = (lax.rem(lon + 1, n_lon), lax.rem(lon + n_lon - 1, n_lon))
    xa, xb = x + 1 - 2 * lax.rem(x, 2), 3 - x
    xo = lax.rem(x + 2, 4)

    def dev(px, pz, py):
        return ((px * nz + pz) * ny + py, rank)

    def first(zz):
        return xa + lax.rem(zz, 2) * (xb - xa)

    def second(zz):
        return xb + lax.rem(zz, 2) * (xa - xb)

    near_first = sorted(range(nz), key=lambda d: min(d, nz - d))
    far_first = near_first[::-1]
    zdev = [dev(x, lax.rem(z + d, nz), y) for d in range(nz)]
    ydev = dev(x, z, 1 - y)

    loads = [
        pltpu.make_async_copy(coarse_hbm, coarse_in, w_sem.at[0]),
        pltpu.make_async_copy(cot_hbm, cot_in, w_sem.at[1]),
        pltpu.make_async_copy(up_hbm, up_w, w_sem.at[2]),
        pltpu.make_async_copy(conv_hbm, conv_w, w_sem.at[3]),
    ]
    for load in loads:
        load.start()

    barrier = pltpu.get_barrier_semaphore()
    greet = [zdev[d] for d in far_first[:-1]]
    greet += [(side, lax.rem(rank + d, 4)) for side in sides for d in range(4)]
    greet += [dev(xo, z, y), dev(xa, z, y), dev(xb, z, y)]
    greet += [(lon, lax.rem(rank + d, 4)) for d in range(1, 4)]
    for peer in greet:
        pl.semaphore_signal(barrier, inc=1, device_id=peer, device_id_type=MESH)

    loads[0].wait()
    for i in range(H):
        c_pos[pl.ds(i, WC, stride=H), :] = coarse_in[i].astype(F32)
    for n in range(4):
        coarse[:, pl.ds(128 * n, 128)] = c_pos[pl.ds(128 * n, 128), :].T.astype(BF16)
    c_end[0] = c_pos[pl.ds(POS - 16, 16), :].astype(BF16)
    c_end[1] = c_pos[pl.ds(0, 16), :].astype(BF16)
    pl.semaphore_wait(barrier, len(greet))

    started = []

    def copy_of(a, b, s, r, to):
        return pltpu.make_async_remote_copy(
            src_ref=a, dst_ref=b, send_sem=s, recv_sem=r, device_id=to, device_id_type=MESH
        )

    def send(a, b, s, r, to):
        copy = copy_of(a, b, s, r, to)
        copy.start()
        started.append(copy)

    def arrived(b, r):
        copy_of(b, b, r, r, (lon, sib)).wait_recv()

    def c_block(r):
        return c_all.at[pl.ds(pl.multiple_of(r * OWN_IN, 16), OWN_IN), :]

    width = FINE // PIECES

    def g_block(r, k):
        return g_all.at[pl.ds(pl.multiple_of(r * OWN_OUT, 16), OWN_OUT), pl.ds(k * width, width)]

    send(coarse, c_block(rank), cs.at[0], cr.at[0], (lon, cross))
    for n, side in enumerate(sides):
        for d in range(4):
            to = (side, lax.rem(rank + d, 4))
            send(c_end.at[n], ce_all.at[n, rank], es.at[0, n, d], er.at[0, n, d], to)
    send(coarse, c_block(rank), cs.at[1], cr.at[1], (lon, sib))
    loads[1].wait()
    g32[...] = cot_in[...].astype(F32).reshape(OWN_OUT * 16, 128)
    for r in range(2):
        for i in range(H):
            r_pos[pl.ds(8 * r + i, 128, stride=16), :] = g32[pl.ds(2 * i + r, OWN_OUT, stride=16), :].T
    for n in range(16):
        cot[:, pl.ds(128 * n, 128)] = r_pos[pl.ds(128 * n, 128), :].T.astype(BF16)
    g_end[0] = r_pos[pl.ds(FINE - 32, 32), :].astype(BF16)
    g_end[1] = r_pos[pl.ds(0, 32), :].astype(BF16)
    for k in range(PIECES):
        own_part = cot.at[:, pl.ds(k * width, width)]
        send(own_part, g_block(rank, k), gs.at[0, k], gr.at[0, k], (lon, cross))
        send(own_part, g_block(rank, k), gs.at[1, k], gr.at[1, k], (lon, sib))
    for n, side in enumerate(sides):
        for d in range(4):
            to = (side, lax.rem(rank + d, 4))
            send(g_end.at[n], ge_all.at[n, rank], es.at[1, n, d], er.at[1, n, d], to)
    c_all[pl.ds(pl.multiple_of(rank * OWN_IN, 16), OWN_IN), :] = coarse[...]
    g_all[pl.ds(pl.multiple_of(rank * OWN_OUT, 16), OWN_OUT), :] = cot[...]

    def pass_on(k):
        arrived(g_block(cross, k), gr.at[0, k])
        send(g_block(cross, k), g_block(cross, k), gs.at[2, k], gr.at[2, k], (lon, sib))

    pad = jnp.zeros((132, 16, 64), BF16)
    for m in range(3):
        cots[:, :, pl.ds(256 * m + COUT, 64)] = pad
    conv_t[...] = jnp.zeros(conv_t.shape, BF16)
    for load in loads[2:]:
        load.wait()
    own_bias = jnp.zeros((1, OWN_OUT), F32)
    for r in range(4):
        own_bias += jnp.where(rank == r, conv_b[:, pl.ds(OWN_OUT * r, OWN_OUT)], 0.0)
    a_of = lax.broadcasted_iota(jnp.int32, (COUT, OWN_OUT), 0)
    b_of = lax.broadcasted_iota(jnp.int32, (COUT, OWN_OUT), 1)
    pick = (a_of == b_of + OWN_OUT * rank).astype(F32).astype(BF16)
    for t in range(9):
        w = conv_w[t // 3, t % 3]
        mine[t] = nn(w, pick).astype(BF16)
        conv_t[pl.ds(768 * (t % 3) + 256 * (2 - t // 3), COUT), :] = w.astype(F32).T.astype(BF16)

    arrived(c_block(cross), cr.at[0])
    send(c_block(cross), c_block(cross), cs.at[2], cr.at[2], (lon, sib))
    a_of = lax.broadcasted_iota(jnp.int32, (CIN, OWN_IN), 0)
    b_of = lax.broadcasted_iota(jnp.int32, (CIN, OWN_IN), 1)
    pick = (a_of == b_of + OWN_IN * rank).astype(F32).astype(BF16)
    for t in range(16):
        own_up[t] = nn(up_w[t // 4, t % 4], pick).astype(BF16)
    for n in range(2):
        for d in range(4):
            arrived(ce_all.at[n, lax.rem(rank + 4 - d, 4)], er.at[0, n, d])
    arrived(c_block(sib), cr.at[1])
    arrived(c_block(diag), cr.at[2])
    for b in range(4):
        xf[pl.ds(1 + 16 * b, 16)] = c_all[:, pl.ds(128 * b, 128)].astype(F32).T.reshape(16, H, CIN)
    left, right = [
        jnp.concatenate([ce_all[n, r].astype(F32) for r in range(4)], 1) for n in range(2)
    ]
    xf[0] = left[8:]
    xf[65] = right[:8]
    xf[66:68] = jnp.zeros((2, H, CIN), F32)

    @pl.loop(0, 3)
    def _(n):
        t0 = n * 22
        rows = pl.ds(pl.multiple_of(t0 * H, 16), 22 * H)
        for d in range(2):
            v = xf[pl.ds(t0 + 1 - d, 22)]
            for s, w in enumerate((down(v), v, up(v))):
                xl[rows, pl.ds((2 * s + d) * CIN, CIN)] = w.reshape(22 * H, CIN).astype(BF16)

    pass_on(0)
    for rp in range(2):
        for cp in range(2):
            taps = ((3, 1), (2, 0))[rp]
            w = jnp.concatenate([up_w[ky, cp + 2 * d] for ky in taps for d in range(2)], 1)
            val = nt(xl[:, pl.ds(rp * 2 * CIN, 4 * CIN)], w)
            pre[:, cp, rp] = val.reshape(66, H, COUT)
        pass_on(1 + rp)

    bias = up_b[...].reshape(1, 1, 1, 1, COUT)

    def activate(n):
        ts = pl.ds(n * 3, 3)
        v = pre[ts] + bias
        s = jax.nn.sigmoid(v)
        fs[ts] = s * (1.0 + v * (1.0 - s))
        h = (v * s).astype(BF16).astype(F32).reshape(6, 2, H, COUT)
        for m, w in enumerate(shifted(h)):
            hid[m, pl.ds(n * 6, 6)] = w

    pl.loop(0, 11)(activate)
    pass_on(3)
    pl.loop(11, 22)(activate)

    def along_x(chunk, p, which):
        send(part.at[chunk, p], rx1.at[p, which], x1s.at[p, which], x1r.at[p, which],
             dev(first(p), z, y))

    def place_cot(at, v, n):
        for m, w in enumerate(shifted(v.reshape(n, 2, H, COUT))):
            cots[pl.ds(at, n), :, pl.ds(256 * m, COUT)] = w

    for k in range(PIECES):
        arrived(g_block(sib, k), gr.at[1, k])
        arrived(g_block(diag, k), gr.at[2, k])
    for b in range(16):
        place_cot(2 + 8 * b, g_all[:, pl.ds(128 * b, 128)].astype(F32).T, 8)
    for n in range(2):
        for d in range(4):
            arrived(ge_all.at[n, lax.rem(rank + 4 - d, 4)], er.at[1, n, d])
        both = jnp.concatenate([ge_all[n, r].astype(F32) for r in range(4)], 1)
        place_cot(130 * n, both, 2)

    @pl.loop(0, 5)
    def _(n):
        g = [cots[pl.ds(n * 26 + 2 - kx, 26)].reshape(416, 768) for kx in range(3)]
        acc = nn(jnp.concatenate(g, 1), conv_t[...])
        ts = pl.ds(n * 13, 13)
        d = (acc.reshape(13, 2, 2, H, COUT) * fs[ts]).astype(BF16).astype(F32)
        for cp in range(2):
            even, odd = d[:, cp, 0], d[:, cp, 1]
            for ky, v in enumerate((down(odd), even, odd, up(even))):
                df[cp, ky, ts] = v

    def window(ky, kx):
        return df[kx % 2, ky, pl.ds(kx // 2, 64)].reshape(POS, COUT).astype(BF16)

    for ky in (xo, xa, xb, x):
        for pair in range(2):
            a, b = [nn(coarse[...], window(ky, kx)) for kx in (2 * pair, 2 * pair + 1)]
            slabs = (a[:, :128], jnp.concatenate([a[:, 128:], b[:, :64]], 1), b[:, 64:])
            for n, slab in enumerate(slabs):
                p = 3 * pair + n
                part[ky, p] = slab.astype(BF16)
                if ky is xo:
                    along_x(xo, p, 1)
                elif ky is (xa, xb)[p % 2]:
                    along_x(ky, p, 0)

    def spot(b):
        return b // 4, 6 + b % 4 // 2, pl.ds(b % 2 * OWN_OUT, OWN_OUT)

    def put(b, v):
        c, p, rows = spot(b)
        part[c, p, rows, :] = v.astype(BF16)

    tails = []
    for t in range(9):
        g = nn(cot[...], hid[t // 3, pl.ds(t % 3, 128)].reshape(FINE, COUT))
        put(t, g[:, :128])
        tails.append(g[:, 128:])
    tails.append(jnp.zeros((OWN_OUT, 64), F32))
    for u in range(5):
        put(9 + u, jnp.concatenate(tails[2 * u:2 * u + 2], 1))
    for b in (14, 15):
        put(b, jnp.zeros((OWN_OUT, 128), F32))
    for p in (6, 7):
        along_x(xo, p, 1)
        along_x(first(p), p, 0)

    total = None
    for t in range(16):
        term = nn(window(t // 4, t % 4), own_up[t])
        total = term if total is None else total + term
    c_pos[...] = total

    for d in far_first:
        zz = lax.rem(z + d, nz)
        q = second(zz)
        for which in range(2):
            arrived(rx1.at[zz, which], x1r.at[zz, which])
        kept[d] = part[x, zz].astype(F32) + rx1[zz, 0].astype(F32)
        sb1[d] = (part[q, zz].astype(F32) + rx1[zz, 1].astype(F32)).astype(BF16)
        send(sb1.at[d], rx2.at[d], x2s.at[d], x2r.at[d], dev(q, z, y))

    def refine(n):
        acc = None
        for t in range(9):
            term = nn(hid[t // 3, pl.ds(16 * n + t % 3, 16)].reshape(256, COUT), mine[t])
            acc = term if acc is None else acc + term
        r_pos[pl.ds(256 * n, 256), :] = acc + own_bias

    for n in range(5):
        refine(n)

    for d in far_first:
        arrived(rx2.at[d], x2r.at[d])
        acc = kept[d] + rx2[d].astype(F32)
        if d > 0:
            sb2[d] = acc.astype(BF16)
            send(sb2.at[d], rz.at[d], zs_s.at[d], zs_r.at[d], zdev[d])
        else:
            kept[0] = acc
    for n in range(5, 8):
        refine(n)
    for r in range(2):
        for i in range(H):
            g32[pl.ds(2 * i + r, OWN_OUT, stride=16), :] = r_pos[pl.ds(8 * r + i, 128, stride=16), :].T
    refined[...] = g32[...].reshape(OWN_OUT, 16, 128).astype(BF16)
    acc = kept[0]
    for d in near_first[1:]:
        arrived(rz.at[d], zs_r.at[d])
        acc = acc + rz[d].astype(F32)
    ys[...] = acc
    send(ys, yr, y_sem.at[0], y_sem.at[1], ydev)
    for i in range(H):
        c_grad[i] = c_pos[pl.ds(i, WC, stride=H), :].astype(BF16)
    arrived(yr, y_sem.at[1])
    res[x, z] = (acc + yr[...]).astype(BF16)
    here = res.at[x, z]
    for d in near_first[1:]:
        send(here, here, azs.at[d], azr.at[d], zdev[d])

    def direct(d):
        return d == nz // 2

    def spread_x(d):
        zz = lax.rem(z + nz - d, nz)
        got = res.at[x, zz]
        if d > 0:
            arrived(got, azr.at[d])
        if direct(d):
            send(got, got, axs.at[2, d], axr.at[2, d], dev(xo, z, y))
        send(got, got, axs.at[0, d], axr.at[0, d], dev(second(zz), z, y))
        send(got, got, axs.at[1, d], axr.at[1, d], dev(first(zz), z, y))

    def forward_x(d):
        zz = lax.rem(z + nz - d, nz)
        got = res.at[second(zz), zz]
        arrived(got, axr.at[0, d])
        if not direct(d):
            send(got, got, axs.at[2, d], axr.at[2, d], dev(first(zz), z, y))

    lag = 3
    for n in range(nz + lag):
        if n < nz:
            spread_x(near_first[n])
        if n >= lag:
            forward_x(near_first[n - lag])
    for d in near_first:
        zz = lax.rem(z + nz - d, nz)
        arrived(res.at[first(zz), zz], axr.at[1, d])
        arrived(res.at[xo, zz], axr.at[2, d])
    for copy in started:
        copy.wait_send()


def strip(dims, *args):
    nx, nz, ny = dims
    dma = pltpu.SemaphoreType.DMA
    vm = pltpu.VMEM
    any_ = pl.BlockSpec(memory_space=pl.ANY)
    return pl.pallas_call(
        functools.partial(kernel, dims),
        out_shape=(
            jax.ShapeDtypeStruct((OWN_OUT, 2 * H, 2 * WC), BF16),
            jax.ShapeDtypeStruct((H, WC, OWN_IN), BF16),
            jax.ShapeDtypeStruct((nx, nz, PIECE, 128), BF16),
        ),
        in_specs=[any_] * 4 + [VM] * 2,
        out_specs=[VM] * 3,
        scratch_shapes=[
            vm((H, WC, OWN_IN), BF16),
            vm((OWN_OUT, 2 * H, 2 * WC), BF16),
            vm((OWN_IN, POS), BF16),
            vm((OWN_OUT, FINE), BF16),
            vm((2, 16, OWN_IN), BF16),
            vm((2, 32, OWN_OUT), BF16),
            vm((OWN_OUT * 2 * H, 2 * WC), F32),
            vm((CIN, POS), BF16),
            vm((COUT, FINE), BF16),
            vm((2, 4, 16, OWN_IN), BF16),
            vm((2, 4, 32, OWN_OUT), BF16),
            vm((4, 4, COUT, CIN), BF16),
            vm((3, 3, COUT, COUT), BF16),
            vm((9 * 256, COUT), BF16),
            vm((9, COUT, OWN_OUT), BF16),
            vm((16, COUT, OWN_IN), BF16),
            vm((68, H, CIN), F32),
            vm((528, 6 * CIN), BF16),
            vm((66, 2, 2, H, COUT), F32),
            vm((66, 2, 2, H, COUT), F32),
            vm((3, 132, 16, COUT), BF16),
            vm((132, 16, 3 * 256), BF16),
            vm((2, 4, 66, H, COUT), F32),
            vm((nx, nz, PIECE, 128), BF16),
            vm((FINE, OWN_OUT), F32),
            vm((POS, OWN_IN), F32),
            vm((nz, 2, PIECE, 128), BF16),
            vm((nz, PIECE, 128), F32),
            vm((nz, PIECE, 128), BF16),
            vm((nz, PIECE, 128), BF16),
            vm((nz, PIECE, 128), BF16),
            vm((nz, PIECE, 128), BF16),
            vm((PIECE, 128), F32),
            vm((PIECE, 128), F32),
            dma((4,)), dma((3,)), dma((3,)), dma((3, PIECES)), dma((3, PIECES)), dma((2, 2, 4)), dma((2, 2, 4)),
            dma((nz, 2)), dma((nz, 2)), dma((nz,)), dma((nz,)), dma((nz,)), dma((nz,)), dma((2,)),
            dma((nz,)), dma((nz,)), dma((3, nz)), dma((3, nz)),
        ],
        compiler_params=pltpu.CompilerParams(
            collective_id=0, has_side_effects=True, vmem_limit_bytes=LIMIT
        ),
        name="strip",
    )(*args)


def unpack_kernel(refined, c_grad, sums, refined_out, c_out, up_grad, conv_grad, ref, cg, src, up, conv, sems, out_sems):
    nx = sums.shape[0]
    loads = [pltpu.make_async_copy(sums.at[k], src.at[k], sems.at[k]) for k in range(nx)]
    loads += [
        pltpu.make_async_copy(refined, ref, sems.at[nx]),
        pltpu.make_async_copy(c_grad, cg, sems.at[nx + 1]),
    ]
    for copy in loads:
        copy.start()
    passes = [
        pltpu.make_async_copy(ref, refined_out, out_sems.at[nx]),
        pltpu.make_async_copy(cg, c_out, out_sems.at[nx + 1]),
    ]
    for ky in range(4):
        loads[ky].wait()
        for pair in range(2):
            a, m, b = [src[ky, 3 * pair + n].astype(F32) for n in range(3)]
            up[ky, 2 * pair] = jnp.concatenate([a, m[:, :64]], 1)
            up[ky, 2 * pair + 1] = jnp.concatenate([m[:, 64:], b], 1)
        copy = pltpu.make_async_copy(up.at[ky], up_grad.at[ky], out_sems.at[ky])
        copy.start()
        passes.append(copy)

    for load, copy in zip(loads[nx:], passes):
        load.wait()
        copy.start()

    def block(b):
        return src[b // 4, 6 + b % 4 // 2, pl.ds(b % 2 * OWN_OUT, OWN_OUT), :].astype(F32)

    for t in range(9):
        tail = block(9 + t // 2)[:, 64 * (t % 2):64 * (t % 2) + 64]
        conv[t // 3, t % 3] = jnp.concatenate([block(t), tail], 1)
    copy = pltpu.make_async_copy(conv, conv_grad, out_sems.at[nx + 2])
    copy.start()
    for copy in passes + [copy]:
        copy.wait()


def unpack(refined, c_grad, sums):
    any_ = pl.BlockSpec(memory_space=pl.ANY)
    up = (4, 4, OWN_IN, COUT)
    conv = (3, 3, OWN_OUT, COUT)
    return pl.pallas_call(
        unpack_kernel,
        out_shape=(
            jax.ShapeDtypeStruct(refined.shape, BF16),
            jax.ShapeDtypeStruct(c_grad.shape, BF16),
            jax.ShapeDtypeStruct(up, F32),
            jax.ShapeDtypeStruct(conv, F32),
        ),
        in_specs=[any_] * 3,
        out_specs=[any_] * 4,
        scratch_shapes=[
            pltpu.VMEM(refined.shape, BF16),
            pltpu.VMEM(c_grad.shape, BF16),
            pltpu.VMEM(sums.shape, BF16),
            pltpu.VMEM(up, F32),
            pltpu.VMEM(conv, F32),
            pltpu.SemaphoreType.DMA((6,)),
            pltpu.SemaphoreType.DMA((7,)),
        ],
        compiler_params=pltpu.CompilerParams(vmem_limit_bytes=LIMIT),
        name="unpack",
    )(refined, c_grad, sums)


def local(dims, coarse, up_weight, up_bias, conv_weight, conv_bias, cotangent):
    refined, c_grad, sums = strip(
        dims, coarse.transpose(1, 2, 0), cotangent, up_weight.transpose(0, 1, 3, 2), conv_weight,
        up_bias.reshape(1, COUT), conv_bias.reshape(1, COUT),
    )
    refined, c_grad, up_grad, conv_grad = unpack(refined, c_grad, sums)
    return refined, c_grad.transpose(2, 0, 1), up_grad, conv_grad.transpose(0, 1, 3, 2)


def solution(mesh):
    dims = (4, 8, 2)
    placed = (P("chan", None, "lon"), P(), P(), P(), P(), P("chan", None, "lon"))
    return jax.shard_map(
        functools.partial(local, dims),
        mesh=mesh,
        in_specs=placed,
        out_specs=(
            P("chan", None, "lon"),
            P("chan", None, "lon"),
            P(None, None, "chan", None),
            P(None, None, None, "chan"),
        ),
        check_vma=False,
    )
```

```python
import functools

import jax
import jax.numpy as jnp
from jax import lax
from jax.experimental import pallas as pl
from jax.experimental.pallas import tpu as pltpu
from jax.sharding import PartitionSpec as P

MESH = pl.DeviceIdType.MESH
F32, BF16 = jnp.float32, jnp.bfloat16
VM = pl.BlockSpec(memory_space=pltpu.VMEM)
CIN, COUT, H, WC = 384, 192, 8, 64
OWN_IN, OWN_OUT = CIN // 4, COUT // 4
POS, FINE = H * WC, 4 * H * WC
PIECE = 96
LIMIT = 60 << 20


def nn(a, b):
    return jnp.dot(a, b, preferred_element_type=F32)


def nt(a, b):
    return lax.dot_general(a, b, (((1,), (1,)), ((), ())), preferred_element_type=F32)


def down(v):
    row = lax.broadcasted_iota(jnp.int32, v.shape, v.ndim - 2)
    return jnp.where(row == 0, 0.0, pltpu.roll(v, 1, v.ndim - 2))


def up(v):
    row = lax.broadcasted_iota(jnp.int32, v.shape, v.ndim - 2)
    return jnp.where(row == H - 1, 0.0, pltpu.roll(v, H - 1, v.ndim - 2))


PIECES = 4


def shifted(v):
    even, odd = v[:, 0], v[:, 1]
    pairs = ((down(odd), even), (even, odd), (odd, up(even)))
    return [jnp.concatenate(pair, 1).astype(BF16) for pair in pairs]


def kernel(dims, coarse_hbm, cot_hbm, up_hbm, conv_hbm, up_b, conv_b,
           refined, c_grad, res,
           coarse_in, cot_in, coarse, cot, c_end, g_end, g32, c_all, g_all, ce_all, ge_all, up_w, conv_w, conv_t, mine, own_up,
           xf, xl, pre, fs, hid, cots, df, part, r_pos, c_pos,
           rx1, kept, sb1, rx2, sb2, rz, ys, yr,
           w_sem, cs, cr, gs, gr, es, er, x1s, x1r, x2s, x2r, zs_s, zs_r, y_sem,
           azs, azr, axs, axr):
    nx, nz, ny = dims
    lon, rank = lax.axis_index("lon"), lax.axis_index("chan")
    n_lon = nx * nz * ny
    x, z, y = lon // (nz * ny), lax.rem(lon // ny, nz), lax.rem(lon, ny)
    far, core = rank // 2, lax.rem(rank, 2)
    sib, cross = far * 2 + 1 - core, (1 - far) * 2 + core
    diag = (1 - far) * 2 + 1 - core
    sides = (lax.rem(lon + 1, n_lon), lax.rem(lon + n_lon - 1, n_lon))
    xa, xb = x + 1 - 2 * lax.rem(x, 2), 3 - x
    xo = lax.rem(x + 2, 4)

    def dev(px, pz, py):
        return ((px * nz + pz) * ny + py, rank)

    def first(zz):
        return xa + lax.rem(zz, 2) * (xb - xa)

    def second(zz):
        return xb + lax.rem(zz, 2) * (xa - xb)

    near_first = sorted(range(nz), key=lambda d: min(d, nz - d))
    far_first = near_first[::-1]
    zdev = [dev(x, lax.rem(z + d, nz), y) for d in range(nz)]
    ydev = dev(x, z, 1 - y)

    loads = [
        pltpu.make_async_copy(coarse_hbm, coarse_in, w_sem.at[0]),
        pltpu.make_async_copy(cot_hbm, cot_in, w_sem.at[1]),
        pltpu.make_async_copy(up_hbm, up_w, w_sem.at[2]),
        pltpu.make_async_copy(conv_hbm, conv_w, w_sem.at[3]),
    ]
    for load in loads:
        load.start()

    barrier = pltpu.get_barrier_semaphore()
    greet = [zdev[d] for d in far_first[:-1]]
    greet += [(side, lax.rem(rank + d, 4)) for side in sides for d in range(4)]
    greet += [dev(xo, z, y), dev(xa, z, y), dev(xb, z, y)]
    greet += [(lon, lax.rem(rank + d, 4)) for d in range(1, 4)]
    for peer in greet:
        pl.semaphore_signal(barrier, inc=1, device_id=peer, device_id_type=MESH)

    loads[0].wait()
    for i in range(H):
        c_pos[pl.ds(i, WC, stride=H), :] = coarse_in[i].astype(F32)
    for n in range(4):
        coarse[:, pl.ds(128 * n, 128)] = c_pos[pl.ds(128 * n, 128), :].T.astype(BF16)
    c_end[0] = c_pos[pl.ds(POS - 16, 16), :].astype(BF16)
    c_end[1] = c_pos[pl.ds(0, 16), :].astype(BF16)
    pl.semaphore_wait(barrier, len(greet))

    started = []

    def copy_of(a, b, s, r, to):
        return pltpu.make_async_remote_copy(
            src_ref=a, dst_ref=b, send_sem=s, recv_sem=r, device_id=to, device_id_type=MESH
        )

    def send(a, b, s, r, to):
        copy = copy_of(a, b, s, r, to)
        copy.start()
        started.append(copy)

    def arrived(b, r):
        copy_of(b, b, r, r, (lon, sib)).wait_recv()

    def c_block(r):
        return c_all.at[pl.ds(pl.multiple_of(r * OWN_IN, 16), OWN_IN), :]

    width = FINE // PIECES

    def g_block(r, k):
        return g_all.at[pl.ds(pl.multiple_of(r * OWN_OUT, 16), OWN_OUT), pl.ds(k * width, width)]

    send(coarse, c_block(rank), cs.at[0], cr.at[0], (lon, cross))
    for n, side in enumerate(sides):
        for d in range(4):
            to = (side, lax.rem(rank + d, 4))
            send(c_end.at[n], ce_all.at[n, rank], es.at[0, n, d], er.at[0, n, d], to)
    send(coarse, c_block(rank), cs.at[1], cr.at[1], (lon, sib))
    loads[1].wait()
    g32[...] = cot_in[...].astype(F32).reshape(OWN_OUT * 16, 128)
    for r in range(2):
        for i in range(H):
            r_pos[pl.ds(8 * r + i, 128, stride=16), :] = g32[pl.ds(2 * i + r, OWN_OUT, stride=16), :].T
    for n in range(16):
        cot[:, pl.ds(128 * n, 128)] = r_pos[pl.ds(128 * n, 128), :].T.astype(BF16)
    gap = jnp.zeros((16, 64 - OWN_OUT), F32)
    for n, at in enumerate((FINE - 32, 0)):
        two = [r_pos[pl.ds(at, 16), :], gap, r_pos[pl.ds(at + 16, 16), :], gap]
        g_end[n] = jnp.concatenate(two, 1).astype(BF16)
    for n, side in enumerate(sides):
        for d in range(4):
            to = (side, lax.rem(rank + d, 4))
            send(g_end.at[n], ge_all.at[n, rank], es.at[1, n, d], er.at[1, n, d], to)
    for k in range(PIECES):
        own_part = cot.at[:, pl.ds(k * width, width)]
        send(own_part, g_block(rank, k), gs.at[0, k], gr.at[0, k], (lon, cross))
        send(own_part, g_block(rank, k), gs.at[1, k], gr.at[1, k], (lon, sib))
    c_all[pl.ds(pl.multiple_of(rank * OWN_IN, 16), OWN_IN), :] = coarse[...]
    g_all[pl.ds(pl.multiple_of(rank * OWN_OUT, 16), OWN_OUT), :] = cot[...]

    def pass_on(k):
        arrived(g_block(cross, k), gr.at[0, k])
        send(g_block(cross, k), g_block(cross, k), gs.at[2, k], gr.at[2, k], (lon, sib))

    pad = jnp.zeros((132, 16, 64), BF16)
    for m in range(3):
        cots[:, :, pl.ds(256 * m + COUT, 64)] = pad
    conv_t[...] = jnp.zeros(conv_t.shape, BF16)
    for load in loads[2:]:
        load.wait()
    own_bias = jnp.zeros((1, OWN_OUT), F32)
    for r in range(4):
        own_bias += jnp.where(rank == r, conv_b[:, pl.ds(OWN_OUT * r, OWN_OUT)], 0.0)
    a_of = lax.broadcasted_iota(jnp.int32, (COUT, OWN_OUT), 0)
    b_of = lax.broadcasted_iota(jnp.int32, (COUT, OWN_OUT), 1)
    pick = (a_of == b_of + OWN_OUT * rank).astype(F32).astype(BF16)
    for t in range(9):
        w = conv_w[t // 3, t % 3]
        mine[t] = nn(w, pick).astype(BF16)
        conv_t[pl.ds(768 * (t % 3) + 256 * (2 - t // 3), COUT), :] = w.astype(F32).T.astype(BF16)

    arrived(c_block(cross), cr.at[0])
    send(c_block(cross), c_block(cross), cs.at[2], cr.at[2], (lon, sib))
    a_of = lax.broadcasted_iota(jnp.int32, (CIN, OWN_IN), 0)
    b_of = lax.broadcasted_iota(jnp.int32, (CIN, OWN_IN), 1)
    pick = (a_of == b_of + OWN_IN * rank).astype(F32).astype(BF16)
    for t in range(16):
        own_up[t] = nn(up_w[t // 4, t % 4], pick).astype(BF16)
    for n in range(2):
        for d in range(4):
            arrived(ce_all.at[n, lax.rem(rank + 4 - d, 4)], er.at[0, n, d])
    arrived(c_block(sib), cr.at[1])
    arrived(c_block(diag), cr.at[2])
    for b in range(4):
        xf[pl.ds(1 + 16 * b, 16)] = c_all[:, pl.ds(128 * b, 128)].astype(F32).T.reshape(16, H, CIN)
    left, right = [
        jnp.concatenate([ce_all[n, r].astype(F32) for r in range(4)], 1) for n in range(2)
    ]
    xf[0] = left[8:]
    xf[65] = right[:8]
    xf[66:68] = jnp.zeros((2, H, CIN), F32)

    @pl.loop(0, 3)
    def _(n):
        t0 = n * 22
        rows = pl.ds(pl.multiple_of(t0 * H, 16), 22 * H)
        for d in range(2):
            v = xf[pl.ds(t0 + 1 - d, 22)]
            for s, w in enumerate((down(v), v, up(v))):
                xl[rows, pl.ds((2 * s + d) * CIN, CIN)] = w.reshape(22 * H, CIN).astype(BF16)

    pass_on(0)
    for rp in range(2):
        for cp in range(2):
            taps = ((3, 1), (2, 0))[rp]
            w = jnp.concatenate([up_w[ky, cp + 2 * d] for ky in taps for d in range(2)], 1)
            val = nt(xl[:, pl.ds(rp * 2 * CIN, 4 * CIN)], w)
            pre[:, cp, rp] = val.reshape(66, H, COUT)
        pass_on(1 + rp)

    bias = up_b[...].reshape(1, 1, 1, 1, COUT)

    def activate(n):
        ts = pl.ds(n * 3, 3)
        v = pre[ts] + bias
        s = jax.nn.sigmoid(v)
        fs[ts] = s * (1.0 + v * (1.0 - s))
        h = (v * s).astype(BF16).astype(F32).reshape(6, 2, H, COUT)
        for m, w in enumerate(shifted(h)):
            hid[m, pl.ds(n * 6, 6)] = w

    pl.loop(0, 11)(activate)
    pass_on(3)
    pl.loop(11, 22)(activate)

    def along_x(chunk, p, which):
        send(part.at[chunk, p], rx1.at[p, which], x1s.at[p, which], x1r.at[p, which],
             dev(first(p), z, y))

    def place_cot(at, v, n):
        for m, w in enumerate(shifted(v.reshape(n, 2, H, COUT))):
            cots[pl.ds(at, n), :, pl.ds(256 * m, COUT)] = w

    def place_edge(n):
        for d in range(4):
            arrived(ge_all.at[n, lax.rem(rank + 4 - d, 4)], er.at[1, n, d])
        cols = []
        for h in (0, 64):
            block = [ge_all[n, r][:, h:h + OWN_OUT].astype(F32) for r in range(4)]
            cols.append(jnp.concatenate(block, 1))
        place_cot(130 * n, jnp.concatenate(cols, 0), 2)

    def place_piece(k):
        arrived(g_block(sib, k), gr.at[1, k])
        arrived(g_block(diag, k), gr.at[2, k])
        for b in range(4 * k, 4 * k + 4):
            place_cot(2 + 8 * b, g_all[:, pl.ds(128 * b, 128)].astype(F32).T, 8)

    def adjoint(n):
        g = [cots[pl.ds(n * 26 + 2 - kx, 26)].reshape(416, 768) for kx in range(3)]
        acc = nn(jnp.concatenate(g, 1), conv_t[...])
        ts = pl.ds(n * 13, 13)
        d = (acc.reshape(13, 2, 2, H, COUT) * fs[ts]).astype(BF16).astype(F32)
        for cp in range(2):
            even, odd = d[:, cp, 0], d[:, cp, 1]
            for ky, v in enumerate((down(odd), even, odd, up(even))):
                df[cp, ky, ts] = v

    place_edge(0)
    place_piece(0)
    place_piece(1)
    pl.loop(0, 2)(adjoint)
    place_edge(1)
    place_piece(2)
    place_piece(3)
    pl.loop(2, 5)(adjoint)

    def window(ky, kx):
        return df[kx % 2, ky, pl.ds(kx // 2, 64)].reshape(POS, COUT).astype(BF16)

    for ky in (xo, xa, xb, x):
        for pair in range(2):
            a, b = [nn(coarse[...], window(ky, kx)) for kx in (2 * pair, 2 * pair + 1)]
            slabs = (a[:, :128], jnp.concatenate([a[:, 128:], b[:, :64]], 1), b[:, 64:])
            for n, slab in enumerate(slabs):
                p = 3 * pair + n
                part[ky, p] = slab.astype(BF16)
                if ky is xo:
                    along_x(xo, p, 1)
                elif ky is (xa, xb)[p % 2]:
                    along_x(ky, p, 0)

    def spot(b):
        return b // 4, 6 + b % 4 // 2, pl.ds(b % 2 * OWN_OUT, OWN_OUT)

    def put(b, v):
        c, p, rows = spot(b)
        part[c, p, rows, :] = v.astype(BF16)

    tails = []
    for t in range(9):
        g = nn(cot[...], hid[t // 3, pl.ds(t % 3, 128)].reshape(FINE, COUT))
        put(t, g[:, :128])
        tails.append(g[:, 128:])
    tails.append(jnp.zeros((OWN_OUT, 64), F32))
    for u in range(5):
        put(9 + u, jnp.concatenate(tails[2 * u:2 * u + 2], 1))
    for b in (14, 15):
        put(b, jnp.zeros((OWN_OUT, 128), F32))
    for p in (6, 7):
        along_x(xo, p, 1)
        along_x(first(p), p, 0)

    for d in far_first:
        zz = lax.rem(z + d, nz)
        q = second(zz)
        for which in range(2):
            arrived(rx1.at[zz, which], x1r.at[zz, which])
        kept[d] = part[x, zz].astype(F32) + rx1[zz, 0].astype(F32)
        sb1[d] = (part[q, zz].astype(F32) + rx1[zz, 1].astype(F32)).astype(BF16)
        send(sb1.at[d], rx2.at[d], x2s.at[d], x2r.at[d], dev(q, z, y))

    total = None
    for t in range(16):
        term = nn(window(t // 4, t % 4), own_up[t])
        total = term if total is None else total + term
    c_pos[...] = total

    def refine(n):
        acc = None
        for t in range(9):
            term = nn(hid[t // 3, pl.ds(16 * n + t % 3, 16)].reshape(256, COUT), mine[t])
            acc = term if acc is None else acc + term
        r_pos[pl.ds(256 * n, 256), :] = acc + own_bias

    for n in range(4):
        refine(n)

    for d in far_first:
        arrived(rx2.at[d], x2r.at[d])
        acc = kept[d] + rx2[d].astype(F32)
        if d > 0:
            sb2[d] = acc.astype(BF16)
            send(sb2.at[d], rz.at[d], zs_s.at[d], zs_r.at[d], zdev[d])
        else:
            kept[0] = acc
    for n in range(4, 8):
        refine(n)
    for r in range(2):
        for i in range(H):
            g32[pl.ds(2 * i + r, OWN_OUT, stride=16), :] = r_pos[pl.ds(8 * r + i, 128, stride=16), :].T
    refined[...] = g32[...].reshape(OWN_OUT, 16, 128).astype(BF16)
    acc = kept[0]
    for d in near_first[1:]:
        arrived(rz.at[d], zs_r.at[d])
        acc = acc + rz[d].astype(F32)
    ys[...] = acc
    send(ys, yr, y_sem.at[0], y_sem.at[1], ydev)
    for i in range(H):
        c_grad[i] = c_pos[pl.ds(i, WC, stride=H), :].astype(BF16)
    arrived(yr, y_sem.at[1])
    res[x, z] = (acc + yr[...]).astype(BF16)
    here = res.at[x, z]
    for d in near_first[1:]:
        send(here, here, azs.at[d], azr.at[d], zdev[d])

    def direct(d):
        return d == nz // 2

    def spread_x(d):
        zz = lax.rem(z + nz - d, nz)
        got = res.at[x, zz]
        if d > 0:
            arrived(got, azr.at[d])
        if direct(d):
            send(got, got, axs.at[2, d], axr.at[2, d], dev(xo, z, y))
        send(got, got, axs.at[0, d], axr.at[0, d], dev(second(zz), z, y))
        send(got, got, axs.at[1, d], axr.at[1, d], dev(first(zz), z, y))

    def forward_x(d):
        zz = lax.rem(z + nz - d, nz)
        got = res.at[second(zz), zz]
        arrived(got, axr.at[0, d])
        if not direct(d):
            send(got, got, axs.at[2, d], axr.at[2, d], dev(first(zz), z, y))

    lag = 3
    for n in range(nz + lag):
        if n < nz:
            spread_x(near_first[n])
        if n >= lag:
            forward_x(near_first[n - lag])
    for d in near_first:
        zz = lax.rem(z + nz - d, nz)
        arrived(res.at[first(zz), zz], axr.at[1, d])
        arrived(res.at[xo, zz], axr.at[2, d])
    for copy in started:
        copy.wait_send()


def strip(dims, *args):
    nx, nz, ny = dims
    dma = pltpu.SemaphoreType.DMA
    vm = pltpu.VMEM
    any_ = pl.BlockSpec(memory_space=pl.ANY)
    return pl.pallas_call(
        functools.partial(kernel, dims),
        out_shape=(
            jax.ShapeDtypeStruct((OWN_OUT, 2 * H, 2 * WC), BF16),
            jax.ShapeDtypeStruct((H, WC, OWN_IN), BF16),
            jax.ShapeDtypeStruct((nx, nz, PIECE, 128), BF16),
        ),
        in_specs=[any_] * 4 + [VM] * 2,
        out_specs=[VM] * 3,
        scratch_shapes=[
            vm((H, WC, OWN_IN), BF16),
            vm((OWN_OUT, 2 * H, 2 * WC), BF16),
            vm((OWN_IN, POS), BF16),
            vm((OWN_OUT, FINE), BF16),
            vm((2, 16, OWN_IN), BF16),
            vm((2, 16, 128), BF16),
            vm((OWN_OUT * 2 * H, 2 * WC), F32),
            vm((CIN, POS), BF16),
            vm((COUT, FINE), BF16),
            vm((2, 4, 16, OWN_IN), BF16),
            vm((2, 4, 16, 128), BF16),
            vm((4, 4, COUT, CIN), BF16),
            vm((3, 3, COUT, COUT), BF16),
            vm((9 * 256, COUT), BF16),
            vm((9, COUT, OWN_OUT), BF16),
            vm((16, COUT, OWN_IN), BF16),
            vm((68, H, CIN), F32),
            vm((528, 6 * CIN), BF16),
            vm((66, 2, 2, H, COUT), F32),
            vm((66, 2, 2, H, COUT), F32),
            vm((3, 132, 16, COUT), BF16),
            vm((132, 16, 3 * 256), BF16),
            vm((2, 4, 66, H, COUT), F32),
            vm((nx, nz, PIECE, 128), BF16),
            vm((FINE, OWN_OUT), F32),
            vm((POS, OWN_IN), F32),
            vm((nz, 2, PIECE, 128), BF16),
            vm((nz, PIECE, 128), F32),
            vm((nz, PIECE, 128), BF16),
            vm((nz, PIECE, 128), BF16),
            vm((nz, PIECE, 128), BF16),
            vm((nz, PIECE, 128), BF16),
            vm((PIECE, 128), F32),
            vm((PIECE, 128), F32),
            dma((4,)), dma((3,)), dma((3,)), dma((3, PIECES)), dma((3, PIECES)), dma((2, 2, 4)), dma((2, 2, 4)),
            dma((nz, 2)), dma((nz, 2)), dma((nz,)), dma((nz,)), dma((nz,)), dma((nz,)), dma((2,)),
            dma((nz,)), dma((nz,)), dma((3, nz)), dma((3, nz)),
        ],
        compiler_params=pltpu.CompilerParams(
            collective_id=0, has_side_effects=True, vmem_limit_bytes=LIMIT
        ),
        name="strip",
    )(*args)


def unpack_kernel(refined, c_grad, sums, refined_out, c_out, up_grad, conv_grad, ref, cg, src, up, conv, sems, out_sems):
    nx = sums.shape[0]
    loads = [pltpu.make_async_copy(sums.at[k], src.at[k], sems.at[k]) for k in range(nx)]
    loads += [
        pltpu.make_async_copy(refined, ref, sems.at[nx]),
        pltpu.make_async_copy(c_grad, cg, sems.at[nx + 1]),
    ]
    for copy in loads:
        copy.start()
    passes = [
        pltpu.make_async_copy(ref, refined_out, out_sems.at[nx]),
        pltpu.make_async_copy(cg, c_out, out_sems.at[nx + 1]),
    ]
    for ky in range(4):
        loads[ky].wait()
        for pair in range(2):
            a, m, b = [src[ky, 3 * pair + n].astype(F32) for n in range(3)]
            up[ky, 2 * pair] = jnp.concatenate([a, m[:, :64]], 1)
            up[ky, 2 * pair + 1] = jnp.concatenate([m[:, 64:], b], 1)
        copy = pltpu.make_async_copy(up.at[ky], up_grad.at[ky], out_sems.at[ky])
        copy.start()
        passes.append(copy)

    for load, copy in zip(loads[nx:], passes):
        load.wait()
        copy.start()

    def block(b):
        return src[b // 4, 6 + b % 4 // 2, pl.ds(b % 2 * OWN_OUT, OWN_OUT), :].astype(F32)

    for t in range(9):
        tail = block(9 + t // 2)[:, 64 * (t % 2):64 * (t % 2) + 64]
        conv[t // 3, t % 3] = jnp.concatenate([block(t), tail], 1)
    copy = pltpu.make_async_copy(conv, conv_grad, out_sems.at[nx + 2])
    copy.start()
    for copy in passes + [copy]:
        copy.wait()


def unpack(refined, c_grad, sums):
    any_ = pl.BlockSpec(memory_space=pl.ANY)
    up = (4, 4, OWN_IN, COUT)
    conv = (3, 3, OWN_OUT, COUT)
    return pl.pallas_call(
        unpack_kernel,
        out_shape=(
            jax.ShapeDtypeStruct(refined.shape, BF16),
            jax.ShapeDtypeStruct(c_grad.shape, BF16),
            jax.ShapeDtypeStruct(up, F32),
            jax.ShapeDtypeStruct(conv, F32),
        ),
        in_specs=[any_] * 3,
        out_specs=[any_] * 4,
        scratch_shapes=[
            pltpu.VMEM(refined.shape, BF16),
            pltpu.VMEM(c_grad.shape, BF16),
            pltpu.VMEM(sums.shape, BF16),
            pltpu.VMEM(up, F32),
            pltpu.VMEM(conv, F32),
            pltpu.SemaphoreType.DMA((6,)),
            pltpu.SemaphoreType.DMA((7,)),
        ],
        compiler_params=pltpu.CompilerParams(vmem_limit_bytes=LIMIT),
        name="unpack",
    )(refined, c_grad, sums)


def local(dims, coarse, up_weight, up_bias, conv_weight, conv_bias, cotangent):
    refined, c_grad, sums = strip(
        dims, coarse.transpose(1, 2, 0), cotangent, up_weight.transpose(0, 1, 3, 2), conv_weight,
        up_bias.reshape(1, COUT), conv_bias.reshape(1, COUT),
    )
    refined, c_grad, up_grad, conv_grad = unpack(refined, c_grad, sums)
    return refined, c_grad.transpose(2, 0, 1), up_grad, conv_grad.transpose(0, 1, 3, 2)


def solution(mesh):
    dims = (4, 8, 2)
    placed = (P("chan", None, "lon"), P(), P(), P(), P(), P("chan", None, "lon"))
    return jax.shard_map(
        functools.partial(local, dims),
        mesh=mesh,
        in_specs=placed,
        out_specs=(
            P("chan", None, "lon"),
            P("chan", None, "lon"),
            P(None, None, "chan", None),
            P(None, None, None, "chan"),
        ),
        check_vma=False,
    )
```

```python
import functools

import jax
import jax.numpy as jnp
from jax import lax
from jax.experimental import pallas as pl
from jax.experimental.pallas import tpu as pltpu
from jax.sharding import PartitionSpec as P

MESH = pl.DeviceIdType.MESH
F32, BF16 = jnp.float32, jnp.bfloat16
VM = pl.BlockSpec(memory_space=pltpu.VMEM)
CIN, COUT, H, WC = 384, 192, 8, 64
OWN_IN, OWN_OUT = CIN // 4, COUT // 4
POS, FINE = H * WC, 4 * H * WC
PIECE = 96
LIMIT = 60 << 20


def nn(a, b):
    return jnp.dot(a, b, preferred_element_type=F32)


def nt(a, b):
    return lax.dot_general(a, b, (((1,), (1,)), ((), ())), preferred_element_type=F32)


def down(v):
    row = lax.broadcasted_iota(jnp.int32, v.shape, v.ndim - 2)
    return jnp.where(row == 0, 0.0, pltpu.roll(v, 1, v.ndim - 2))


def up(v):
    row = lax.broadcasted_iota(jnp.int32, v.shape, v.ndim - 2)
    return jnp.where(row == H - 1, 0.0, pltpu.roll(v, H - 1, v.ndim - 2))


PIECES = 4


def shifted(v):
    even, odd = v[:, 0], v[:, 1]
    pairs = ((down(odd), even), (even, odd), (odd, up(even)))
    return [jnp.concatenate(pair, 1).astype(BF16) for pair in pairs]


def kernel(dims, coarse_hbm, cot_hbm, up_hbm, conv_hbm, up_b, conv_b,
           refined, c_grad, res,
           coarse_in, cot_in, coarse, cot, cot3, c_end, g_end, g32, c_all, g_all, ce_all, ge_all, up_w, conv_w, conv_t, mine, own_up,
           xf, xl, pre, fs, hid, cots, df, part, r_pos, c_pos,
           rx1, kept, sb1, rx2, sb2, rz, ys, yr,
           w_sem, cs, cr, gs, gr, es, er, x1s, x1r, x2s, x2r, zs_s, zs_r, y_sem,
           azs, azr, axs, axr):
    nx, nz, ny = dims
    lon, rank = lax.axis_index("lon"), lax.axis_index("chan")
    n_lon = nx * nz * ny
    x, z, y = lon // (nz * ny), lax.rem(lon // ny, nz), lax.rem(lon, ny)
    far, core = rank // 2, lax.rem(rank, 2)
    sib, cross = far * 2 + 1 - core, (1 - far) * 2 + core
    diag = (1 - far) * 2 + 1 - core
    sides = (lax.rem(lon + 1, n_lon), lax.rem(lon + n_lon - 1, n_lon))
    xa, xb = x + 1 - 2 * lax.rem(x, 2), 3 - x
    xo = lax.rem(x + 2, 4)

    def dev(px, pz, py):
        return ((px * nz + pz) * ny + py, rank)

    def first(zz):
        return xa + lax.rem(zz, 2) * (xb - xa)

    def second(zz):
        return xb + lax.rem(zz, 2) * (xa - xb)

    near_first = sorted(range(nz), key=lambda d: min(d, nz - d))
    far_first = near_first[::-1]
    zdev = [dev(x, lax.rem(z + d, nz), y) for d in range(nz)]
    ydev = dev(x, z, 1 - y)

    loads = [
        pltpu.make_async_copy(coarse_hbm, coarse_in, w_sem.at[0]),
        pltpu.make_async_copy(cot_hbm, cot_in, w_sem.at[1]),
        pltpu.make_async_copy(up_hbm, up_w, w_sem.at[2]),
        pltpu.make_async_copy(conv_hbm, conv_w, w_sem.at[3]),
    ]
    for load in loads:
        load.start()

    barrier = pltpu.get_barrier_semaphore()
    greet = [zdev[d] for d in far_first[:-1]]
    greet += [(side, lax.rem(rank + d, 4)) for side in sides for d in range(4)]
    greet += [dev(xo, z, y), dev(xa, z, y), dev(xb, z, y)]
    greet += [(lon, lax.rem(rank + d, 4)) for d in range(1, 4)]
    for peer in greet:
        pl.semaphore_signal(barrier, inc=1, device_id=peer, device_id_type=MESH)

    loads[0].wait()
    for i in range(H):
        c_pos[pl.ds(i, WC, stride=H), :] = coarse_in[i].astype(F32)
    for n in range(4):
        coarse[:, pl.ds(128 * n, 128)] = c_pos[pl.ds(128 * n, 128), :].T.astype(BF16)
    c_end[0] = c_pos[pl.ds(POS - 16, 16), :].astype(BF16)
    c_end[1] = c_pos[pl.ds(0, 16), :].astype(BF16)
    pl.semaphore_wait(barrier, len(greet))

    started = []

    def copy_of(a, b, s, r, to):
        return pltpu.make_async_remote_copy(
            src_ref=a, dst_ref=b, send_sem=s, recv_sem=r, device_id=to, device_id_type=MESH
        )

    def send(a, b, s, r, to):
        copy = copy_of(a, b, s, r, to)
        copy.start()
        started.append(copy)

    def arrived(b, r):
        copy_of(b, b, r, r, (lon, sib)).wait_recv()

    def c_block(r):
        return c_all.at[pl.ds(pl.multiple_of(r * OWN_IN, 16), OWN_IN), :]

    width = FINE // PIECES

    def g_block(r, k):
        return g_all.at[pl.ds(pl.multiple_of(r * OWN_OUT, 16), OWN_OUT), pl.ds(k * width, width)]

    send(coarse, c_block(rank), cs.at[0], cr.at[0], (lon, cross))
    for n, side in enumerate(sides):
        for d in range(4):
            to = (side, lax.rem(rank + d, 4))
            send(c_end.at[n], ce_all.at[n, rank], es.at[0, n, d], er.at[0, n, d], to)
    send(coarse, c_block(rank), cs.at[1], cr.at[1], (lon, sib))
    loads[1].wait()
    g32[...] = cot_in[...].astype(F32).reshape(OWN_OUT * 16, 128)
    for r in range(2):
        for i in range(H):
            r_pos[pl.ds(8 * r + i, 128, stride=16), :] = g32[pl.ds(2 * i + r, OWN_OUT, stride=16), :].T
    for n in range(16):
        cot[:, pl.ds(128 * n, 128)] = r_pos[pl.ds(128 * n, 128), :].T.astype(BF16)
    gap = jnp.zeros((16, 64 - OWN_OUT), F32)
    for n, at in enumerate((FINE - 32, 0)):
        two = [r_pos[pl.ds(at, 16), :], gap, r_pos[pl.ds(at + 16, 16), :], gap]
        g_end[n] = jnp.concatenate(two, 1).astype(BF16)
    for n, side in enumerate(sides):
        for d in range(4):
            to = (side, lax.rem(rank + d, 4))
            send(g_end.at[n], ge_all.at[n, rank], es.at[1, n, d], er.at[1, n, d], to)
    for k in range(PIECES):
        own_part = cot.at[:, pl.ds(k * width, width)]
        send(own_part, g_block(rank, k), gs.at[0, k], gr.at[0, k], (lon, cross))
        send(own_part, g_block(rank, k), gs.at[1, k], gr.at[1, k], (lon, sib))
    c_all[pl.ds(pl.multiple_of(rank * OWN_IN, 16), OWN_IN), :] = coarse[...]
    g_all[pl.ds(pl.multiple_of(rank * OWN_OUT, 16), OWN_OUT), :] = cot[...]

    def pass_on(k):
        arrived(g_block(cross, k), gr.at[0, k])
        send(g_block(cross, k), g_block(cross, k), gs.at[2, k], gr.at[2, k], (lon, sib))

    pad = jnp.zeros((132, 16, 64), BF16)
    for m in range(3):
        cots[:, :, pl.ds(256 * m + COUT, 64)] = pad
    conv_t[...] = jnp.zeros(conv_t.shape, BF16)
    cot3[pl.ds(OWN_OUT, OWN_OUT), :] = cot[...]
    for m in (0, 2):
        for r in range(2):
            for i in range(H):
                p = 2 * i + r + m - 1
                rows = pl.ds(8 * r + i, 128, stride=16)
                if 0 <= p < 16:
                    r_pos[rows, :] = g32[pl.ds(p, OWN_OUT, stride=16), :].T
                else:
                    r_pos[rows, :] = jnp.zeros((128, OWN_OUT), F32)
        for n in range(16):
            cot3[pl.ds(OWN_OUT * m, OWN_OUT), pl.ds(128 * n, 128)] = r_pos[pl.ds(128 * n, 128), :].T.astype(BF16)

    for load in loads[2:]:
        load.wait()
    own_bias = jnp.zeros((1, OWN_OUT), F32)
    for r in range(4):
        own_bias += jnp.where(rank == r, conv_b[:, pl.ds(OWN_OUT * r, OWN_OUT)], 0.0)
    a_of = lax.broadcasted_iota(jnp.int32, (COUT, OWN_OUT), 0)
    b_of = lax.broadcasted_iota(jnp.int32, (COUT, OWN_OUT), 1)
    pick = (a_of == b_of + OWN_OUT * rank).astype(F32).astype(BF16)
    for t in range(9):
        w = conv_w[t // 3, t % 3]
        mine[t] = nn(w, pick).astype(BF16)
        conv_t[pl.ds(768 * (t % 3) + 256 * (2 - t // 3), COUT), :] = w.astype(F32).T.astype(BF16)

    arrived(c_block(cross), cr.at[0])
    send(c_block(cross), c_block(cross), cs.at[2], cr.at[2], (lon, sib))
    a_of = lax.broadcasted_iota(jnp.int32, (CIN, OWN_IN), 0)
    b_of = lax.broadcasted_iota(jnp.int32, (CIN, OWN_IN), 1)
    pick = (a_of == b_of + OWN_IN * rank).astype(F32).astype(BF16)
    for t in range(16):
        own_up[t] = nn(up_w[t // 4, t % 4], pick).astype(BF16)
    for n in range(2):
        for d in range(4):
            arrived(ce_all.at[n, lax.rem(rank + 4 - d, 4)], er.at[0, n, d])
    arrived(c_block(sib), cr.at[1])
    arrived(c_block(diag), cr.at[2])
    for b in range(4):
        xf[pl.ds(1 + 16 * b, 16)] = c_all[:, pl.ds(128 * b, 128)].astype(F32).T.reshape(16, H, CIN)
    left, right = [
        jnp.concatenate([ce_all[n, r].astype(F32) for r in range(4)], 1) for n in range(2)
    ]
    xf[0] = left[8:]
    xf[65] = right[:8]
    xf[66:68] = jnp.zeros((2, H, CIN), F32)

    @pl.loop(0, 3)
    def _(n):
        t0 = n * 22
        rows = pl.ds(pl.multiple_of(t0 * H, 16), 22 * H)
        for d in range(2):
            v = xf[pl.ds(t0 + 1 - d, 22)]
            for s, w in enumerate((down(v), v, up(v))):
                xl[rows, pl.ds((2 * s + d) * CIN, CIN)] = w.reshape(22 * H, CIN).astype(BF16)

    pass_on(0)
    for rp in range(2):
        for cp in range(2):
            taps = ((3, 1), (2, 0))[rp]
            w = jnp.concatenate([up_w[ky, cp + 2 * d] for ky in taps for d in range(2)], 1)
            val = nt(xl[:, pl.ds(rp * 2 * CIN, 4 * CIN)], w)
            pre[:, cp, rp] = val.reshape(66, H, COUT)
        pass_on(1 + rp)

    bias = up_b[...].reshape(1, 1, 1, 1, COUT)

    def activate(n):
        ts = pl.ds(n * 3, 3)
        v = pre[ts] + bias
        s = jax.nn.sigmoid(v)
        fs[ts] = s * (1.0 + v * (1.0 - s))
        h = (v * s).astype(BF16).astype(F32).reshape(6, 2, H, COUT)
        for m, w in enumerate(shifted(h)):
            hid[m, pl.ds(n * 6, 6)] = w

    pl.loop(0, 11)(activate)
    pass_on(3)
    pl.loop(11, 22)(activate)

    def along_x(chunk, p, which):
        send(part.at[chunk, p], rx1.at[p, which], x1s.at[p, which], x1r.at[p, which],
             dev(first(p), z, y))

    def spot(b):
        return b // 4, 6 + b % 4 // 2, pl.ds(b % 2 * OWN_OUT, OWN_OUT)

    def put(b, v):
        c, p, rows = spot(b)
        part[c, p, rows, :] = v.astype(BF16)

    tails = []
    taps = [nn(cot3[...], hid[1, pl.ds(kx, 128)].reshape(FINE, COUT)) for kx in range(3)]
    for t in range(9):
        g = taps[t % 3][OWN_OUT * (2 - t // 3):OWN_OUT * (3 - t // 3)]
        put(t, g[:, :128])
        tails.append(g[:, 128:])
    tails.append(jnp.zeros((OWN_OUT, 64), F32))
    for u in range(5):
        put(9 + u, jnp.concatenate(tails[2 * u:2 * u + 2], 1))
    for b in (14, 15):
        put(b, jnp.zeros((OWN_OUT, 128), F32))
    for p in (6, 7):
        along_x(xo, p, 1)
        along_x(first(p), p, 0)

    def place_cot(at, v, n):
        for m, w in enumerate(shifted(v.reshape(n, 2, H, COUT))):
            cots[pl.ds(at, n), :, pl.ds(256 * m, COUT)] = w

    def place_edge(n):
        for d in range(4):
            arrived(ge_all.at[n, lax.rem(rank + 4 - d, 4)], er.at[1, n, d])
        cols = []
        for h in (0, 64):
            block = [ge_all[n, r][:, h:h + OWN_OUT].astype(F32) for r in range(4)]
            cols.append(jnp.concatenate(block, 1))
        place_cot(130 * n, jnp.concatenate(cols, 0), 2)

    def place_piece(k):
        arrived(g_block(sib, k), gr.at[1, k])
        arrived(g_block(diag, k), gr.at[2, k])
        for b in range(4 * k, 4 * k + 4):
            place_cot(2 + 8 * b, g_all[:, pl.ds(128 * b, 128)].astype(F32).T, 8)

    def adjoint(n):
        g = [cots[pl.ds(n * 26 + 2 - kx, 26)].reshape(416, 768) for kx in range(3)]
        acc = nn(jnp.concatenate(g, 1), conv_t[...])
        ts = pl.ds(n * 13, 13)
        d = (acc.reshape(13, 2, 2, H, COUT) * fs[ts]).astype(BF16).astype(F32)
        for cp in range(2):
            even, odd = d[:, cp, 0], d[:, cp, 1]
            for ky, v in enumerate((down(odd), even, odd, up(even))):
                df[cp, ky, ts] = v

    place_edge(0)
    place_piece(0)
    place_piece(1)
    pl.loop(0, 2)(adjoint)
    place_edge(1)
    place_piece(2)
    place_piece(3)
    pl.loop(2, 5)(adjoint)

    def window(ky, kx):
        return df[kx % 2, ky, pl.ds(kx // 2, 64)].reshape(POS, COUT).astype(BF16)

    for ky in (xo, xa, xb, x):
        for pair in range(2):
            a, b = [nn(coarse[...], window(ky, kx)) for kx in (2 * pair, 2 * pair + 1)]
            slabs = (a[:, :128], jnp.concatenate([a[:, 128:], b[:, :64]], 1), b[:, 64:])
            for n, slab in enumerate(slabs):
                p = 3 * pair + n
                part[ky, p] = slab.astype(BF16)
                if ky is xo:
                    along_x(xo, p, 1)
                elif ky is (xa, xb)[p % 2]:
                    along_x(ky, p, 0)

    for d in far_first:
        zz = lax.rem(z + d, nz)
        q = second(zz)
        for which in range(2):
            arrived(rx1.at[zz, which], x1r.at[zz, which])
        kept[d] = part[x, zz].astype(F32) + rx1[zz, 0].astype(F32)
        sb1[d] = (part[q, zz].astype(F32) + rx1[zz, 1].astype(F32)).astype(BF16)
        send(sb1.at[d], rx2.at[d], x2s.at[d], x2r.at[d], dev(q, z, y))

    total = None
    for t in range(16):
        term = nn(window(t // 4, t % 4), own_up[t])
        total = term if total is None else total + term
    c_pos[...] = total

    def refine(n):
        acc = None
        for t in range(9):
            term = nn(hid[t // 3, pl.ds(16 * n + t % 3, 16)].reshape(256, COUT), mine[t])
            acc = term if acc is None else acc + term
        r_pos[pl.ds(256 * n, 256), :] = acc + own_bias

    for n in range(4):
        refine(n)

    for d in far_first:
        arrived(rx2.at[d], x2r.at[d])
        acc = kept[d] + rx2[d].astype(F32)
        if d > 0:
            sb2[d] = acc.astype(BF16)
            send(sb2.at[d], rz.at[d], zs_s.at[d], zs_r.at[d], zdev[d])
        else:
            kept[0] = acc
    for n in range(4, 8):
        refine(n)
    acc = kept[0]
    for d in near_first[1:]:
        arrived(rz.at[d], zs_r.at[d])
        acc = acc + rz[d].astype(F32)
    ys[...] = acc
    send(ys, yr, y_sem.at[0], y_sem.at[1], ydev)
    arrived(yr, y_sem.at[1])
    res[x, z] = (acc + yr[...]).astype(BF16)
    here = res.at[x, z]
    for d in near_first[1:]:
        send(here, here, azs.at[d], azr.at[d], zdev[d])

    def direct(d):
        return d == nz // 2

    def spread_x(d):
        zz = lax.rem(z + nz - d, nz)
        got = res.at[x, zz]
        if d > 0:
            arrived(got, azr.at[d])
        if direct(d):
            send(got, got, axs.at[2, d], axr.at[2, d], dev(xo, z, y))
        send(got, got, axs.at[0, d], axr.at[0, d], dev(second(zz), z, y))
        send(got, got, axs.at[1, d], axr.at[1, d], dev(first(zz), z, y))

    def forward_x(d):
        zz = lax.rem(z + nz - d, nz)
        got = res.at[second(zz), zz]
        arrived(got, axr.at[0, d])
        if not direct(d):
            send(got, got, axs.at[2, d], axr.at[2, d], dev(first(zz), z, y))

    lag = 3
    for n in range(nz + lag):
        if n < nz:
            spread_x(near_first[n])
        if n == 0:
            for r in range(2):
                for i in range(H):
                    g32[pl.ds(2 * i + r, OWN_OUT, stride=16), :] = r_pos[pl.ds(8 * r + i, 128, stride=16), :].T
            refined[...] = g32[...].reshape(OWN_OUT, 16, 128).astype(BF16)
            for i in range(H):
                c_grad[i] = c_pos[pl.ds(i, WC, stride=H), :].astype(BF16)
        if n >= lag:
            forward_x(near_first[n - lag])
    for d in near_first:
        zz = lax.rem(z + nz - d, nz)
        arrived(res.at[first(zz), zz], axr.at[1, d])
        arrived(res.at[xo, zz], axr.at[2, d])
    for copy in started:
        copy.wait_send()


def strip(dims, *args):
    nx, nz, ny = dims
    dma = pltpu.SemaphoreType.DMA
    vm = pltpu.VMEM
    any_ = pl.BlockSpec(memory_space=pl.ANY)
    return pl.pallas_call(
        functools.partial(kernel, dims),
        out_shape=(
            jax.ShapeDtypeStruct((OWN_OUT, 2 * H, 2 * WC), BF16),
            jax.ShapeDtypeStruct((H, WC, OWN_IN), BF16),
            jax.ShapeDtypeStruct((nx, nz, PIECE, 128), BF16),
        ),
        in_specs=[any_] * 4 + [VM] * 2,
        out_specs=[VM] * 3,
        scratch_shapes=[
            vm((H, WC, OWN_IN), BF16),
            vm((OWN_OUT, 2 * H, 2 * WC), BF16),
            vm((OWN_IN, POS), BF16),
            vm((OWN_OUT, FINE), BF16),
            vm((3 * OWN_OUT, FINE), BF16),
            vm((2, 16, OWN_IN), BF16),
            vm((2, 16, 128), BF16),
            vm((OWN_OUT * 2 * H, 2 * WC), F32),
            vm((CIN, POS), BF16),
            vm((COUT, FINE), BF16),
            vm((2, 4, 16, OWN_IN), BF16),
            vm((2, 4, 16, 128), BF16),
            vm((4, 4, COUT, CIN), BF16),
            vm((3, 3, COUT, COUT), BF16),
            vm((9 * 256, COUT), BF16),
            vm((9, COUT, OWN_OUT), BF16),
            vm((16, COUT, OWN_IN), BF16),
            vm((68, H, CIN), F32),
            vm((528, 6 * CIN), BF16),
            vm((66, 2, 2, H, COUT), F32),
            vm((66, 2, 2, H, COUT), F32),
            vm((3, 132, 16, COUT), BF16),
            vm((132, 16, 3 * 256), BF16),
            vm((2, 4, 66, H, COUT), F32),
            vm((nx, nz, PIECE, 128), BF16),
            vm((FINE, OWN_OUT), F32),
            vm((POS, OWN_IN), F32),
            vm((nz, 2, PIECE, 128), BF16),
            vm((nz, PIECE, 128), F32),
            vm((nz, PIECE, 128), BF16),
            vm((nz, PIECE, 128), BF16),
            vm((nz, PIECE, 128), BF16),
            vm((nz, PIECE, 128), BF16),
            vm((PIECE, 128), F32),
            vm((PIECE, 128), F32),
            dma((4,)), dma((3,)), dma((3,)), dma((3, PIECES)), dma((3, PIECES)), dma((2, 2, 4)), dma((2, 2, 4)),
            dma((nz, 2)), dma((nz, 2)), dma((nz,)), dma((nz,)), dma((nz,)), dma((nz,)), dma((2,)),
            dma((nz,)), dma((nz,)), dma((3, nz)), dma((3, nz)),
        ],
        compiler_params=pltpu.CompilerParams(
            collective_id=0, has_side_effects=True, vmem_limit_bytes=LIMIT
        ),
        name="strip",
    )(*args)


def unpack_kernel(refined, c_grad, sums, refined_out, c_out, up_grad, conv_grad, ref, cg, src, up, conv, sems, out_sems):
    nx = sums.shape[0]
    loads = [pltpu.make_async_copy(sums.at[k], src.at[k], sems.at[k]) for k in range(nx)]
    loads += [
        pltpu.make_async_copy(refined, ref, sems.at[nx]),
        pltpu.make_async_copy(c_grad, cg, sems.at[nx + 1]),
    ]
    for copy in loads:
        copy.start()
    passes = [
        pltpu.make_async_copy(ref, refined_out, out_sems.at[nx]),
        pltpu.make_async_copy(cg, c_out, out_sems.at[nx + 1]),
    ]
    for ky in range(4):
        loads[ky].wait()
        for pair in range(2):
            a, m, b = [src[ky, 3 * pair + n].astype(F32) for n in range(3)]
            up[ky, 2 * pair] = jnp.concatenate([a, m[:, :64]], 1)
            up[ky, 2 * pair + 1] = jnp.concatenate([m[:, 64:], b], 1)
        copy = pltpu.make_async_copy(up.at[ky], up_grad.at[ky], out_sems.at[ky])
        copy.start()
        passes.append(copy)

    for load, copy in zip(loads[nx:], passes):
        load.wait()
        copy.start()

    def block(b):
        return src[b // 4, 6 + b % 4 // 2, pl.ds(b % 2 * OWN_OUT, OWN_OUT), :].astype(F32)

    for t in range(9):
        tail = block(9 + t // 2)[:, 64 * (t % 2):64 * (t % 2) + 64]
        conv[t // 3, t % 3] = jnp.concatenate([block(t), tail], 1)
    copy = pltpu.make_async_copy(conv, conv_grad, out_sems.at[nx + 2])
    copy.start()
    for copy in passes + [copy]:
        copy.wait()


def unpack(refined, c_grad, sums):
    any_ = pl.BlockSpec(memory_space=pl.ANY)
    up = (4, 4, OWN_IN, COUT)
    conv = (3, 3, OWN_OUT, COUT)
    return pl.pallas_call(
        unpack_kernel,
        out_shape=(
            jax.ShapeDtypeStruct(refined.shape, BF16),
            jax.ShapeDtypeStruct(c_grad.shape, BF16),
            jax.ShapeDtypeStruct(up, F32),
            jax.ShapeDtypeStruct(conv, F32),
        ),
        in_specs=[any_] * 3,
        out_specs=[any_] * 4,
        scratch_shapes=[
            pltpu.VMEM(refined.shape, BF16),
            pltpu.VMEM(c_grad.shape, BF16),
            pltpu.VMEM(sums.shape, BF16),
            pltpu.VMEM(up, F32),
            pltpu.VMEM(conv, F32),
            pltpu.SemaphoreType.DMA((6,)),
            pltpu.SemaphoreType.DMA((7,)),
        ],
        compiler_params=pltpu.CompilerParams(vmem_limit_bytes=LIMIT),
        name="unpack",
    )(refined, c_grad, sums)


def local(dims, coarse, up_weight, up_bias, conv_weight, conv_bias, cotangent):
    refined, c_grad, sums = strip(
        dims, coarse.transpose(1, 2, 0), cotangent, up_weight.transpose(0, 1, 3, 2), conv_weight,
        up_bias.reshape(1, COUT), conv_bias.reshape(1, COUT),
    )
    refined, c_grad, up_grad, conv_grad = unpack(refined, c_grad, sums)
    return refined, c_grad.transpose(2, 0, 1), up_grad, conv_grad.transpose(0, 1, 3, 2)


def solution(mesh):
    dims = (4, 8, 2)
    placed = (P("chan", None, "lon"), P(), P(), P(), P(), P("chan", None, "lon"))
    return jax.shard_map(
        functools.partial(local, dims),
        mesh=mesh,
        in_specs=placed,
        out_specs=(
            P("chan", None, "lon"),
            P("chan", None, "lon"),
            P(None, None, "chan", None),
            P(None, None, None, "chan"),
        ),
        check_vma=False,
    )
```

```python
import functools

import jax
import jax.numpy as jnp
from jax import lax
from jax.experimental import pallas as pl
from jax.experimental.pallas import tpu as pltpu
from jax.sharding import PartitionSpec as P

MESH = pl.DeviceIdType.MESH
F32, BF16 = jnp.float32, jnp.bfloat16
VM = pl.BlockSpec(memory_space=pltpu.VMEM)
CIN, COUT, H, WC = 384, 192, 8, 64
OWN_IN, OWN_OUT = CIN // 4, COUT // 4
POS, FINE = H * WC, 4 * H * WC
PIECE = 96
LIMIT = 60 << 20


def nn(a, b):
    return jnp.dot(a, b, preferred_element_type=F32)


def nt(a, b):
    return lax.dot_general(a, b, (((1,), (1,)), ((), ())), preferred_element_type=F32)


def down(v):
    row = lax.broadcasted_iota(jnp.int32, v.shape, v.ndim - 2)
    return jnp.where(row == 0, 0.0, pltpu.roll(v, 1, v.ndim - 2))


def up(v):
    row = lax.broadcasted_iota(jnp.int32, v.shape, v.ndim - 2)
    return jnp.where(row == H - 1, 0.0, pltpu.roll(v, H - 1, v.ndim - 2))


PIECES = 4


def shifted(v):
    even, odd = v[:, 0], v[:, 1]
    pairs = ((down(odd), even), (even, odd), (odd, up(even)))
    return [jnp.concatenate(pair, 1).astype(BF16) for pair in pairs]


def kernel(dims, coarse_hbm, cot_hbm, up_hbm, conv_hbm, up_b, conv_b,
           refined, c_grad, res,
           coarse_in, cot_in, coarse, cot, cot3, c_end, g_end, g32, c_all, g_all, ce_all, ge_all, up_w, conv_w, conv_t, mine, own_up,
           xf, xl, pre, fs, hid, cots, df, part, r_pos, c_pos,
           rx1, kept, sb1, rx2, sb2, rz, ys, yr,
           w_sem, cs, cr, gs, gr, es, er, x1s, x1r, x2s, x2r, zs_s, zs_r, y_sem,
           azs, azr, axs, axr):
    nx, nz, ny = dims
    lon, rank = lax.axis_index("lon"), lax.axis_index("chan")
    n_lon = nx * nz * ny
    x, z, y = lon // (nz * ny), lax.rem(lon // ny, nz), lax.rem(lon, ny)
    far, core = rank // 2, lax.rem(rank, 2)
    sib, cross = far * 2 + 1 - core, (1 - far) * 2 + core
    diag = (1 - far) * 2 + 1 - core
    sides = (lax.rem(lon + 1, n_lon), lax.rem(lon + n_lon - 1, n_lon))
    xa, xb = x + 1 - 2 * lax.rem(x, 2), 3 - x
    xo = lax.rem(x + 2, 4)

    def dev(px, pz, py):
        return ((px * nz + pz) * ny + py, rank)

    def first(zz):
        return xa + lax.rem(zz, 2) * (xb - xa)

    def second(zz):
        return xb + lax.rem(zz, 2) * (xa - xb)

    near_first = sorted(range(nz), key=lambda d: min(d, nz - d))
    far_first = near_first[::-1]
    zdev = [dev(x, lax.rem(z + d, nz), y) for d in range(nz)]
    ydev = dev(x, z, 1 - y)

    loads = [
        pltpu.make_async_copy(coarse_hbm, coarse_in, w_sem.at[0]),
        pltpu.make_async_copy(cot_hbm, cot_in, w_sem.at[1]),
        pltpu.make_async_copy(up_hbm, up_w, w_sem.at[2]),
        pltpu.make_async_copy(conv_hbm, conv_w, w_sem.at[3]),
    ]
    for load in loads:
        load.start()

    barrier = pltpu.get_barrier_semaphore()
    greet = [zdev[d] for d in far_first[:-1]]
    greet += [(side, lax.rem(rank + d, 4)) for side in sides for d in range(4)]
    greet += [dev(xo, z, y), dev(xa, z, y), dev(xb, z, y)]
    greet += [(lon, lax.rem(rank + d, 4)) for d in range(1, 4)]
    for peer in greet:
        pl.semaphore_signal(barrier, inc=1, device_id=peer, device_id_type=MESH)

    loads[0].wait()
    for i in range(H):
        c_pos[pl.ds(i, WC, stride=H), :] = coarse_in[i].astype(F32)
    for n in range(4):
        coarse[:, pl.ds(128 * n, 128)] = c_pos[pl.ds(128 * n, 128), :].T.astype(BF16)
    c_end[0] = c_pos[pl.ds(POS - 16, 16), :].astype(BF16)
    c_end[1] = c_pos[pl.ds(0, 16), :].astype(BF16)
    pl.semaphore_wait(barrier, len(greet))

    started = []

    def copy_of(a, b, s, r, to):
        return pltpu.make_async_remote_copy(
            src_ref=a, dst_ref=b, send_sem=s, recv_sem=r, device_id=to, device_id_type=MESH
        )

    def send(a, b, s, r, to):
        copy = copy_of(a, b, s, r, to)
        copy.start()
        started.append(copy)

    def arrived(b, r):
        copy_of(b, b, r, r, (lon, sib)).wait_recv()

    def c_block(r):
        return c_all.at[pl.ds(pl.multiple_of(r * OWN_IN, 16), OWN_IN), :]

    width = FINE // PIECES

    def g_block(r, k):
        return g_all.at[pl.ds(pl.multiple_of(r * OWN_OUT, 16), OWN_OUT), pl.ds(k * width, width)]

    send(coarse, c_block(rank), cs.at[0], cr.at[0], (lon, cross))
    for n, side in enumerate(sides):
        for d in range(4):
            to = (side, lax.rem(rank + d, 4))
            send(c_end.at[n], ce_all.at[n, rank], es.at[0, n, d], er.at[0, n, d], to)
    send(coarse, c_block(rank), cs.at[1], cr.at[1], (lon, sib))
    loads[1].wait()
    g32[...] = cot_in[...].astype(F32).reshape(OWN_OUT * 16, 128)
    for r in range(2):
        for i in range(H):
            r_pos[pl.ds(8 * r + i, 128, stride=16), :] = g32[pl.ds(2 * i + r, OWN_OUT, stride=16), :].T
    for n in range(16):
        cot[:, pl.ds(128 * n, 128)] = r_pos[pl.ds(128 * n, 128), :].T.astype(BF16)
    gap = jnp.zeros((16, 64 - OWN_OUT), F32)
    for n, at in enumerate((FINE - 32, 0)):
        two = [r_pos[pl.ds(at, 16), :], gap, r_pos[pl.ds(at + 16, 16), :], gap]
        g_end[n] = jnp.concatenate(two, 1).astype(BF16)
    for n, side in enumerate(sides):
        for d in range(4):
            to = (side, lax.rem(rank + d, 4))
            send(g_end.at[n], ge_all.at[n, rank], es.at[1, n, d], er.at[1, n, d], to)
    for k in range(PIECES):
        own_part = cot.at[:, pl.ds(k * width, width)]
        send(own_part, g_block(rank, k), gs.at[0, k], gr.at[0, k], (lon, cross))
        send(own_part, g_block(rank, k), gs.at[1, k], gr.at[1, k], (lon, sib))
    c_all[pl.ds(pl.multiple_of(rank * OWN_IN, 16), OWN_IN), :] = coarse[...]
    g_all[pl.ds(pl.multiple_of(rank * OWN_OUT, 16), OWN_OUT), :] = cot[...]

    def pass_on(k):
        arrived(g_block(cross, k), gr.at[0, k])
        send(g_block(cross, k), g_block(cross, k), gs.at[2, k], gr.at[2, k], (lon, sib))

    pad = jnp.zeros((132, 16, 64), BF16)
    for m in range(3):
        cots[:, :, pl.ds(256 * m + COUT, 64)] = pad
    conv_t[...] = jnp.zeros(conv_t.shape, BF16)
    cot3[pl.ds(OWN_OUT, OWN_OUT), :] = cot[...]
    for m in (0, 2):
        for r in range(2):
            for i in range(H):
                p = 2 * i + r + m - 1
                rows = pl.ds(8 * r + i, 128, stride=16)
                if 0 <= p < 16:
                    r_pos[rows, :] = g32[pl.ds(p, OWN_OUT, stride=16), :].T
                else:
                    r_pos[rows, :] = jnp.zeros((128, OWN_OUT), F32)
        for n in range(16):
            cot3[pl.ds(OWN_OUT * m, OWN_OUT), pl.ds(128 * n, 128)] = r_pos[pl.ds(128 * n, 128), :].T.astype(BF16)

    for load in loads[2:]:
        load.wait()
    own_bias = jnp.zeros((1, OWN_OUT), F32)
    for r in range(4):
        own_bias += jnp.where(rank == r, conv_b[:, pl.ds(OWN_OUT * r, OWN_OUT)], 0.0)
    for t in range(9):
        w = conv_w[t // 3, t % 3]
        conv_t[pl.ds(768 * (t % 3) + 256 * (2 - t // 3), COUT), :] = w.astype(F32).T.astype(BF16)

    arrived(c_block(cross), cr.at[0])
    send(c_block(cross), c_block(cross), cs.at[2], cr.at[2], (lon, sib))
    for n in range(2):
        for d in range(4):
            arrived(ce_all.at[n, lax.rem(rank + 4 - d, 4)], er.at[0, n, d])
    arrived(c_block(sib), cr.at[1])
    arrived(c_block(diag), cr.at[2])
    for b in range(4):
        xf[pl.ds(1 + 16 * b, 16)] = c_all[:, pl.ds(128 * b, 128)].astype(F32).T.reshape(16, H, CIN)
    left, right = [
        jnp.concatenate([ce_all[n, r].astype(F32) for r in range(4)], 1) for n in range(2)
    ]
    xf[0] = left[8:]
    xf[65] = right[:8]
    xf[66:68] = jnp.zeros((2, H, CIN), F32)

    @pl.loop(0, 3)
    def _(n):
        t0 = n * 22
        rows = pl.ds(pl.multiple_of(t0 * H, 16), 22 * H)
        for d in range(2):
            v = xf[pl.ds(t0 + 1 - d, 22)]
            for s, w in enumerate((down(v), v, up(v))):
                xl[rows, pl.ds((2 * s + d) * CIN, CIN)] = w.reshape(22 * H, CIN).astype(BF16)

    pass_on(0)
    for rp in range(2):
        for cp in range(2):
            taps = ((3, 1), (2, 0))[rp]
            w = jnp.concatenate([up_w[ky, cp + 2 * d] for ky in taps for d in range(2)], 1)
            val = nt(xl[:, pl.ds(rp * 2 * CIN, 4 * CIN)], w)
            pre[:, cp, rp] = val.reshape(66, H, COUT)
        pass_on(1 + rp)

    bias = up_b[...].reshape(1, 1, 1, 1, COUT)

    def activate(n):
        ts = pl.ds(n * 3, 3)
        v = pre[ts] + bias
        s = jax.nn.sigmoid(v)
        fs[ts] = s * (1.0 + v * (1.0 - s))
        h = (v * s).astype(BF16).astype(F32).reshape(6, 2, H, COUT)
        hid[1, pl.ds(n * 6, 6)] = h.reshape(6, 16, COUT).astype(BF16)

    pl.loop(0, 11)(activate)
    pass_on(3)
    pl.loop(11, 22)(activate)

    def along_x(chunk, p, which):
        send(part.at[chunk, p], rx1.at[p, which], x1s.at[p, which], x1r.at[p, which],
             dev(first(p), z, y))

    def spot(b):
        return b // 4, 6 + b % 4 // 2, pl.ds(b % 2 * OWN_OUT, OWN_OUT)

    def put(b, v):
        c, p, rows = spot(b)
        part[c, p, rows, :] = v.astype(BF16)

    tails = []
    taps = [nn(cot3[...], hid[1, pl.ds(kx, 128)].reshape(FINE, COUT)) for kx in range(3)]
    for t in range(9):
        g = taps[t % 3][OWN_OUT * (2 - t // 3):OWN_OUT * (3 - t // 3)]
        put(t, g[:, :128])
        tails.append(g[:, 128:])
    tails.append(jnp.zeros((OWN_OUT, 64), F32))
    for u in range(5):
        put(9 + u, jnp.concatenate(tails[2 * u:2 * u + 2], 1))
    for b in (14, 15):
        put(b, jnp.zeros((OWN_OUT, 128), F32))
    for p in (6, 7):
        along_x(xo, p, 1)
        along_x(first(p), p, 0)

    def place_cot(at, v, n):
        for m, w in enumerate(shifted(v.reshape(n, 2, H, COUT))):
            cots[pl.ds(at, n), :, pl.ds(256 * m, COUT)] = w

    def place_edge(n):
        for d in range(4):
            arrived(ge_all.at[n, lax.rem(rank + 4 - d, 4)], er.at[1, n, d])
        cols = []
        for h in (0, 64):
            block = [ge_all[n, r][:, h:h + OWN_OUT].astype(F32) for r in range(4)]
            cols.append(jnp.concatenate(block, 1))
        place_cot(130 * n, jnp.concatenate(cols, 0), 2)

    def place_piece(k):
        arrived(g_block(sib, k), gr.at[1, k])
        arrived(g_block(diag, k), gr.at[2, k])
        for b in range(4 * k, 4 * k + 4):
            place_cot(2 + 8 * b, g_all[:, pl.ds(128 * b, 128)].astype(F32).T, 8)

    def adjoint(n):
        g = [cots[pl.ds(n * 26 + 2 - kx, 26)].reshape(416, 768) for kx in range(3)]
        acc = nn(jnp.concatenate(g, 1), conv_t[...])
        ts = pl.ds(n * 13, 13)
        d = (acc.reshape(13, 2, 2, H, COUT) * fs[ts]).astype(BF16).astype(F32)
        for cp in range(2):
            even, odd = d[:, cp, 0], d[:, cp, 1]
            for ky, v in enumerate((down(odd), even, odd, up(even))):
                df[cp, ky, ts] = v

    place_edge(0)
    place_piece(0)
    place_piece(1)
    pl.loop(0, 2)(adjoint)
    place_edge(1)
    place_piece(2)
    place_piece(3)
    pl.loop(2, 5)(adjoint)

    def window(ky, kx):
        return df[kx % 2, ky, pl.ds(kx // 2, 64)].reshape(POS, COUT).astype(BF16)

    for ky in (xo, xa, xb, x):
        for pair in range(2):
            a, b = [nn(coarse[...], window(ky, kx)) for kx in (2 * pair, 2 * pair + 1)]
            slabs = (a[:, :128], jnp.concatenate([a[:, 128:], b[:, :64]], 1), b[:, 64:])
            for n, slab in enumerate(slabs):
                p = 3 * pair + n
                part[ky, p] = slab.astype(BF16)
                if ky is xo:
                    along_x(xo, p, 1)
                elif ky is (xa, xb)[p % 2]:
                    along_x(ky, p, 0)

    def picked(count, size):
        row = lax.broadcasted_iota(jnp.int32, (count, size), 0)
        col = lax.broadcasted_iota(jnp.int32, (count, size), 1)
        return (row == col + size * rank).astype(F32).astype(BF16)

    pick = picked(CIN, OWN_IN)
    for t in range(16):
        own_up[t] = nn(up_w[t // 4, t % 4], pick).astype(BF16)

    for d in far_first:
        zz = lax.rem(z + d, nz)
        q = second(zz)
        for which in range(2):
            arrived(rx1.at[zz, which], x1r.at[zz, which])
        kept[d] = part[x, zz].astype(F32) + rx1[zz, 0].astype(F32)
        sb1[d] = (part[q, zz].astype(F32) + rx1[zz, 1].astype(F32)).astype(BF16)
        send(sb1.at[d], rx2.at[d], x2s.at[d], x2r.at[d], dev(q, z, y))

    total = None
    for t in range(16):
        term = nn(window(t // 4, t % 4), own_up[t])
        total = term if total is None else total + term
    c_pos[...] = total

    pick = picked(COUT, OWN_OUT)
    for t in range(9):
        mine[t] = nn(conv_w[t // 3, t % 3], pick).astype(BF16)

    @pl.loop(0, 22)
    def _(n):
        v = hid[1, pl.ds(n * 6, 6)].astype(F32).reshape(6, 2, H, COUT)
        above, _, below = shifted(v)
        hid[0, pl.ds(n * 6, 6)] = above
        hid[2, pl.ds(n * 6, 6)] = below

    def refine(n):
        acc = None
        for t in range(9):
            term = nn(hid[t // 3, pl.ds(16 * n + t % 3, 16)].reshape(256, COUT), mine[t])
            acc = term if acc is None else acc + term
        r_pos[pl.ds(256 * n, 256), :] = acc + own_bias


    for d in far_first:
        arrived(rx2.at[d], x2r.at[d])
        acc = kept[d] + rx2[d].astype(F32)
        if d > 0:
            sb2[d] = acc.astype(BF16)
            send(sb2.at[d], rz.at[d], zs_s.at[d], zs_r.at[d], zdev[d])
        else:
            kept[0] = acc
    for n in range(8):
        refine(n)
    acc = kept[0]
    for d in near_first[1:]:
        arrived(rz.at[d], zs_r.at[d])
        acc = acc + rz[d].astype(F32)
    ys[...] = acc
    send(ys, yr, y_sem.at[0], y_sem.at[1], ydev)
    arrived(yr, y_sem.at[1])
    res[x, z] = (acc + yr[...]).astype(BF16)
    here = res.at[x, z]
    for d in near_first[1:]:
        send(here, here, azs.at[d], azr.at[d], zdev[d])

    def direct(d):
        return d == nz // 2

    def spread_x(d):
        zz = lax.rem(z + nz - d, nz)
        got = res.at[x, zz]
        if d > 0:
            arrived(got, azr.at[d])
        if direct(d):
            send(got, got, axs.at[2, d], axr.at[2, d], dev(xo, z, y))
        send(got, got, axs.at[0, d], axr.at[0, d], dev(second(zz), z, y))
        send(got, got, axs.at[1, d], axr.at[1, d], dev(first(zz), z, y))

    def forward_x(d):
        zz = lax.rem(z + nz - d, nz)
        got = res.at[second(zz), zz]
        arrived(got, axr.at[0, d])
        if not direct(d):
            send(got, got, axs.at[2, d], axr.at[2, d], dev(first(zz), z, y))

    lag = 3
    for n in range(nz + lag):
        if n < nz:
            spread_x(near_first[n])
        if n == 0:
            for r in range(2):
                for i in range(H):
                    g32[pl.ds(2 * i + r, OWN_OUT, stride=16), :] = r_pos[pl.ds(8 * r + i, 128, stride=16), :].T
            refined[...] = g32[...].reshape(OWN_OUT, 16, 128).astype(BF16)
            for i in range(H):
                c_grad[i] = c_pos[pl.ds(i, WC, stride=H), :].astype(BF16)
        if n >= lag:
            forward_x(near_first[n - lag])
    for d in near_first:
        zz = lax.rem(z + nz - d, nz)
        arrived(res.at[first(zz), zz], axr.at[1, d])
        arrived(res.at[xo, zz], axr.at[2, d])
    for copy in started:
        copy.wait_send()


def strip(dims, *args):
    nx, nz, ny = dims
    dma = pltpu.SemaphoreType.DMA
    vm = pltpu.VMEM
    any_ = pl.BlockSpec(memory_space=pl.ANY)
    return pl.pallas_call(
        functools.partial(kernel, dims),
        out_shape=(
            jax.ShapeDtypeStruct((OWN_OUT, 2 * H, 2 * WC), BF16),
            jax.ShapeDtypeStruct((H, WC, OWN_IN), BF16),
            jax.ShapeDtypeStruct((nx, nz, PIECE, 128), BF16),
        ),
        in_specs=[any_] * 4 + [VM] * 2,
        out_specs=[VM] * 3,
        scratch_shapes=[
            vm((H, WC, OWN_IN), BF16),
            vm((OWN_OUT, 2 * H, 2 * WC), BF16),
            vm((OWN_IN, POS), BF16),
            vm((OWN_OUT, FINE), BF16),
            vm((3 * OWN_OUT, FINE), BF16),
            vm((2, 16, OWN_IN), BF16),
            vm((2, 16, 128), BF16),
            vm((OWN_OUT * 2 * H, 2 * WC), F32),
            vm((CIN, POS), BF16),
            vm((COUT, FINE), BF16),
            vm((2, 4, 16, OWN_IN), BF16),
            vm((2, 4, 16, 128), BF16),
            vm((4, 4, COUT, CIN), BF16),
            vm((3, 3, COUT, COUT), BF16),
            vm((9 * 256, COUT), BF16),
            vm((9, COUT, OWN_OUT), BF16),
            vm((16, COUT, OWN_IN), BF16),
            vm((68, H, CIN), F32),
            vm((528, 6 * CIN), BF16),
            vm((66, 2, 2, H, COUT), F32),
            vm((66, 2, 2, H, COUT), F32),
            vm((3, 132, 16, COUT), BF16),
            vm((132, 16, 3 * 256), BF16),
            vm((2, 4, 66, H, COUT), F32),
            vm((nx, nz, PIECE, 128), BF16),
            vm((FINE, OWN_OUT), F32),
            vm((POS, OWN_IN), F32),
            vm((nz, 2, PIECE, 128), BF16),
            vm((nz, PIECE, 128), F32),
            vm((nz, PIECE, 128), BF16),
            vm((nz, PIECE, 128), BF16),
            vm((nz, PIECE, 128), BF16),
            vm((nz, PIECE, 128), BF16),
            vm((PIECE, 128), F32),
            vm((PIECE, 128), F32),
            dma((4,)), dma((3,)), dma((3,)), dma((3, PIECES)), dma((3, PIECES)), dma((2, 2, 4)), dma((2, 2, 4)),
            dma((nz, 2)), dma((nz, 2)), dma((nz,)), dma((nz,)), dma((nz,)), dma((nz,)), dma((2,)),
            dma((nz,)), dma((nz,)), dma((3, nz)), dma((3, nz)),
        ],
        compiler_params=pltpu.CompilerParams(
            collective_id=0, has_side_effects=True, vmem_limit_bytes=LIMIT
        ),
        name="strip",
    )(*args)


def unpack_kernel(refined, c_grad, sums, refined_out, c_out, up_grad, conv_grad, ref, cg, src, up, conv, sems, out_sems):
    nx = sums.shape[0]
    loads = [pltpu.make_async_copy(sums.at[k], src.at[k], sems.at[k]) for k in range(nx)]
    loads += [
        pltpu.make_async_copy(refined, ref, sems.at[nx]),
        pltpu.make_async_copy(c_grad, cg, sems.at[nx + 1]),
    ]
    for copy in loads:
        copy.start()
    passes = [
        pltpu.make_async_copy(ref, refined_out, out_sems.at[nx]),
        pltpu.make_async_copy(cg, c_out, out_sems.at[nx + 1]),
    ]
    for ky in range(4):
        loads[ky].wait()
        for pair in range(2):
            a, m, b = [src[ky, 3 * pair + n].astype(F32) for n in range(3)]
            up[ky, 2 * pair] = jnp.concatenate([a, m[:, :64]], 1)
            up[ky, 2 * pair + 1] = jnp.concatenate([m[:, 64:], b], 1)
        copy = pltpu.make_async_copy(up.at[ky], up_grad.at[ky], out_sems.at[ky])
        copy.start()
        passes.append(copy)

    for load, copy in zip(loads[nx:], passes):
        load.wait()
        copy.start()

    def block(b):
        return src[b // 4, 6 + b % 4 // 2, pl.ds(b % 2 * OWN_OUT, OWN_OUT), :].astype(F32)

    for t in range(9):
        tail = block(9 + t // 2)[:, 64 * (t % 2):64 * (t % 2) + 64]
        conv[t // 3, t % 3] = jnp.concatenate([block(t), tail], 1)
    copy = pltpu.make_async_copy(conv, conv_grad, out_sems.at[nx + 2])
    copy.start()
    for copy in passes + [copy]:
        copy.wait()


def unpack(refined, c_grad, sums):
    any_ = pl.BlockSpec(memory_space=pl.ANY)
    up = (4, 4, OWN_IN, COUT)
    conv = (3, 3, OWN_OUT, COUT)
    return pl.pallas_call(
        unpack_kernel,
        out_shape=(
            jax.ShapeDtypeStruct(refined.shape, BF16),
            jax.ShapeDtypeStruct(c_grad.shape, BF16),
            jax.ShapeDtypeStruct(up, F32),
            jax.ShapeDtypeStruct(conv, F32),
        ),
        in_specs=[any_] * 3,
        out_specs=[any_] * 4,
        scratch_shapes=[
            pltpu.VMEM(refined.shape, BF16),
            pltpu.VMEM(c_grad.shape, BF16),
            pltpu.VMEM(sums.shape, BF16),
            pltpu.VMEM(up, F32),
            pltpu.VMEM(conv, F32),
            pltpu.SemaphoreType.DMA((6,)),
            pltpu.SemaphoreType.DMA((7,)),
        ],
        compiler_params=pltpu.CompilerParams(vmem_limit_bytes=LIMIT),
        name="unpack",
    )(refined, c_grad, sums)


def local(dims, coarse, up_weight, up_bias, conv_weight, conv_bias, cotangent):
    refined, c_grad, sums = strip(
        dims, coarse.transpose(1, 2, 0), cotangent, up_weight.transpose(0, 1, 3, 2), conv_weight,
        up_bias.reshape(1, COUT), conv_bias.reshape(1, COUT),
    )
    refined, c_grad, up_grad, conv_grad = unpack(refined, c_grad, sums)
    return refined, c_grad.transpose(2, 0, 1), up_grad, conv_grad.transpose(0, 1, 3, 2)


def solution(mesh):
    dims = (4, 8, 2)
    placed = (P("chan", None, "lon"), P(), P(), P(), P(), P("chan", None, "lon"))
    return jax.shard_map(
        functools.partial(local, dims),
        mesh=mesh,
        in_specs=placed,
        out_specs=(
            P("chan", None, "lon"),
            P("chan", None, "lon"),
            P(None, None, "chan", None),
            P(None, None, None, "chan"),
        ),
        check_vma=False,
    )
```

```python
import functools

import jax
import jax.numpy as jnp
from jax import lax
from jax.experimental import pallas as pl
from jax.experimental.pallas import tpu as pltpu
from jax.sharding import PartitionSpec as P

MESH = pl.DeviceIdType.MESH
F32, BF16 = jnp.float32, jnp.bfloat16
VM = pl.BlockSpec(memory_space=pltpu.VMEM)
CIN, COUT, H, WC = 384, 192, 8, 64
OWN_IN, OWN_OUT = CIN // 4, COUT // 4
POS, FINE = H * WC, 4 * H * WC
PIECE = 96
LIMIT = 60 << 20


def nn(a, b):
    return jnp.dot(a, b, preferred_element_type=F32)


def nt(a, b):
    return lax.dot_general(a, b, (((1,), (1,)), ((), ())), preferred_element_type=F32)


def down(v):
    row = lax.broadcasted_iota(jnp.int32, v.shape, v.ndim - 2)
    return jnp.where(row == 0, 0.0, pltpu.roll(v, 1, v.ndim - 2))


def up(v):
    row = lax.broadcasted_iota(jnp.int32, v.shape, v.ndim - 2)
    return jnp.where(row == H - 1, 0.0, pltpu.roll(v, H - 1, v.ndim - 2))


PIECES = 4


def shifted(v):
    even, odd = v[:, 0], v[:, 1]
    pairs = ((down(odd), even), (even, odd), (odd, up(even)))
    return [jnp.concatenate(pair, 1).astype(BF16) for pair in pairs]


def kernel(dims, coarse_hbm, cot_hbm, up_hbm, conv_hbm, up_b_hbm, conv_b_hbm,
           refined, c_grad, res,
           up_b, conv_b, coarse_in, cot_in, coarse, cot, cot3, c_end, g_end, g32, c_all, g_all, ce_all, ge_all, up_w, conv_w, conv_t, mine, own_up,
           xf, xl, pre, fs, hid, cots, df, part, r_pos, c_pos,
           rx1, kept, sb2, rz, ys, yr,
           w_sem, cs, cr, gs, gr, es, er, x1s, x1r, zs_s, zs_r, y_sem,
           azs, azr, axs, axr):
    nx, nz, ny = dims
    lon, rank = lax.axis_index("lon"), lax.axis_index("chan")
    n_lon = nx * nz * ny
    x, z, y = lon // (nz * ny), lax.rem(lon // ny, nz), lax.rem(lon, ny)
    far, core = rank // 2, lax.rem(rank, 2)
    sib, cross = far * 2 + 1 - core, (1 - far) * 2 + core
    diag = (1 - far) * 2 + 1 - core
    sides = (lax.rem(lon + 1, n_lon), lax.rem(lon + n_lon - 1, n_lon))
    xa, xb = x + 1 - 2 * lax.rem(x, 2), 3 - x
    xo = lax.rem(x + 2, 4)

    def dev(px, pz, py):
        return ((px * nz + pz) * ny + py, rank)

    def first(zz):
        return xa + lax.rem(zz, 2) * (xb - xa)

    def second(zz):
        return xb + lax.rem(zz, 2) * (xa - xb)

    near_first = sorted(range(nz), key=lambda d: min(d, nz - d))
    far_first = near_first[::-1]
    zdev = [dev(x, lax.rem(z + d, nz), y) for d in range(nz)]
    ydev = dev(x, z, 1 - y)

    loads = [
        pltpu.make_async_copy(coarse_hbm, coarse_in, w_sem.at[0]),
        pltpu.make_async_copy(cot_hbm, cot_in, w_sem.at[1]),
        pltpu.make_async_copy(up_hbm, up_w, w_sem.at[2]),
        pltpu.make_async_copy(conv_hbm, conv_w, w_sem.at[3]),
        pltpu.make_async_copy(up_b_hbm, up_b, w_sem.at[4]),
        pltpu.make_async_copy(conv_b_hbm, conv_b, w_sem.at[5]),
    ]
    for load in loads:
        load.start()

    barrier = pltpu.get_barrier_semaphore()
    greet = [zdev[d] for d in far_first[:-1]]
    greet += [(side, lax.rem(rank + d, 4)) for side in sides for d in range(4)]
    greet += [dev(xo, z, y), dev(xa, z, y), dev(xb, z, y)]
    greet += [(lon, lax.rem(rank + d, 4)) for d in range(1, 4)]
    for peer in greet:
        pl.semaphore_signal(barrier, inc=1, device_id=peer, device_id_type=MESH)

    loads[0].wait()
    for i in range(H):
        c_pos[pl.ds(i, WC, stride=H), :] = coarse_in[i].astype(F32)
    for n in range(4):
        coarse[:, pl.ds(128 * n, 128)] = c_pos[pl.ds(128 * n, 128), :].T.astype(BF16)
    c_end[0] = c_pos[pl.ds(POS - 16, 16), :].astype(BF16)
    c_end[1] = c_pos[pl.ds(0, 16), :].astype(BF16)
    pl.semaphore_wait(barrier, len(greet))

    started = []

    def copy_of(a, b, s, r, to):
        return pltpu.make_async_remote_copy(
            src_ref=a, dst_ref=b, send_sem=s, recv_sem=r, device_id=to, device_id_type=MESH
        )

    def send(a, b, s, r, to):
        copy = copy_of(a, b, s, r, to)
        copy.start()
        started.append(copy)

    def arrived(b, r):
        copy_of(b, b, r, r, (lon, sib)).wait_recv()

    def c_block(r):
        return c_all.at[pl.ds(pl.multiple_of(r * OWN_IN, 16), OWN_IN), :]

    width = FINE // PIECES

    def g_block(r, k):
        return g_all.at[pl.ds(pl.multiple_of(r * OWN_OUT, 16), OWN_OUT), pl.ds(k * width, width)]

    send(coarse, c_block(rank), cs.at[0], cr.at[0], (lon, cross))
    for n, side in enumerate(sides):
        for d in range(4):
            to = (side, lax.rem(rank + d, 4))
            send(c_end.at[n], ce_all.at[n, rank], es.at[0, n, d], er.at[0, n, d], to)
    send(coarse, c_block(rank), cs.at[1], cr.at[1], (lon, sib))
    loads[1].wait()
    g32[...] = cot_in[...].astype(F32).reshape(OWN_OUT * 16, 128)
    for r in range(2):
        for i in range(H):
            r_pos[pl.ds(8 * r + i, 128, stride=16), :] = g32[pl.ds(2 * i + r, OWN_OUT, stride=16), :].T
    for n in range(16):
        cot[:, pl.ds(128 * n, 128)] = r_pos[pl.ds(128 * n, 128), :].T.astype(BF16)
    gap = jnp.zeros((16, 64 - OWN_OUT), F32)
    for n, at in enumerate((FINE - 32, 0)):
        two = [r_pos[pl.ds(at, 16), :], gap, r_pos[pl.ds(at + 16, 16), :], gap]
        g_end[n] = jnp.concatenate(two, 1).astype(BF16)
    for n, side in enumerate(sides):
        for d in range(4):
            to = (side, lax.rem(rank + d, 4))
            send(g_end.at[n], ge_all.at[n, rank], es.at[1, n, d], er.at[1, n, d], to)
    for k in range(PIECES):
        own_part = cot.at[:, pl.ds(k * width, width)]
        send(own_part, g_block(rank, k), gs.at[0, k], gr.at[0, k], (lon, cross))
        send(own_part, g_block(rank, k), gs.at[1, k], gr.at[1, k], (lon, sib))
    c_all[pl.ds(pl.multiple_of(rank * OWN_IN, 16), OWN_IN), :] = coarse[...]
    g_all[pl.ds(pl.multiple_of(rank * OWN_OUT, 16), OWN_OUT), :] = cot[...]

    def pass_on(k):
        arrived(g_block(cross, k), gr.at[0, k])
        send(g_block(cross, k), g_block(cross, k), gs.at[2, k], gr.at[2, k], (lon, sib))

    pad = jnp.zeros((132, 16, 64), BF16)
    for m in range(3):
        cots[:, :, pl.ds(256 * m + COUT, 64)] = pad
    conv_t[...] = jnp.zeros(conv_t.shape, BF16)
    cot3[pl.ds(OWN_OUT, OWN_OUT), :] = cot[...]
    for m in (0, 2):
        for r in range(2):
            for i in range(H):
                p = 2 * i + r + m - 1
                rows = pl.ds(8 * r + i, 128, stride=16)
                if 0 <= p < 16:
                    r_pos[rows, :] = g32[pl.ds(p, OWN_OUT, stride=16), :].T
                else:
                    r_pos[rows, :] = jnp.zeros((128, OWN_OUT), F32)
        for n in range(16):
            cot3[pl.ds(OWN_OUT * m, OWN_OUT), pl.ds(128 * n, 128)] = r_pos[pl.ds(128 * n, 128), :].T.astype(BF16)

    for load in loads[2:]:
        load.wait()
    own_bias = jnp.zeros((1, OWN_OUT), F32)
    for r in range(4):
        own_bias += jnp.where(rank == r, conv_b[:, pl.ds(OWN_OUT * r, OWN_OUT)], 0.0)
    for t in range(9):
        w = conv_w[t // 3, t % 3]
        conv_t[pl.ds(768 * (t % 3) + 256 * (2 - t // 3), COUT), :] = w.astype(F32).T.astype(BF16)

    arrived(c_block(cross), cr.at[0])
    send(c_block(cross), c_block(cross), cs.at[2], cr.at[2], (lon, sib))
    for n in range(2):
        for d in range(4):
            arrived(ce_all.at[n, lax.rem(rank + 4 - d, 4)], er.at[0, n, d])
    arrived(c_block(sib), cr.at[1])
    arrived(c_block(diag), cr.at[2])
    for b in range(4):
        xf[pl.ds(1 + 16 * b, 16)] = c_all[:, pl.ds(128 * b, 128)].astype(F32).T.reshape(16, H, CIN)
    left, right = [
        jnp.concatenate([ce_all[n, r].astype(F32) for r in range(4)], 1) for n in range(2)
    ]
    xf[0] = left[8:]
    xf[65] = right[:8]
    xf[66:68] = jnp.zeros((2, H, CIN), F32)

    @pl.loop(0, 3)
    def _(n):
        t0 = n * 22
        rows = pl.ds(pl.multiple_of(t0 * H, 16), 22 * H)
        for d in range(2):
            v = xf[pl.ds(t0 + 1 - d, 22)]
            for s, w in enumerate((down(v), v, up(v))):
                xl[rows, pl.ds((2 * s + d) * CIN, CIN)] = w.reshape(22 * H, CIN).astype(BF16)

    pass_on(0)
    for rp in range(2):
        for cp in range(2):
            taps = ((3, 1), (2, 0))[rp]
            w = jnp.concatenate([up_w[ky, cp + 2 * d] for ky in taps for d in range(2)], 1)
            val = nt(xl[:, pl.ds(rp * 2 * CIN, 4 * CIN)], w)
            pre[:, cp, rp] = val.reshape(66, H, COUT)
        pass_on(1 + rp)

    bias = up_b[...].reshape(1, 1, 1, 1, COUT)

    def activate(n):
        ts = pl.ds(n * 3, 3)
        v = pre[ts] + bias
        s = jax.nn.sigmoid(v)
        fs[ts] = s * (1.0 + v * (1.0 - s))
        h = (v * s).astype(BF16).astype(F32).reshape(6, 2, H, COUT)
        hid[1, pl.ds(n * 6, 6)] = h.reshape(6, 16, COUT).astype(BF16)

    pl.loop(0, 11)(activate)
    pass_on(3)
    pl.loop(11, 22)(activate)

    peers = (xa, xb, xo)

    def along_x(p, which):
        send(part.at[peers[which], p], rx1.at[p, which], x1s.at[p, which], x1r.at[p, which],
             dev(peers[which], z, y))

    def spot(b):
        return b // 4, 6 + b % 4 // 2, pl.ds(b % 2 * OWN_OUT, OWN_OUT)

    def put(b, v):
        c, p, rows = spot(b)
        part[c, p, rows, :] = v.astype(BF16)

    tails = []
    taps = [nn(cot3[...], hid[1, pl.ds(kx, 128)].reshape(FINE, COUT)) for kx in range(3)]
    for t in range(9):
        g = taps[t % 3][OWN_OUT * (2 - t // 3):OWN_OUT * (3 - t // 3)]
        put(t, g[:, :128])
        tails.append(g[:, 128:])
    tails.append(jnp.zeros((OWN_OUT, 64), F32))
    for u in range(5):
        put(9 + u, jnp.concatenate(tails[2 * u:2 * u + 2], 1))
    for b in (14, 15):
        put(b, jnp.zeros((OWN_OUT, 128), F32))
    for p in (6, 7):
        for which in (2, 0, 1):
            along_x(p, which)

    def place_cot(at, v, n):
        for m, w in enumerate(shifted(v.reshape(n, 2, H, COUT))):
            cots[pl.ds(at, n), :, pl.ds(256 * m, COUT)] = w

    def place_edge(n):
        for d in range(4):
            arrived(ge_all.at[n, lax.rem(rank + 4 - d, 4)], er.at[1, n, d])
        cols = []
        for h in (0, 64):
            block = [ge_all[n, r][:, h:h + OWN_OUT].astype(F32) for r in range(4)]
            cols.append(jnp.concatenate(block, 1))
        place_cot(130 * n, jnp.concatenate(cols, 0), 2)

    def place_piece(k):
        arrived(g_block(sib, k), gr.at[1, k])
        arrived(g_block(diag, k), gr.at[2, k])
        for b in range(4 * k, 4 * k + 4):
            place_cot(2 + 8 * b, g_all[:, pl.ds(128 * b, 128)].astype(F32).T, 8)

    def adjoint(n):
        g = [cots[pl.ds(n * 26 + 2 - kx, 26)].reshape(416, 768) for kx in range(3)]
        acc = nn(jnp.concatenate(g, 1), conv_t[...])
        ts = pl.ds(n * 13, 13)
        d = (acc.reshape(13, 2, 2, H, COUT) * fs[ts]).astype(BF16).astype(F32)
        for cp in range(2):
            even, odd = d[:, cp, 0], d[:, cp, 1]
            for ky, v in enumerate((down(odd), even, odd, up(even))):
                df[cp, ky, ts] = v

    place_edge(0)
    place_piece(0)
    place_piece(1)
    pl.loop(0, 2)(adjoint)
    place_edge(1)
    place_piece(2)
    place_piece(3)
    pl.loop(2, 5)(adjoint)

    def window(ky, kx):
        return df[kx % 2, ky, pl.ds(kx // 2, 64)].reshape(POS, COUT).astype(BF16)

    for which in (2, 0, 1, 3):
        ky = (xa, xb, xo, x)[which]
        for pair in range(2):
            a, b = [nn(coarse[...], window(ky, kx)) for kx in (2 * pair, 2 * pair + 1)]
            slabs = (a[:, :128], jnp.concatenate([a[:, 128:], b[:, :64]], 1), b[:, 64:])
            for n, slab in enumerate(slabs):
                p = 3 * pair + n
                part[ky, p] = slab.astype(BF16)
                if which < 3:
                    along_x(p, which)

    def picked(count, size):
        row = lax.broadcasted_iota(jnp.int32, (count, size), 0)
        col = lax.broadcasted_iota(jnp.int32, (count, size), 1)
        return (row == col + size * rank).astype(F32).astype(BF16)

    pick = picked(CIN, OWN_IN)
    for t in range(16):
        own_up[t] = nn(up_w[t // 4, t % 4], pick).astype(BF16)

    total = None
    for t in range(16):
        term = nn(window(t // 4, t % 4), own_up[t])
        total = term if total is None else total + term
    c_pos[...] = total

    pick = picked(COUT, OWN_OUT)
    for t in range(9):
        mine[t] = nn(conv_w[t // 3, t % 3], pick).astype(BF16)

    @pl.loop(0, 22)
    def _(n):
        v = hid[1, pl.ds(n * 6, 6)].astype(F32).reshape(6, 2, H, COUT)
        above, _, below = shifted(v)
        hid[0, pl.ds(n * 6, 6)] = above
        hid[2, pl.ds(n * 6, 6)] = below

    def refine(n):
        acc = None
        for t in range(9):
            term = nn(hid[t // 3, pl.ds(16 * n + t % 3, 16)].reshape(256, COUT), mine[t])
            acc = term if acc is None else acc + term
        r_pos[pl.ds(256 * n, 256), :] = acc + own_bias


    for d in far_first:
        zz = lax.rem(z + d, nz)
        acc = part[x, zz].astype(F32)
        for which in range(3):
            arrived(rx1.at[zz, which], x1r.at[zz, which])
            acc = acc + rx1[zz, which].astype(F32)
        if d > 0:
            sb2[d] = acc.astype(BF16)
            send(sb2.at[d], rz.at[d], zs_s.at[d], zs_r.at[d], zdev[d])
        else:
            kept[...] = acc
    for n in range(8):
        refine(n)
    acc = kept[...]
    for d in near_first[1:]:
        arrived(rz.at[d], zs_r.at[d])
        acc = acc + rz[d].astype(F32)
    ys[...] = acc
    send(ys, yr, y_sem.at[0], y_sem.at[1], ydev)
    arrived(yr, y_sem.at[1])
    res[x, z] = (acc + yr[...]).astype(BF16)
    here = res.at[x, z]
    for d in near_first[1:]:
        send(here, here, azs.at[d], azr.at[d], zdev[d])

    def direct(d):
        return d == nz // 2

    def spread_x(d):
        zz = lax.rem(z + nz - d, nz)
        got = res.at[x, zz]
        if d > 0:
            arrived(got, azr.at[d])
        if direct(d):
            send(got, got, axs.at[2, d], axr.at[2, d], dev(xo, z, y))
        send(got, got, axs.at[0, d], axr.at[0, d], dev(second(zz), z, y))
        send(got, got, axs.at[1, d], axr.at[1, d], dev(first(zz), z, y))

    def forward_x(d):
        zz = lax.rem(z + nz - d, nz)
        got = res.at[second(zz), zz]
        arrived(got, axr.at[0, d])
        if not direct(d):
            send(got, got, axs.at[2, d], axr.at[2, d], dev(first(zz), z, y))

    lag = 3
    for n in range(nz + lag):
        if n < nz:
            spread_x(near_first[n])
        if n == 0:
            for r in range(2):
                for i in range(H):
                    g32[pl.ds(2 * i + r, OWN_OUT, stride=16), :] = r_pos[pl.ds(8 * r + i, 128, stride=16), :].T
            refined[...] = g32[...].reshape(OWN_OUT, 16, 128).astype(BF16)
            for i in range(H):
                c_grad[i] = c_pos[pl.ds(i, WC, stride=H), :].astype(BF16)
        if n >= lag:
            forward_x(near_first[n - lag])
    for d in near_first:
        zz = lax.rem(z + nz - d, nz)
        arrived(res.at[first(zz), zz], axr.at[1, d])
        arrived(res.at[xo, zz], axr.at[2, d])
    for copy in started:
        copy.wait_send()


def strip(dims, *args):
    nx, nz, ny = dims
    dma = pltpu.SemaphoreType.DMA
    vm = pltpu.VMEM
    any_ = pl.BlockSpec(memory_space=pl.ANY)
    return pl.pallas_call(
        functools.partial(kernel, dims),
        out_shape=(
            jax.ShapeDtypeStruct((OWN_OUT, 2 * H, 2 * WC), BF16),
            jax.ShapeDtypeStruct((H, WC, OWN_IN), BF16),
            jax.ShapeDtypeStruct((nx, nz, PIECE, 128), BF16),
        ),
        in_specs=[any_] * 6,
        out_specs=[VM] * 3,
        scratch_shapes=[
            vm((1, COUT), F32),
            vm((1, COUT), F32),
            vm((H, WC, OWN_IN), BF16),
            vm((OWN_OUT, 2 * H, 2 * WC), BF16),
            vm((OWN_IN, POS), BF16),
            vm((OWN_OUT, FINE), BF16),
            vm((3 * OWN_OUT, FINE), BF16),
            vm((2, 16, OWN_IN), BF16),
            vm((2, 16, 128), BF16),
            vm((OWN_OUT * 2 * H, 2 * WC), F32),
            vm((CIN, POS), BF16),
            vm((COUT, FINE), BF16),
            vm((2, 4, 16, OWN_IN), BF16),
            vm((2, 4, 16, 128), BF16),
            vm((4, 4, COUT, CIN), BF16),
            vm((3, 3, COUT, COUT), BF16),
            vm((9 * 256, COUT), BF16),
            vm((9, COUT, OWN_OUT), BF16),
            vm((16, COUT, OWN_IN), BF16),
            vm((68, H, CIN), F32),
            vm((528, 6 * CIN), BF16),
            vm((66, 2, 2, H, COUT), F32),
            vm((66, 2, 2, H, COUT), F32),
            vm((3, 132, 16, COUT), BF16),
            vm((132, 16, 3 * 256), BF16),
            vm((2, 4, 66, H, COUT), F32),
            vm((nx, nz, PIECE, 128), BF16),
            vm((FINE, OWN_OUT), F32),
            vm((POS, OWN_IN), F32),
            vm((nz, 3, PIECE, 128), BF16),
            vm((PIECE, 128), F32),
            vm((nz, PIECE, 128), BF16),
            vm((nz, PIECE, 128), BF16),
            vm((PIECE, 128), F32),
            vm((PIECE, 128), F32),
            dma((6,)), dma((3,)), dma((3,)), dma((3, PIECES)), dma((3, PIECES)), dma((2, 2, 4)), dma((2, 2, 4)),
            dma((nz, 3)), dma((nz, 3)), dma((nz,)), dma((nz,)), dma((2,)),
            dma((nz,)), dma((nz,)), dma((3, nz)), dma((3, nz)),
        ],
        compiler_params=pltpu.CompilerParams(
            collective_id=0, has_side_effects=True, vmem_limit_bytes=LIMIT
        ),
        name="strip",
    )(*args)


def unpack_kernel(refined, c_grad, sums, refined_out, c_out, up_grad, conv_grad, ref, cg, src, up, conv, sems, out_sems):
    nx = sums.shape[0]
    loads = [pltpu.make_async_copy(sums.at[k], src.at[k], sems.at[k]) for k in range(nx)]
    loads += [
        pltpu.make_async_copy(refined, ref, sems.at[nx]),
        pltpu.make_async_copy(c_grad, cg, sems.at[nx + 1]),
    ]
    for copy in loads:
        copy.start()
    passes = [
        pltpu.make_async_copy(ref, refined_out, out_sems.at[nx]),
        pltpu.make_async_copy(cg, c_out, out_sems.at[nx + 1]),
    ]
    for ky in range(4):
        loads[ky].wait()
        for pair in range(2):
            a, m, b = [src[ky, 3 * pair + n].astype(F32) for n in range(3)]
            up[ky, 2 * pair] = jnp.concatenate([a, m[:, :64]], 1)
            up[ky, 2 * pair + 1] = jnp.concatenate([m[:, 64:], b], 1)
        copy = pltpu.make_async_copy(up.at[ky], up_grad.at[ky], out_sems.at[ky])
        copy.start()
        passes.append(copy)

    for load, copy in zip(loads[nx:], passes):
        load.wait()
        copy.start()

    def block(b):
        return src[b // 4, 6 + b % 4 // 2, pl.ds(b % 2 * OWN_OUT, OWN_OUT), :].astype(F32)

    for t in range(9):
        tail = block(9 + t // 2)[:, 64 * (t % 2):64 * (t % 2) + 64]
        conv[t // 3, t % 3] = jnp.concatenate([block(t), tail], 1)
    copy = pltpu.make_async_copy(conv, conv_grad, out_sems.at[nx + 2])
    copy.start()
    for copy in passes + [copy]:
        copy.wait()


def unpack(refined, c_grad, sums):
    any_ = pl.BlockSpec(memory_space=pl.ANY)
    up = (4, 4, OWN_IN, COUT)
    conv = (3, 3, OWN_OUT, COUT)
    return pl.pallas_call(
        unpack_kernel,
        out_shape=(
            jax.ShapeDtypeStruct(refined.shape, BF16),
            jax.ShapeDtypeStruct(c_grad.shape, BF16),
            jax.ShapeDtypeStruct(up, F32),
            jax.ShapeDtypeStruct(conv, F32),
        ),
        in_specs=[any_] * 3,
        out_specs=[any_] * 4,
        scratch_shapes=[
            pltpu.VMEM(refined.shape, BF16),
            pltpu.VMEM(c_grad.shape, BF16),
            pltpu.VMEM(sums.shape, BF16),
            pltpu.VMEM(up, F32),
            pltpu.VMEM(conv, F32),
            pltpu.SemaphoreType.DMA((6,)),
            pltpu.SemaphoreType.DMA((7,)),
        ],
        compiler_params=pltpu.CompilerParams(vmem_limit_bytes=LIMIT),
        name="unpack",
    )(refined, c_grad, sums)


def local(dims, coarse, up_weight, up_bias, conv_weight, conv_bias, cotangent):
    refined, c_grad, sums = strip(
        dims, coarse.transpose(1, 2, 0), cotangent, up_weight.transpose(0, 1, 3, 2), conv_weight,
        up_bias.reshape(1, COUT), conv_bias.reshape(1, COUT),
    )
    refined, c_grad, up_grad, conv_grad = unpack(refined, c_grad, sums)
    return refined, c_grad.transpose(2, 0, 1), up_grad, conv_grad.transpose(0, 1, 3, 2)


def solution(mesh):
    dims = (4, 8, 2)
    placed = (P("chan", None, "lon"), P(), P(), P(), P(), P("chan", None, "lon"))
    return jax.shard_map(
        functools.partial(local, dims),
        mesh=mesh,
        in_specs=placed,
        out_specs=(
            P("chan", None, "lon"),
            P("chan", None, "lon"),
            P(None, None, "chan", None),
            P(None, None, None, "chan"),
        ),
        check_vma=False,
    )
```

```python
import functools

import jax
import jax.numpy as jnp
from jax import lax
from jax.experimental import pallas as pl
from jax.experimental.pallas import tpu as pltpu
from jax.sharding import PartitionSpec as P

MESH = pl.DeviceIdType.MESH
F32, BF16 = jnp.float32, jnp.bfloat16
VM = pl.BlockSpec(memory_space=pltpu.VMEM)
CIN, COUT, H, WC = 384, 192, 8, 64
OWN_IN, OWN_OUT = CIN // 4, COUT // 4
POS, FINE = H * WC, 4 * H * WC
PIECE = 96
LIMIT = 60 << 20


def nn(a, b):
    return jnp.dot(a, b, preferred_element_type=F32)


def nt(a, b):
    return lax.dot_general(a, b, (((1,), (1,)), ((), ())), preferred_element_type=F32)


def down(v):
    row = lax.broadcasted_iota(jnp.int32, v.shape, v.ndim - 2)
    return jnp.where(row == 0, 0.0, pltpu.roll(v, 1, v.ndim - 2))


def up(v):
    row = lax.broadcasted_iota(jnp.int32, v.shape, v.ndim - 2)
    return jnp.where(row == H - 1, 0.0, pltpu.roll(v, H - 1, v.ndim - 2))


PIECES = 4


def shifted(v):
    even, odd = v[:, 0], v[:, 1]
    pairs = ((down(odd), even), (even, odd), (odd, up(even)))
    return [jnp.concatenate(pair, 1).astype(BF16) for pair in pairs]


def kernel(dims, coarse_hbm, cot_hbm, up_hbm, conv_hbm, up_b_hbm, conv_b_hbm,
           refined, c_grad, res,
           up_b, conv_b, coarse_in, cot_in, coarse, cot, cot3, c_end, g_end, g32, c_all, g_all, ce_all, ge_all, up_w, conv_w, conv_t, mine, own_up,
           xf, xl, pre, fs, hid, cots, df, part, r_pos, c_pos,
           rx1, kept, sb2, rz, ys, yr,
           w_sem, cs, cr, gs, gr, es, er, x1s, x1r, zs_s, zs_r, y_sem,
           azs, azr, axs, axr):
    nx, nz, ny = dims
    lon, rank = lax.axis_index("lon"), lax.axis_index("chan")
    n_lon = nx * nz * ny
    x, z, y = lon // (nz * ny), lax.rem(lon // ny, nz), lax.rem(lon, ny)
    far, core = rank // 2, lax.rem(rank, 2)
    sib, cross = far * 2 + 1 - core, (1 - far) * 2 + core
    diag = (1 - far) * 2 + 1 - core
    sides = (lax.rem(lon + 1, n_lon), lax.rem(lon + n_lon - 1, n_lon))
    xa, xb = x + 1 - 2 * lax.rem(x, 2), 3 - x
    xo = lax.rem(x + 2, 4)

    def dev(px, pz, py):
        return ((px * nz + pz) * ny + py, rank)

    def first(zz):
        return xa + lax.rem(zz, 2) * (xb - xa)

    def second(zz):
        return xb + lax.rem(zz, 2) * (xa - xb)

    near_first = sorted(range(nz), key=lambda d: min(d, nz - d))
    far_first = near_first[::-1]
    zdev = [dev(x, lax.rem(z + d, nz), y) for d in range(nz)]
    ydev = dev(x, z, 1 - y)

    loads = [
        pltpu.make_async_copy(coarse_hbm, coarse_in, w_sem.at[0]),
        pltpu.make_async_copy(cot_hbm, cot_in, w_sem.at[1]),
        pltpu.make_async_copy(up_hbm, up_w, w_sem.at[2]),
        pltpu.make_async_copy(conv_hbm, conv_w, w_sem.at[3]),
        pltpu.make_async_copy(up_b_hbm, up_b, w_sem.at[4]),
        pltpu.make_async_copy(conv_b_hbm, conv_b, w_sem.at[5]),
    ]
    for load in loads:
        load.start()

    barrier = pltpu.get_barrier_semaphore()
    greet = [zdev[d] for d in far_first[:-1]]
    greet += [(side, lax.rem(rank + d, 4)) for side in sides for d in range(4)]
    greet += [dev(xo, z, y), dev(xa, z, y), dev(xb, z, y)]
    greet += [(lon, lax.rem(rank + d, 4)) for d in range(1, 4)]
    for peer in greet:
        pl.semaphore_signal(barrier, inc=1, device_id=peer, device_id_type=MESH)

    loads[0].wait()
    for i in range(H):
        c_pos[pl.ds(i, WC, stride=H), :] = coarse_in[i].astype(F32)
    for n in range(4):
        coarse[:, pl.ds(128 * n, 128)] = c_pos[pl.ds(128 * n, 128), :].T.astype(BF16)
    c_end[0] = c_pos[pl.ds(POS - 16, 16), :].astype(BF16)
    c_end[1] = c_pos[pl.ds(0, 16), :].astype(BF16)
    loads[1].wait()
    g32[...] = cot_in[...].astype(F32).reshape(OWN_OUT * 16, 128)
    for r in range(2):
        for i in range(H):
            r_pos[pl.ds(8 * r + i, 128, stride=16), :] = g32[pl.ds(2 * i + r, OWN_OUT, stride=16), :].T
    for n in range(16):
        cot[:, pl.ds(128 * n, 128)] = r_pos[pl.ds(128 * n, 128), :].T.astype(BF16)
    gap = jnp.zeros((16, 64 - OWN_OUT), F32)
    for n, at in enumerate((FINE - 32, 0)):
        two = [r_pos[pl.ds(at, 16), :], gap, r_pos[pl.ds(at + 16, 16), :], gap]
        g_end[n] = jnp.concatenate(two, 1).astype(BF16)
    pl.semaphore_wait(barrier, len(greet))

    started = []

    def copy_of(a, b, s, r, to):
        return pltpu.make_async_remote_copy(
            src_ref=a, dst_ref=b, send_sem=s, recv_sem=r, device_id=to, device_id_type=MESH
        )

    def send(a, b, s, r, to):
        copy = copy_of(a, b, s, r, to)
        copy.start()
        started.append(copy)

    def arrived(b, r):
        copy_of(b, b, r, r, (lon, sib)).wait_recv()

    c_width = POS // 2

    def c_block(r, k):
        rows = pl.ds(pl.multiple_of(r * OWN_IN, 16), OWN_IN)
        return c_all.at[rows, pl.ds(k * c_width, c_width)]

    width = FINE // PIECES

    def g_block(r, k):
        return g_all.at[pl.ds(pl.multiple_of(r * OWN_OUT, 16), OWN_OUT), pl.ds(k * width, width)]

    c_own = [coarse.at[:, pl.ds(k * c_width, c_width)] for k in range(2)]
    for k in range(2):
        send(c_own[k], c_block(rank, k), cs.at[0, k], cr.at[0, k], (lon, cross))
    for n, side in enumerate(sides):
        for d in range(4):
            to = (side, lax.rem(rank + d, 4))
            send(c_end.at[n], ce_all.at[n, rank], es.at[0, n, d], er.at[0, n, d], to)
    for k in range(2):
        send(c_own[k], c_block(rank, k), cs.at[1, k], cr.at[1, k], (lon, sib))
    for n, side in enumerate(sides):
        for d in range(4):
            to = (side, lax.rem(rank + d, 4))
            send(g_end.at[n], ge_all.at[n, rank], es.at[1, n, d], er.at[1, n, d], to)
    for k in range(PIECES):
        own_part = cot.at[:, pl.ds(k * width, width)]
        send(own_part, g_block(rank, k), gs.at[0, k], gr.at[0, k], (lon, cross))
        send(own_part, g_block(rank, k), gs.at[1, k], gr.at[1, k], (lon, sib))
    c_all[pl.ds(pl.multiple_of(rank * OWN_IN, 16), OWN_IN), :] = coarse[...]
    g_all[pl.ds(pl.multiple_of(rank * OWN_OUT, 16), OWN_OUT), :] = cot[...]

    def pass_on(k):
        arrived(g_block(cross, k), gr.at[0, k])
        send(g_block(cross, k), g_block(cross, k), gs.at[2, k], gr.at[2, k], (lon, sib))

    pad = jnp.zeros((132, 16, 64), BF16)
    for m in range(3):
        cots[:, :, pl.ds(256 * m + COUT, 64)] = pad
    conv_t[...] = jnp.zeros(conv_t.shape, BF16)
    cot3[pl.ds(OWN_OUT, OWN_OUT), :] = cot[...]
    for m in (0, 2):
        for r in range(2):
            for i in range(H):
                p = 2 * i + r + m - 1
                rows = pl.ds(8 * r + i, 128, stride=16)
                if 0 <= p < 16:
                    r_pos[rows, :] = g32[pl.ds(p, OWN_OUT, stride=16), :].T
                else:
                    r_pos[rows, :] = jnp.zeros((128, OWN_OUT), F32)
        for n in range(16):
            cot3[pl.ds(OWN_OUT * m, OWN_OUT), pl.ds(128 * n, 128)] = r_pos[pl.ds(128 * n, 128), :].T.astype(BF16)

    for load in loads[2:]:
        load.wait()
    own_bias = jnp.zeros((1, OWN_OUT), F32)
    for r in range(4):
        own_bias += jnp.where(rank == r, conv_b[:, pl.ds(OWN_OUT * r, OWN_OUT)], 0.0)
    for t in range(9):
        w = conv_w[t // 3, t % 3]
        conv_t[pl.ds(768 * (t % 3) + 256 * (2 - t // 3), COUT), :] = w.astype(F32).T.astype(BF16)

    for k in range(2):
        arrived(c_block(cross, k), cr.at[0, k])
        send(c_block(cross, k), c_block(cross, k), cs.at[2, k], cr.at[2, k], (lon, sib))
    for k in range(2):
        arrived(c_block(sib, k), cr.at[1, k])
        arrived(c_block(diag, k), cr.at[2, k])
        for b in (2 * k, 2 * k + 1):
            xf[pl.ds(1 + 16 * b, 16)] = c_all[:, pl.ds(128 * b, 128)].astype(F32).T.reshape(16, H, CIN)
    for n in range(2):
        for d in range(4):
            arrived(ce_all.at[n, lax.rem(rank + 4 - d, 4)], er.at[0, n, d])
    left, right = [
        jnp.concatenate([ce_all[n, r].astype(F32) for r in range(4)], 1) for n in range(2)
    ]
    xf[0] = left[8:]
    xf[65] = right[:8]
    xf[66:68] = jnp.zeros((2, H, CIN), F32)

    @pl.loop(0, 3)
    def _(n):
        t0 = n * 22
        rows = pl.ds(pl.multiple_of(t0 * H, 16), 22 * H)
        for d in range(2):
            v = xf[pl.ds(t0 + 1 - d, 22)]
            for s, w in enumerate((down(v), v, up(v))):
                xl[rows, pl.ds((2 * s + d) * CIN, CIN)] = w.reshape(22 * H, CIN).astype(BF16)

    pass_on(0)
    for rp in range(2):
        for cp in range(2):
            taps = ((3, 1), (2, 0))[rp]
            w = jnp.concatenate([up_w[ky, cp + 2 * d] for ky in taps for d in range(2)], 1)
            val = nt(xl[:, pl.ds(rp * 2 * CIN, 4 * CIN)], w)
            pre[:, cp, rp] = val.reshape(66, H, COUT)
        pass_on(1 + rp)

    bias = up_b[...].reshape(1, 1, 1, 1, COUT)

    def activate(n):
        ts = pl.ds(n * 3, 3)
        v = pre[ts] + bias
        s = jax.nn.sigmoid(v)
        fs[ts] = s * (1.0 + v * (1.0 - s))
        h = (v * s).astype(BF16).astype(F32).reshape(6, 2, H, COUT)
        hid[1, pl.ds(n * 6, 6)] = h.reshape(6, 16, COUT).astype(BF16)

    pl.loop(0, 11)(activate)
    pass_on(3)
    pl.loop(11, 22)(activate)

    peers = (xa, xb, xo)

    def along_x(p, which):
        send(part.at[peers[which], p], rx1.at[p, which], x1s.at[p, which], x1r.at[p, which],
             dev(peers[which], z, y))

    def spot(b):
        return b // 4, 6 + b % 4 // 2, pl.ds(b % 2 * OWN_OUT, OWN_OUT)

    def put(b, v):
        c, p, rows = spot(b)
        part[c, p, rows, :] = v.astype(BF16)

    tails = []
    taps = [nn(cot3[...], hid[1, pl.ds(kx, 128)].reshape(FINE, COUT)) for kx in range(3)]
    for t in range(9):
        g = taps[t % 3][OWN_OUT * (2 - t // 3):OWN_OUT * (3 - t // 3)]
        put(t, g[:, :128])
        tails.append(g[:, 128:])
    tails.append(jnp.zeros((OWN_OUT, 64), F32))
    for u in range(5):
        put(9 + u, jnp.concatenate(tails[2 * u:2 * u + 2], 1))
    for b in (14, 15):
        put(b, jnp.zeros((OWN_OUT, 128), F32))
    for p in (6, 7):
        for which in (2, 0, 1):
            along_x(p, which)

    def place_cot(at, v, n):
        for m, w in enumerate(shifted(v.reshape(n, 2, H, COUT))):
            cots[pl.ds(at, n), :, pl.ds(256 * m, COUT)] = w

    def place_edge(n):
        for d in range(4):
            arrived(ge_all.at[n, lax.rem(rank + 4 - d, 4)], er.at[1, n, d])
        cols = []
        for h in (0, 64):
            block = [ge_all[n, r][:, h:h + OWN_OUT].astype(F32) for r in range(4)]
            cols.append(jnp.concatenate(block, 1))
        place_cot(130 * n, jnp.concatenate(cols, 0), 2)

    def place_piece(k):
        arrived(g_block(sib, k), gr.at[1, k])
        arrived(g_block(diag, k), gr.at[2, k])
        for b in range(4 * k, 4 * k + 4):
            place_cot(2 + 8 * b, g_all[:, pl.ds(128 * b, 128)].astype(F32).T, 8)

    def adjoint(n):
        g = [cots[pl.ds(n * 26 + 2 - kx, 26)].reshape(416, 768) for kx in range(3)]
        acc = nn(jnp.concatenate(g, 1), conv_t[...])
        ts = pl.ds(n * 13, 13)
        d = (acc.reshape(13, 2, 2, H, COUT) * fs[ts]).astype(BF16).astype(F32)
        for cp in range(2):
            even, odd = d[:, cp, 0], d[:, cp, 1]
            for ky, v in enumerate((down(odd), even, odd, up(even))):
                df[cp, ky, ts] = v

    place_edge(0)
    place_piece(0)
    place_piece(1)
    pl.loop(0, 2)(adjoint)
    place_edge(1)
    place_piece(2)
    place_piece(3)
    pl.loop(2, 5)(adjoint)

    def window(ky, kx):
        return df[kx % 2, ky, pl.ds(kx // 2, 64)].reshape(POS, COUT).astype(BF16)

    for which in (2, 0, 1, 3):
        ky = (xa, xb, xo, x)[which]
        for pair in range(2):
            a, b = [nn(coarse[...], window(ky, kx)) for kx in (2 * pair, 2 * pair + 1)]
            slabs = (a[:, :128], jnp.concatenate([a[:, 128:], b[:, :64]], 1), b[:, 64:])
            for n, slab in enumerate(slabs):
                p = 3 * pair + n
                part[ky, p] = slab.astype(BF16)
                if which < 3:
                    along_x(p, which)

    def picked(count, size):
        row = lax.broadcasted_iota(jnp.int32, (count, size), 0)
        col = lax.broadcasted_iota(jnp.int32, (count, size), 1)
        return (row == col + size * rank).astype(F32).astype(BF16)

    pick = picked(CIN, OWN_IN)
    for t in range(16):
        own_up[t] = nn(up_w[t // 4, t % 4], pick).astype(BF16)

    total = None
    for t in range(16):
        term = nn(window(t // 4, t % 4), own_up[t])
        total = term if total is None else total + term
    c_pos[...] = total

    pick = picked(COUT, OWN_OUT)
    for t in range(9):
        mine[t] = nn(conv_w[t // 3, t % 3], pick).astype(BF16)

    @pl.loop(0, 22)
    def _(n):
        v = hid[1, pl.ds(n * 6, 6)].astype(F32).reshape(6, 2, H, COUT)
        above, _, below = shifted(v)
        hid[0, pl.ds(n * 6, 6)] = above
        hid[2, pl.ds(n * 6, 6)] = below

    def refine(n):
        acc = None
        for t in range(9):
            term = nn(hid[t // 3, pl.ds(16 * n + t % 3, 16)].reshape(256, COUT), mine[t])
            acc = term if acc is None else acc + term
        r_pos[pl.ds(256 * n, 256), :] = acc + own_bias


    for d in far_first:
        zz = lax.rem(z + d, nz)
        acc = part[x, zz].astype(F32)
        for which in range(3):
            arrived(rx1.at[zz, which], x1r.at[zz, which])
            acc = acc + rx1[zz, which].astype(F32)
        if d > 0:
            sb2[d] = acc.astype(BF16)
            send(sb2.at[d], rz.at[d], zs_s.at[d], zs_r.at[d], zdev[d])
        else:
            kept[...] = acc
    for n in range(8):
        refine(n)
    acc = kept[...]
    for d in near_first[1:]:
        arrived(rz.at[d], zs_r.at[d])
        acc = acc + rz[d].astype(F32)
    ys[...] = acc
    send(ys, yr, y_sem.at[0], y_sem.at[1], ydev)
    arrived(yr, y_sem.at[1])
    res[x, z] = (acc + yr[...]).astype(BF16)
    here = res.at[x, z]
    for d in near_first[1:]:
        send(here, here, azs.at[d], azr.at[d], zdev[d])

    def direct(d):
        return d == nz // 2

    def spread_x(d):
        zz = lax.rem(z + nz - d, nz)
        got = res.at[x, zz]
        if d > 0:
            arrived(got, azr.at[d])
        if direct(d):
            send(got, got, axs.at[2, d], axr.at[2, d], dev(xo, z, y))
        send(got, got, axs.at[0, d], axr.at[0, d], dev(second(zz), z, y))
        send(got, got, axs.at[1, d], axr.at[1, d], dev(first(zz), z, y))

    def forward_x(d):
        zz = lax.rem(z + nz - d, nz)
        got = res.at[second(zz), zz]
        arrived(got, axr.at[0, d])
        if not direct(d):
            send(got, got, axs.at[2, d], axr.at[2, d], dev(first(zz), z, y))

    lag = 3
    for n in range(nz + lag):
        if n < nz:
            spread_x(near_first[n])
        if n == 0:
            for r in range(2):
                for i in range(H):
                    g32[pl.ds(2 * i + r, OWN_OUT, stride=16), :] = r_pos[pl.ds(8 * r + i, 128, stride=16), :].T
            refined[...] = g32[...].reshape(OWN_OUT, 16, 128).astype(BF16)
            for i in range(H):
                c_grad[i] = c_pos[pl.ds(i, WC, stride=H), :].astype(BF16)
        if n >= lag:
            forward_x(near_first[n - lag])
    for d in near_first:
        zz = lax.rem(z + nz - d, nz)
        arrived(res.at[first(zz), zz], axr.at[1, d])
        arrived(res.at[xo, zz], axr.at[2, d])
    for copy in started:
        copy.wait_send()


def strip(dims, *args):
    nx, nz, ny = dims
    dma = pltpu.SemaphoreType.DMA
    vm = pltpu.VMEM
    any_ = pl.BlockSpec(memory_space=pl.ANY)
    return pl.pallas_call(
        functools.partial(kernel, dims),
        out_shape=(
            jax.ShapeDtypeStruct((OWN_OUT, 2 * H, 2 * WC), BF16),
            jax.ShapeDtypeStruct((H, WC, OWN_IN), BF16),
            jax.ShapeDtypeStruct((nx, nz, PIECE, 128), BF16),
        ),
        in_specs=[any_] * 6,
        out_specs=[VM] * 3,
        scratch_shapes=[
            vm((1, COUT), F32),
            vm((1, COUT), F32),
            vm((H, WC, OWN_IN), BF16),
            vm((OWN_OUT, 2 * H, 2 * WC), BF16),
            vm((OWN_IN, POS), BF16),
            vm((OWN_OUT, FINE), BF16),
            vm((3 * OWN_OUT, FINE), BF16),
            vm((2, 16, OWN_IN), BF16),
            vm((2, 16, 128), BF16),
            vm((OWN_OUT * 2 * H, 2 * WC), F32),
            vm((CIN, POS), BF16),
            vm((COUT, FINE), BF16),
            vm((2, 4, 16, OWN_IN), BF16),
            vm((2, 4, 16, 128), BF16),
            vm((4, 4, COUT, CIN), BF16),
            vm((3, 3, COUT, COUT), BF16),
            vm((9 * 256, COUT), BF16),
            vm((9, COUT, OWN_OUT), BF16),
            vm((16, COUT, OWN_IN), BF16),
            vm((68, H, CIN), F32),
            vm((528, 6 * CIN), BF16),
            vm((66, 2, 2, H, COUT), F32),
            vm((66, 2, 2, H, COUT), F32),
            vm((3, 132, 16, COUT), BF16),
            vm((132, 16, 3 * 256), BF16),
            vm((2, 4, 66, H, COUT), F32),
            vm((nx, nz, PIECE, 128), BF16),
            vm((FINE, OWN_OUT), F32),
            vm((POS, OWN_IN), F32),
            vm((nz, 3, PIECE, 128), BF16),
            vm((PIECE, 128), F32),
            vm((nz, PIECE, 128), BF16),
            vm((nz, PIECE, 128), BF16),
            vm((PIECE, 128), F32),
            vm((PIECE, 128), F32),
            dma((6,)), dma((3, 2)), dma((3, 2)), dma((3, PIECES)), dma((3, PIECES)), dma((2, 2, 4)), dma((2, 2, 4)),
            dma((nz, 3)), dma((nz, 3)), dma((nz,)), dma((nz,)), dma((2,)),
            dma((nz,)), dma((nz,)), dma((3, nz)), dma((3, nz)),
        ],
        compiler_params=pltpu.CompilerParams(
            collective_id=0, has_side_effects=True, vmem_limit_bytes=LIMIT
        ),
        name="strip",
    )(*args)


def unpack_kernel(refined, c_grad, sums, refined_out, c_out, up_grad, conv_grad, ref, cg, src, up, conv, sems, out_sems):
    nx = sums.shape[0]
    loads = [pltpu.make_async_copy(sums.at[k], src.at[k], sems.at[k]) for k in range(nx)]
    loads += [
        pltpu.make_async_copy(refined, ref, sems.at[nx]),
        pltpu.make_async_copy(c_grad, cg, sems.at[nx + 1]),
    ]
    for copy in loads:
        copy.start()
    passes = [
        pltpu.make_async_copy(ref, refined_out, out_sems.at[nx]),
        pltpu.make_async_copy(cg, c_out, out_sems.at[nx + 1]),
    ]
    for ky in range(4):
        loads[ky].wait()
        for pair in range(2):
            a, m, b = [src[ky, 3 * pair + n].astype(F32) for n in range(3)]
            up[ky, 2 * pair] = jnp.concatenate([a, m[:, :64]], 1)
            up[ky, 2 * pair + 1] = jnp.concatenate([m[:, 64:], b], 1)
        copy = pltpu.make_async_copy(up.at[ky], up_grad.at[ky], out_sems.at[ky])
        copy.start()
        passes.append(copy)

    for load, copy in zip(loads[nx:], passes):
        load.wait()
        copy.start()

    def block(b):
        return src[b // 4, 6 + b % 4 // 2, pl.ds(b % 2 * OWN_OUT, OWN_OUT), :].astype(F32)

    for t in range(9):
        tail = block(9 + t // 2)[:, 64 * (t % 2):64 * (t % 2) + 64]
        conv[t // 3, t % 3] = jnp.concatenate([block(t), tail], 1)
    copy = pltpu.make_async_copy(conv, conv_grad, out_sems.at[nx + 2])
    copy.start()
    for copy in passes + [copy]:
        copy.wait()


def unpack(refined, c_grad, sums):
    any_ = pl.BlockSpec(memory_space=pl.ANY)
    up = (4, 4, OWN_IN, COUT)
    conv = (3, 3, OWN_OUT, COUT)
    return pl.pallas_call(
        unpack_kernel,
        out_shape=(
            jax.ShapeDtypeStruct(refined.shape, BF16),
            jax.ShapeDtypeStruct(c_grad.shape, BF16),
            jax.ShapeDtypeStruct(up, F32),
            jax.ShapeDtypeStruct(conv, F32),
        ),
        in_specs=[any_] * 3,
        out_specs=[any_] * 4,
        scratch_shapes=[
            pltpu.VMEM(refined.shape, BF16),
            pltpu.VMEM(c_grad.shape, BF16),
            pltpu.VMEM(sums.shape, BF16),
            pltpu.VMEM(up, F32),
            pltpu.VMEM(conv, F32),
            pltpu.SemaphoreType.DMA((6,)),
            pltpu.SemaphoreType.DMA((7,)),
        ],
        compiler_params=pltpu.CompilerParams(vmem_limit_bytes=LIMIT),
        name="unpack",
    )(refined, c_grad, sums)


def local(dims, coarse, up_weight, up_bias, conv_weight, conv_bias, cotangent):
    refined, c_grad, sums = strip(
        dims, coarse.transpose(1, 2, 0), cotangent, up_weight.transpose(0, 1, 3, 2), conv_weight,
        up_bias.reshape(1, COUT), conv_bias.reshape(1, COUT),
    )
    refined, c_grad, up_grad, conv_grad = unpack(refined, c_grad, sums)
    return refined, c_grad.transpose(2, 0, 1), up_grad, conv_grad.transpose(0, 1, 3, 2)


def solution(mesh):
    dims = (4, 8, 2)
    placed = (P("chan", None, "lon"), P(), P(), P(), P(), P("chan", None, "lon"))
    return jax.shard_map(
        functools.partial(local, dims),
        mesh=mesh,
        in_specs=placed,
        out_specs=(
            P("chan", None, "lon"),
            P("chan", None, "lon"),
            P(None, None, "chan", None),
            P(None, None, None, "chan"),
        ),
        check_vma=False,
    )
```

```python
import functools

import jax
import jax.numpy as jnp
from jax import lax
from jax.experimental import pallas as pl
from jax.experimental.pallas import tpu as pltpu
from jax.sharding import PartitionSpec as P

MESH = pl.DeviceIdType.MESH
F32, BF16 = jnp.float32, jnp.bfloat16
VM = pl.BlockSpec(memory_space=pltpu.VMEM)
CIN, COUT, H, WC = 384, 192, 8, 64
OWN_IN, OWN_OUT = CIN // 4, COUT // 4
POS, FINE = H * WC, 4 * H * WC
PIECE = 96
LIMIT = 52 << 20


def nn(a, b):
    return jnp.dot(a, b, preferred_element_type=F32)


def nt(a, b):
    return lax.dot_general(a, b, (((1,), (1,)), ((), ())), preferred_element_type=F32)


def down(v):
    row = lax.broadcasted_iota(jnp.int32, v.shape, v.ndim - 2)
    return jnp.where(row == 0, 0.0, pltpu.roll(v, 1, v.ndim - 2))


def up(v):
    row = lax.broadcasted_iota(jnp.int32, v.shape, v.ndim - 2)
    return jnp.where(row == H - 1, 0.0, pltpu.roll(v, H - 1, v.ndim - 2))


PIECES = 4


def shifted(v):
    even, odd = v[:, 0], v[:, 1]
    pairs = ((down(odd), even), (even, odd), (odd, up(even)))
    return [jnp.concatenate(pair, 1).astype(BF16) for pair in pairs]


def kernel(dims, coarse_hbm, cot_hbm, up_hbm, conv_hbm, up_b_hbm, conv_b_hbm,
           refined, c_grad, res,
           up_b, conv_b, coarse_in, cot_in, coarse, cot, cot3, c_end, g_end, g32, c_all, g_all, ce_all, ge_all, up_w, conv_w, conv_t, mine, own_up,
           xf, xl, pre, fs, hid, cots, df, part, r_pos, c_pos,
           rx1, kept, sb2, rz, ys, yr,
           w_sem, cs, cr, gs, gr, es, er, x1s, x1r, zs_s, zs_r, y_sem,
           azs, azr, axs, axr):
    nx, nz, ny = dims
    lon, rank = lax.axis_index("lon"), lax.axis_index("chan")
    n_lon = nx * nz * ny
    x, z, y = lon // (nz * ny), lax.rem(lon // ny, nz), lax.rem(lon, ny)
    far, core = rank // 2, lax.rem(rank, 2)
    sib, cross = far * 2 + 1 - core, (1 - far) * 2 + core
    diag = (1 - far) * 2 + 1 - core
    sides = (lax.rem(lon + 1, n_lon), lax.rem(lon + n_lon - 1, n_lon))
    xa, xb = x + 1 - 2 * lax.rem(x, 2), 3 - x
    xo = lax.rem(x + 2, 4)

    def dev(px, pz, py):
        return ((px * nz + pz) * ny + py, rank)

    def first(zz):
        return xa + lax.rem(zz, 2) * (xb - xa)

    def second(zz):
        return xb + lax.rem(zz, 2) * (xa - xb)

    near_first = sorted(range(nz), key=lambda d: min(d, nz - d))
    far_first = near_first[::-1]
    zdev = [dev(x, lax.rem(z + d, nz), y) for d in range(nz)]
    ydev = dev(x, z, 1 - y)

    loads = [
        pltpu.make_async_copy(coarse_hbm, coarse_in, w_sem.at[0]),
        pltpu.make_async_copy(cot_hbm, cot_in, w_sem.at[1]),
        pltpu.make_async_copy(up_hbm, up_w, w_sem.at[2]),
        pltpu.make_async_copy(conv_hbm, conv_w, w_sem.at[3]),
        pltpu.make_async_copy(up_b_hbm, up_b, w_sem.at[4]),
        pltpu.make_async_copy(conv_b_hbm, conv_b, w_sem.at[5]),
    ]
    for load in loads:
        load.start()

    barrier = pltpu.get_barrier_semaphore()
    greet = [zdev[d] for d in far_first[:-1]]
    greet += [(side, lax.rem(rank + d, 4)) for side in sides for d in range(4)]
    greet += [dev(xo, z, y), dev(xa, z, y), dev(xb, z, y)]
    greet += [(lon, lax.rem(rank + d, 4)) for d in range(1, 4)]
    for peer in greet:
        pl.semaphore_signal(barrier, inc=1, device_id=peer, device_id_type=MESH)

    loads[0].wait()
    for i in range(H):
        c_pos[pl.ds(i, WC, stride=H), :] = coarse_in[i].astype(F32)
    for n in range(4):
        coarse[:, pl.ds(128 * n, 128)] = c_pos[pl.ds(128 * n, 128), :].T.astype(BF16)
    c_end[0] = c_pos[pl.ds(POS - 16, 16), :].astype(BF16)
    c_end[1] = c_pos[pl.ds(0, 16), :].astype(BF16)
    loads[1].wait()
    g32[...] = cot_in[...].astype(F32).reshape(OWN_OUT * 16, 128)
    for r in range(2):
        for i in range(H):
            r_pos[pl.ds(8 * r + i, 128, stride=16), :] = g32[pl.ds(2 * i + r, OWN_OUT, stride=16), :].T
    for n in range(16):
        cot[:, pl.ds(128 * n, 128)] = r_pos[pl.ds(128 * n, 128), :].T.astype(BF16)
    gap = jnp.zeros((16, 64 - OWN_OUT), F32)
    for n, at in enumerate((FINE - 32, 0)):
        two = [r_pos[pl.ds(at, 16), :], gap, r_pos[pl.ds(at + 16, 16), :], gap]
        g_end[n] = jnp.concatenate(two, 1).astype(BF16)
    pl.semaphore_wait(barrier, len(greet))

    started = []

    def copy_of(a, b, s, r, to):
        return pltpu.make_async_remote_copy(
            src_ref=a, dst_ref=b, send_sem=s, recv_sem=r, device_id=to, device_id_type=MESH
        )

    def send(a, b, s, r, to):
        copy = copy_of(a, b, s, r, to)
        copy.start()
        started.append(copy)

    def arrived(b, r):
        copy_of(b, b, r, r, (lon, sib)).wait_recv()

    c_width = POS // 2

    def c_block(r, k):
        rows = pl.ds(pl.multiple_of(r * OWN_IN, 16), OWN_IN)
        return c_all.at[rows, pl.ds(k * c_width, c_width)]

    width = FINE // PIECES

    def g_block(r, k):
        return g_all.at[pl.ds(pl.multiple_of(r * OWN_OUT, 16), OWN_OUT), pl.ds(k * width, width)]

    c_own = [coarse.at[:, pl.ds(k * c_width, c_width)] for k in range(2)]
    for k in range(2):
        send(c_own[k], c_block(rank, k), cs.at[0, k], cr.at[0, k], (lon, cross))
    for n, side in enumerate(sides):
        for d in range(4):
            to = (side, lax.rem(rank + d, 4))
            send(c_end.at[n], ce_all.at[n, rank], es.at[0, n, d], er.at[0, n, d], to)
    for k in range(2):
        send(c_own[k], c_block(rank, k), cs.at[1, k], cr.at[1, k], (lon, sib))
    for n, side in enumerate(sides):
        for d in range(4):
            to = (side, lax.rem(rank + d, 4))
            send(g_end.at[n], ge_all.at[n, rank], es.at[1, n, d], er.at[1, n, d], to)
    for k in range(PIECES):
        own_part = cot.at[:, pl.ds(k * width, width)]
        send(own_part, g_block(rank, k), gs.at[0, k], gr.at[0, k], (lon, cross))
        send(own_part, g_block(rank, k), gs.at[1, k], gr.at[1, k], (lon, sib))
    c_all[pl.ds(pl.multiple_of(rank * OWN_IN, 16), OWN_IN), :] = coarse[...]
    g_all[pl.ds(pl.multiple_of(rank * OWN_OUT, 16), OWN_OUT), :] = cot[...]

    def pass_on(k):
        arrived(g_block(cross, k), gr.at[0, k])
        send(g_block(cross, k), g_block(cross, k), gs.at[2, k], gr.at[2, k], (lon, sib))

    pad = jnp.zeros((132, 16, 64), BF16)
    for m in range(3):
        cots[:, :, pl.ds(256 * m + COUT, 64)] = pad
    conv_t[...] = jnp.zeros(conv_t.shape, BF16)
    cot3[pl.ds(OWN_OUT, OWN_OUT), :] = cot[...]
    for m in (0, 2):
        for r in range(2):
            for i in range(H):
                p = 2 * i + r + m - 1
                rows = pl.ds(8 * r + i, 128, stride=16)
                if 0 <= p < 16:
                    r_pos[rows, :] = g32[pl.ds(p, OWN_OUT, stride=16), :].T
                else:
                    r_pos[rows, :] = jnp.zeros((128, OWN_OUT), F32)
        for n in range(16):
            cot3[pl.ds(OWN_OUT * m, OWN_OUT), pl.ds(128 * n, 128)] = r_pos[pl.ds(128 * n, 128), :].T.astype(BF16)

    for load in loads[2:]:
        load.wait()
    own_bias = jnp.zeros((1, OWN_OUT), F32)
    for r in range(4):
        own_bias += jnp.where(rank == r, conv_b[:, pl.ds(OWN_OUT * r, OWN_OUT)], 0.0)
    for t in range(9):
        w = conv_w[t // 3, t % 3]
        conv_t[pl.ds(768 * (t % 3) + 256 * (2 - t // 3), COUT), :] = w.astype(F32).T.astype(BF16)

    for k in range(2):
        arrived(c_block(cross, k), cr.at[0, k])
        send(c_block(cross, k), c_block(cross, k), cs.at[2, k], cr.at[2, k], (lon, sib))
    for k in range(2):
        arrived(c_block(sib, k), cr.at[1, k])
        arrived(c_block(diag, k), cr.at[2, k])
        for b in (2 * k, 2 * k + 1):
            xf[pl.ds(1 + 16 * b, 16)] = c_all[:, pl.ds(128 * b, 128)].astype(F32).T.reshape(16, H, CIN)
    for n in range(2):
        for d in range(4):
            arrived(ce_all.at[n, lax.rem(rank + 4 - d, 4)], er.at[0, n, d])
    left, right = [
        jnp.concatenate([ce_all[n, r].astype(F32) for r in range(4)], 1) for n in range(2)
    ]
    xf[0] = left[8:]
    xf[65] = right[:8]
    xf[66:68] = jnp.zeros((2, H, CIN), F32)

    @pl.loop(0, 3)
    def _(n):
        t0 = n * 22
        rows = pl.ds(pl.multiple_of(t0 * H, 16), 22 * H)
        for d in range(2):
            v = xf[pl.ds(t0 + 1 - d, 22)]
            for s, w in enumerate((down(v), v, up(v))):
                xl[rows, pl.ds((2 * s + d) * CIN, CIN)] = w.reshape(22 * H, CIN).astype(BF16)

    pass_on(0)
    for rp in range(2):
        for cp in range(2):
            taps = ((3, 1), (2, 0))[rp]
            w = jnp.concatenate([up_w[ky, cp + 2 * d] for ky in taps for d in range(2)], 1)
            val = nt(xl[:, pl.ds(rp * 2 * CIN, 4 * CIN)], w)
            pre[:, cp, rp] = val.reshape(66, H, COUT)
        pass_on(1 + rp)

    bias = up_b[...].reshape(1, 1, 1, 1, COUT)

    def activate(n):
        ts = pl.ds(n * 3, 3)
        v = pre[ts] + bias
        s = jax.nn.sigmoid(v)
        fs[ts] = s * (1.0 + v * (1.0 - s))
        h = (v * s).astype(BF16).astype(F32).reshape(6, 2, H, COUT)
        hid[1, pl.ds(n * 6, 6)] = h.reshape(6, 16, COUT).astype(BF16)

    pl.loop(0, 11)(activate)
    pass_on(3)
    pl.loop(11, 22)(activate)

    peers = (xa, xb, xo)

    def along_x(p, which):
        send(part.at[peers[which], p], rx1.at[p, which], x1s.at[p, which], x1r.at[p, which],
             dev(peers[which], z, y))

    def spot(b):
        return b // 4, 6 + b % 4 // 2, pl.ds(b % 2 * OWN_OUT, OWN_OUT)

    def put(b, v):
        c, p, rows = spot(b)
        part[c, p, rows, :] = v.astype(BF16)

    tails = []
    taps = [nn(cot3[...], hid[1, pl.ds(kx, 128)].reshape(FINE, COUT)) for kx in range(3)]
    for t in range(9):
        g = taps[t % 3][OWN_OUT * (2 - t // 3):OWN_OUT * (3 - t // 3)]
        put(t, g[:, :128])
        tails.append(g[:, 128:])
    tails.append(jnp.zeros((OWN_OUT, 64), F32))
    for u in range(5):
        put(9 + u, jnp.concatenate(tails[2 * u:2 * u + 2], 1))
    for b in (14, 15):
        put(b, jnp.zeros((OWN_OUT, 128), F32))
    for p in (6, 7):
        for which in (2, 0, 1):
            along_x(p, which)

    def place_cot(at, v, n):
        for m, w in enumerate(shifted(v.reshape(n, 2, H, COUT))):
            cots[pl.ds(at, n), :, pl.ds(256 * m, COUT)] = w

    def place_edge(n):
        for d in range(4):
            arrived(ge_all.at[n, lax.rem(rank + 4 - d, 4)], er.at[1, n, d])
        cols = []
        for h in (0, 64):
            block = [ge_all[n, r][:, h:h + OWN_OUT].astype(F32) for r in range(4)]
            cols.append(jnp.concatenate(block, 1))
        place_cot(130 * n, jnp.concatenate(cols, 0), 2)

    def place_piece(k):
        arrived(g_block(sib, k), gr.at[1, k])
        arrived(g_block(diag, k), gr.at[2, k])
        for b in range(4 * k, 4 * k + 4):
            place_cot(2 + 8 * b, g_all[:, pl.ds(128 * b, 128)].astype(F32).T, 8)

    def adjoint(n):
        g = [cots[pl.ds(n * 26 + 2 - kx, 26)].reshape(416, 768) for kx in range(3)]
        acc = nn(jnp.concatenate(g, 1), conv_t[...])
        ts = pl.ds(n * 13, 13)
        d = (acc.reshape(13, 2, 2, H, COUT) * fs[ts]).astype(BF16).astype(F32)
        for cp in range(2):
            even, odd = d[:, cp, 0], d[:, cp, 1]
            for ky, v in enumerate((down(odd), even, odd, up(even))):
                df[cp, ky, ts] = v

    place_edge(0)
    place_piece(0)
    place_piece(1)
    pl.loop(0, 2)(adjoint)
    place_edge(1)
    place_piece(2)
    place_piece(3)
    pl.loop(2, 5)(adjoint)

    def window(ky, kx):
        return df[kx % 2, ky, pl.ds(kx // 2, 64)].reshape(POS, COUT).astype(BF16)

    for which in (2, 0, 1, 3):
        ky = (xa, xb, xo, x)[which]
        for pair in range(2):
            a, b = [nn(coarse[...], window(ky, kx)) for kx in (2 * pair, 2 * pair + 1)]
            slabs = (a[:, :128], jnp.concatenate([a[:, 128:], b[:, :64]], 1), b[:, 64:])
            for n, slab in enumerate(slabs):
                p = 3 * pair + n
                part[ky, p] = slab.astype(BF16)
                if which < 3:
                    along_x(p, which)

    def picked(count, size):
        row = lax.broadcasted_iota(jnp.int32, (count, size), 0)
        col = lax.broadcasted_iota(jnp.int32, (count, size), 1)
        return (row == col + size * rank).astype(F32).astype(BF16)

    pick = picked(CIN, OWN_IN)
    for t in range(16):
        own_up[t] = nn(up_w[t // 4, t % 4], pick).astype(BF16)

    total = None
    for t in range(16):
        term = nn(window(t // 4, t % 4), own_up[t])
        total = term if total is None else total + term
    c_pos[...] = total

    pick = picked(COUT, OWN_OUT)
    for t in range(9):
        mine[t] = nn(conv_w[t // 3, t % 3], pick).astype(BF16)

    @pl.loop(0, 22)
    def _(n):
        v = hid[1, pl.ds(n * 6, 6)].astype(F32).reshape(6, 2, H, COUT)
        above, _, below = shifted(v)
        hid[0, pl.ds(n * 6, 6)] = above
        hid[2, pl.ds(n * 6, 6)] = below

    def refine(n):
        acc = None
        for t in range(9):
            term = nn(hid[t // 3, pl.ds(16 * n + t % 3, 16)].reshape(256, COUT), mine[t])
            acc = term if acc is None else acc + term
        r_pos[pl.ds(256 * n, 256), :] = acc + own_bias


    for d in far_first:
        zz = lax.rem(z + d, nz)
        acc = part[x, zz].astype(F32)
        for which in range(3):
            arrived(rx1.at[zz, which], x1r.at[zz, which])
            acc = acc + rx1[zz, which].astype(F32)
        if d > 0:
            sb2[d] = acc.astype(BF16)
            send(sb2.at[d], rz.at[d], zs_s.at[d], zs_r.at[d], zdev[d])
        else:
            kept[...] = acc
    for n in range(8):
        refine(n)
    acc = kept[...]
    for d in near_first[1:]:
        arrived(rz.at[d], zs_r.at[d])
        acc = acc + rz[d].astype(F32)
    ys[...] = acc
    send(ys, yr, y_sem.at[0], y_sem.at[1], ydev)
    arrived(yr, y_sem.at[1])
    res[x, z] = (acc + yr[...]).astype(BF16)
    here = res.at[x, z]
    for d in near_first[1:]:
        send(here, here, azs.at[d], azr.at[d], zdev[d])

    def direct(d):
        return d == nz // 2

    def spread_x(d):
        zz = lax.rem(z + nz - d, nz)
        got = res.at[x, zz]
        if d > 0:
            arrived(got, azr.at[d])
        if direct(d):
            send(got, got, axs.at[2, d], axr.at[2, d], dev(xo, z, y))
        send(got, got, axs.at[0, d], axr.at[0, d], dev(second(zz), z, y))
        send(got, got, axs.at[1, d], axr.at[1, d], dev(first(zz), z, y))

    def forward_x(d):
        zz = lax.rem(z + nz - d, nz)
        got = res.at[second(zz), zz]
        arrived(got, axr.at[0, d])
        if not direct(d):
            send(got, got, axs.at[2, d], axr.at[2, d], dev(first(zz), z, y))

    lag = 3
    for n in range(nz + lag):
        if n < nz:
            spread_x(near_first[n])
        if n == 0:
            for r in range(2):
                for i in range(H):
                    g32[pl.ds(2 * i + r, OWN_OUT, stride=16), :] = r_pos[pl.ds(8 * r + i, 128, stride=16), :].T
            refined[...] = g32[...].reshape(OWN_OUT, 16, 128).astype(BF16)
            for i in range(H):
                c_grad[i] = c_pos[pl.ds(i, WC, stride=H), :].astype(BF16)
        if n >= lag:
            forward_x(near_first[n - lag])
    for d in near_first:
        zz = lax.rem(z + nz - d, nz)
        arrived(res.at[first(zz), zz], axr.at[1, d])
        arrived(res.at[xo, zz], axr.at[2, d])
    for copy in started:
        copy.wait_send()


def strip(dims, *args):
    nx, nz, ny = dims
    dma = pltpu.SemaphoreType.DMA
    vm = pltpu.VMEM
    hbm = pl.BlockSpec(memory_space=pltpu.HBM)
    return pl.pallas_call(
        functools.partial(kernel, dims),
        out_shape=(
            jax.ShapeDtypeStruct((OWN_OUT, 2 * H, 2 * WC), BF16),
            jax.ShapeDtypeStruct((H, WC, OWN_IN), BF16),
            jax.ShapeDtypeStruct((nx, nz, PIECE, 128), BF16),
        ),
        in_specs=[hbm] * 6,
        out_specs=[VM] * 3,
        scratch_shapes=[
            vm((1, COUT), F32),
            vm((1, COUT), F32),
            vm((H, WC, OWN_IN), BF16),
            vm((OWN_OUT, 2 * H, 2 * WC), BF16),
            vm((OWN_IN, POS), BF16),
            vm((OWN_OUT, FINE), BF16),
            vm((3 * OWN_OUT, FINE), BF16),
            vm((2, 16, OWN_IN), BF16),
            vm((2, 16, 128), BF16),
            vm((OWN_OUT * 2 * H, 2 * WC), F32),
            vm((CIN, POS), BF16),
            vm((COUT, FINE), BF16),
            vm((2, 4, 16, OWN_IN), BF16),
            vm((2, 4, 16, 128), BF16),
            vm((4, 4, COUT, CIN), BF16),
            vm((3, 3, COUT, COUT), BF16),
            vm((9 * 256, COUT), BF16),
            vm((9, COUT, OWN_OUT), BF16),
            vm((16, COUT, OWN_IN), BF16),
            vm((68, H, CIN), F32),
            vm((528, 6 * CIN), BF16),
            vm((66, 2, 2, H, COUT), F32),
            vm((66, 2, 2, H, COUT), F32),
            vm((3, 132, 16, COUT), BF16),
            vm((132, 16, 3 * 256), BF16),
            vm((2, 4, 66, H, COUT), F32),
            vm((nx, nz, PIECE, 128), BF16),
            vm((FINE, OWN_OUT), F32),
            vm((POS, OWN_IN), F32),
            vm((nz, 3, PIECE, 128), BF16),
            vm((PIECE, 128), F32),
            vm((nz, PIECE, 128), BF16),
            vm((nz, PIECE, 128), BF16),
            vm((PIECE, 128), F32),
            vm((PIECE, 128), F32),
            dma((6,)), dma((3, 2)), dma((3, 2)), dma((3, PIECES)), dma((3, PIECES)), dma((2, 2, 4)), dma((2, 2, 4)),
            dma((nz, 3)), dma((nz, 3)), dma((nz,)), dma((nz,)), dma((2,)),
            dma((nz,)), dma((nz,)), dma((3, nz)), dma((3, nz)),
        ],
        compiler_params=pltpu.CompilerParams(
            collective_id=0, has_side_effects=True, vmem_limit_bytes=LIMIT
        ),
        name="strip",
    )(*args)


def unpack_kernel(refined, c_grad, sums, refined_out, c_out, up_grad, conv_grad, ref, cg, src, up, conv, sems, out_sems):
    nx = sums.shape[0]
    loads = [pltpu.make_async_copy(sums.at[k], src.at[k], sems.at[k]) for k in range(nx)]
    loads += [
        pltpu.make_async_copy(refined, ref, sems.at[nx]),
        pltpu.make_async_copy(c_grad, cg, sems.at[nx + 1]),
    ]
    for copy in loads:
        copy.start()
    passes = [
        pltpu.make_async_copy(ref, refined_out, out_sems.at[nx]),
        pltpu.make_async_copy(cg, c_out, out_sems.at[nx + 1]),
    ]
    for ky in range(4):
        loads[ky].wait()
        for pair in range(2):
            a, m, b = [src[ky, 3 * pair + n].astype(F32) for n in range(3)]
            up[ky, 2 * pair] = jnp.concatenate([a, m[:, :64]], 1)
            up[ky, 2 * pair + 1] = jnp.concatenate([m[:, 64:], b], 1)
        copy = pltpu.make_async_copy(up.at[ky], up_grad.at[ky], out_sems.at[ky])
        copy.start()
        passes.append(copy)

    for load, copy in zip(loads[nx:], passes):
        load.wait()
        copy.start()

    def block(b):
        return src[b // 4, 6 + b % 4 // 2, pl.ds(b % 2 * OWN_OUT, OWN_OUT), :].astype(F32)

    for t in range(9):
        tail = block(9 + t // 2)[:, 64 * (t % 2):64 * (t % 2) + 64]
        conv[t // 3, t % 3] = jnp.concatenate([block(t), tail], 1)
    copy = pltpu.make_async_copy(conv, conv_grad, out_sems.at[nx + 2])
    copy.start()
    for copy in passes + [copy]:
        copy.wait()


def unpack(refined, c_grad, sums):
    any_ = pl.BlockSpec(memory_space=pl.ANY)
    hbm = pl.BlockSpec(memory_space=pltpu.HBM)
    up = (4, 4, OWN_IN, COUT)
    conv = (3, 3, OWN_OUT, COUT)
    return pl.pallas_call(
        unpack_kernel,
        out_shape=(
            jax.ShapeDtypeStruct(refined.shape, BF16),
            jax.ShapeDtypeStruct(c_grad.shape, BF16),
            jax.ShapeDtypeStruct(up, F32),
            jax.ShapeDtypeStruct(conv, F32),
        ),
        in_specs=[any_] * 3,
        out_specs=[hbm] * 4,
        scratch_shapes=[
            pltpu.VMEM(refined.shape, BF16),
            pltpu.VMEM(c_grad.shape, BF16),
            pltpu.VMEM(sums.shape, BF16),
            pltpu.VMEM(up, F32),
            pltpu.VMEM(conv, F32),
            pltpu.SemaphoreType.DMA((6,)),
            pltpu.SemaphoreType.DMA((7,)),
        ],
        compiler_params=pltpu.CompilerParams(vmem_limit_bytes=12 << 20),
        name="unpack",
    )(refined, c_grad, sums)


def local(dims, coarse, up_weight, up_bias, conv_weight, conv_bias, cotangent):
    refined, c_grad, sums = strip(
        dims, coarse.transpose(1, 2, 0), cotangent, up_weight.transpose(0, 1, 3, 2), conv_weight,
        up_bias.reshape(1, COUT), conv_bias.reshape(1, COUT),
    )
    refined, c_grad, up_grad, conv_grad = unpack(refined, c_grad, sums)
    return refined, c_grad.transpose(2, 0, 1), up_grad, conv_grad.transpose(0, 1, 3, 2)


def solution(mesh):
    dims = (4, 8, 2)
    placed = (P("chan", None, "lon"), P(), P(), P(), P(), P("chan", None, "lon"))
    return jax.shard_map(
        functools.partial(local, dims),
        mesh=mesh,
        in_specs=placed,
        out_specs=(
            P("chan", None, "lon"),
            P("chan", None, "lon"),
            P(None, None, "chan", None),
            P(None, None, None, "chan"),
        ),
        check_vma=False,
    )
```

```python
import functools

import jax
import jax.numpy as jnp
from jax import lax
from jax.experimental import pallas as pl
from jax.experimental.pallas import tpu as pltpu
from jax.sharding import PartitionSpec as P

MESH = pl.DeviceIdType.MESH
F32, BF16 = jnp.float32, jnp.bfloat16
VM = pl.BlockSpec(memory_space=pltpu.VMEM)
CIN, COUT, H, WC = 384, 192, 8, 64
OWN_IN, OWN_OUT = CIN // 4, COUT // 4
POS, FINE = H * WC, 4 * H * WC
PIECE = 96
LIMIT = 60 << 20


def nn(a, b):
    return jnp.dot(a, b, preferred_element_type=F32)


def nt(a, b):
    return lax.dot_general(a, b, (((1,), (1,)), ((), ())), preferred_element_type=F32)


def down(v):
    row = lax.broadcasted_iota(jnp.int32, v.shape, v.ndim - 2)
    return jnp.where(row == 0, 0.0, pltpu.roll(v, 1, v.ndim - 2))


def up(v):
    row = lax.broadcasted_iota(jnp.int32, v.shape, v.ndim - 2)
    return jnp.where(row == H - 1, 0.0, pltpu.roll(v, H - 1, v.ndim - 2))


PIECES = 4


def shifted(v):
    even, odd = v[:, 0], v[:, 1]
    pairs = ((down(odd), even), (even, odd), (odd, up(even)))
    return [jnp.concatenate(pair, 1).astype(BF16) for pair in pairs]


def kernel(dims, coarse_hbm, cot_hbm, up_hbm, conv_hbm, up_b_hbm, conv_b_hbm,
           refined, c_grad, res,
           up_b, conv_b, coarse_in, cot_in, coarse, cot, cot3, c_end, g_end, g32, c_all, g_all, ce_all, ge_all, up_w, conv_w, conv_t, mine, own_up,
           xf, xl, pre, fs, hid, cots, df, part, r_pos, c_pos,
           rx1, kept, sb2, rz, ys, yr,
           w_sem, cs, cr, gs, gr, es, er, x1s, x1r, zs_s, zs_r, y_sem,
           azs, azr, axs, axr):
    nx, nz, ny = dims
    lon, rank = lax.axis_index("lon"), lax.axis_index("chan")
    n_lon = nx * nz * ny
    x, z, y = lon // (nz * ny), lax.rem(lon // ny, nz), lax.rem(lon, ny)
    far, core = rank // 2, lax.rem(rank, 2)
    sib, cross = far * 2 + 1 - core, (1 - far) * 2 + core
    diag = (1 - far) * 2 + 1 - core
    sides = (lax.rem(lon + 1, n_lon), lax.rem(lon + n_lon - 1, n_lon))
    xa, xb = x + 1 - 2 * lax.rem(x, 2), 3 - x
    xo = lax.rem(x + 2, 4)

    def dev(px, pz, py):
        return ((px * nz + pz) * ny + py, rank)

    def first(zz):
        return xa + lax.rem(zz, 2) * (xb - xa)

    def second(zz):
        return xb + lax.rem(zz, 2) * (xa - xb)

    near_first = sorted(range(nz), key=lambda d: min(d, nz - d))
    far_first = near_first[::-1]
    zdev = [dev(x, lax.rem(z + d, nz), y) for d in range(nz)]
    ydev = dev(x, z, 1 - y)

    loads = [
        pltpu.make_async_copy(coarse_hbm, coarse_in, w_sem.at[0]),
        pltpu.make_async_copy(cot_hbm, cot_in, w_sem.at[1]),
        pltpu.make_async_copy(up_hbm, up_w, w_sem.at[2]),
        pltpu.make_async_copy(conv_hbm, conv_w, w_sem.at[3]),
        pltpu.make_async_copy(up_b_hbm, up_b, w_sem.at[4]),
        pltpu.make_async_copy(conv_b_hbm, conv_b, w_sem.at[5]),
    ]
    for load in loads:
        load.start()

    barrier = pltpu.get_barrier_semaphore()
    greet = [zdev[d] for d in far_first[:-1]]
    greet += [(side, lax.rem(rank + d, 4)) for side in sides for d in range(4)]
    greet += [dev(xo, z, y), dev(xa, z, y), dev(xb, z, y)]
    greet += [(lon, lax.rem(rank + d, 4)) for d in range(1, 4)]
    for peer in greet:
        pl.semaphore_signal(barrier, inc=1, device_id=peer, device_id_type=MESH)

    loads[0].wait()
    for i in range(H):
        c_pos[pl.ds(i, WC, stride=H), :] = coarse_in[i].astype(F32)
    for n in range(4):
        coarse[:, pl.ds(128 * n, 128)] = c_pos[pl.ds(128 * n, 128), :].T.astype(BF16)
    c_end[0] = c_pos[pl.ds(POS - 16, 16), :].astype(BF16)
    c_end[1] = c_pos[pl.ds(0, 16), :].astype(BF16)
    loads[1].wait()
    g32[...] = cot_in[...].astype(F32).reshape(OWN_OUT * 16, 128)
    for r in range(2):
        for i in range(H):
            r_pos[pl.ds(8 * r + i, 128, stride=16), :] = g32[pl.ds(2 * i + r, OWN_OUT, stride=16), :].T
    for n in range(16):
        cot[:, pl.ds(128 * n, 128)] = r_pos[pl.ds(128 * n, 128), :].T.astype(BF16)
    gap = jnp.zeros((16, 64 - OWN_OUT), F32)
    for n, at in enumerate((FINE - 32, 0)):
        two = [r_pos[pl.ds(at, 16), :], gap, r_pos[pl.ds(at + 16, 16), :], gap]
        g_end[n] = jnp.concatenate(two, 1).astype(BF16)
    pl.semaphore_wait(barrier, len(greet))

    started = []

    def copy_of(a, b, s, r, to):
        return pltpu.make_async_remote_copy(
            src_ref=a, dst_ref=b, send_sem=s, recv_sem=r, device_id=to, device_id_type=MESH
        )

    def send(a, b, s, r, to):
        copy = copy_of(a, b, s, r, to)
        copy.start()
        started.append(copy)

    def arrived(b, r):
        copy_of(b, b, r, r, (lon, sib)).wait_recv()

    c_width = POS // 2

    def c_block(r, k):
        rows = pl.ds(pl.multiple_of(r * OWN_IN, 16), OWN_IN)
        return c_all.at[rows, pl.ds(k * c_width, c_width)]

    width = FINE // PIECES

    def g_block(r, k):
        return g_all.at[pl.ds(pl.multiple_of(r * OWN_OUT, 16), OWN_OUT), pl.ds(k * width, width)]

    c_own = [coarse.at[:, pl.ds(k * c_width, c_width)] for k in range(2)]
    for k in range(2):
        send(c_own[k], c_block(rank, k), cs.at[0, k], cr.at[0, k], (lon, cross))
    for n, side in enumerate(sides):
        for d in range(4):
            to = (side, lax.rem(rank + d, 4))
            send(c_end.at[n], ce_all.at[n, rank], es.at[0, n, d], er.at[0, n, d], to)
    for k in range(2):
        send(c_own[k], c_block(rank, k), cs.at[1, k], cr.at[1, k], (lon, sib))
    for n, side in enumerate(sides):
        for d in range(4):
            to = (side, lax.rem(rank + d, 4))
            send(g_end.at[n], ge_all.at[n, rank], es.at[1, n, d], er.at[1, n, d], to)
    for k in range(PIECES):
        own_part = cot.at[:, pl.ds(k * width, width)]
        send(own_part, g_block(rank, k), gs.at[0, k], gr.at[0, k], (lon, cross))
        send(own_part, g_block(rank, k), gs.at[1, k], gr.at[1, k], (lon, sib))
    c_all[pl.ds(pl.multiple_of(rank * OWN_IN, 16), OWN_IN), :] = coarse[...]
    g_all[pl.ds(pl.multiple_of(rank * OWN_OUT, 16), OWN_OUT), :] = cot[...]

    def pass_on(k):
        arrived(g_block(cross, k), gr.at[0, k])
        send(g_block(cross, k), g_block(cross, k), gs.at[2, k], gr.at[2, k], (lon, sib))

    pad = jnp.zeros((132, 16, 64), BF16)
    for m in range(3):
        cots[:, :, pl.ds(256 * m + COUT, 64)] = pad
    conv_t[...] = jnp.zeros(conv_t.shape, BF16)
    cot3[pl.ds(OWN_OUT, OWN_OUT), :] = cot[...]
    for m in (0, 2):
        for r in range(2):
            for i in range(H):
                p = 2 * i + r + m - 1
                rows = pl.ds(8 * r + i, 128, stride=16)
                if 0 <= p < 16:
                    r_pos[rows, :] = g32[pl.ds(p, OWN_OUT, stride=16), :].T
                else:
                    r_pos[rows, :] = jnp.zeros((128, OWN_OUT), F32)
        for n in range(16):
            cot3[pl.ds(OWN_OUT * m, OWN_OUT), pl.ds(128 * n, 128)] = r_pos[pl.ds(128 * n, 128), :].T.astype(BF16)

    for load in loads[2:]:
        load.wait()
    own_bias = jnp.zeros((1, OWN_OUT), F32)
    for r in range(4):
        own_bias += jnp.where(rank == r, conv_b[:, pl.ds(OWN_OUT * r, OWN_OUT)], 0.0)
    for t in range(9):
        w = conv_w[t // 3, t % 3]
        conv_t[pl.ds(768 * (t % 3) + 256 * (2 - t // 3), COUT), :] = w.astype(F32).T.astype(BF16)

    for k in range(2):
        arrived(c_block(cross, k), cr.at[0, k])
        send(c_block(cross, k), c_block(cross, k), cs.at[2, k], cr.at[2, k], (lon, sib))
    for k in range(2):
        arrived(c_block(sib, k), cr.at[1, k])
        arrived(c_block(diag, k), cr.at[2, k])
        for b in (2 * k, 2 * k + 1):
            xf[pl.ds(1 + 16 * b, 16)] = c_all[:, pl.ds(128 * b, 128)].astype(F32).T.reshape(16, H, CIN)
    for n in range(2):
        for d in range(4):
            arrived(ce_all.at[n, lax.rem(rank + 4 - d, 4)], er.at[0, n, d])
    left, right = [
        jnp.concatenate([ce_all[n, r].astype(F32) for r in range(4)], 1) for n in range(2)
    ]
    xf[0] = left[8:]
    xf[65] = right[:8]
    xf[66:68] = jnp.zeros((2, H, CIN), F32)

    @pl.loop(0, 3)
    def _(n):
        t0 = n * 22
        rows = pl.ds(pl.multiple_of(t0 * H, 16), 22 * H)
        for d in range(2):
            v = xf[pl.ds(t0 + 1 - d, 22)]
            for s, w in enumerate((down(v), v, up(v))):
                xl[rows, pl.ds((2 * s + d) * CIN, CIN)] = w.reshape(22 * H, CIN).astype(BF16)

    pass_on(0)
    for rp in range(2):
        for cp in range(2):
            taps = ((3, 1), (2, 0))[rp]
            w = jnp.concatenate([up_w[ky, cp + 2 * d] for ky in taps for d in range(2)], 1)
            val = nt(xl[:, pl.ds(rp * 2 * CIN, 4 * CIN)], w)
            pre[:, cp, rp] = val.reshape(66, H, COUT)
        pass_on(1 + rp)

    bias = up_b[...].reshape(1, 1, 1, 1, COUT)

    def activate(n):
        ts = pl.ds(n * 3, 3)
        v = pre[ts] + bias
        s = jax.nn.sigmoid(v)
        fs[ts] = s * (1.0 + v * (1.0 - s))
        h = (v * s).astype(BF16).astype(F32).reshape(6, 2, H, COUT)
        hid[1, pl.ds(n * 6, 6)] = h.reshape(6, 16, COUT).astype(BF16)

    pass_on(3)
    pl.loop(0, 22)(activate)

    peers = (xa, xb, xo)

    def along_x(p, which):
        send(part.at[peers[which], p], rx1.at[p, which], x1s.at[p, which], x1r.at[p, which],
             dev(peers[which], z, y))

    def spot(b):
        return b // 4, 6 + b % 4 // 2, pl.ds(b % 2 * OWN_OUT, OWN_OUT)

    def put(b, v):
        c, p, rows = spot(b)
        part[c, p, rows, :] = v.astype(BF16)

    tails = []
    taps = [nn(cot3[...], hid[1, pl.ds(kx, 128)].reshape(FINE, COUT)) for kx in range(3)]
    for t in range(9):
        g = taps[t % 3][OWN_OUT * (2 - t // 3):OWN_OUT * (3 - t // 3)]
        put(t, g[:, :128])
        tails.append(g[:, 128:])
    tails.append(jnp.zeros((OWN_OUT, 64), F32))
    for u in range(5):
        put(9 + u, jnp.concatenate(tails[2 * u:2 * u + 2], 1))
    for b in (14, 15):
        put(b, jnp.zeros((OWN_OUT, 128), F32))
    for p in (6, 7):
        for which in (2, 0, 1):
            along_x(p, which)

    def place_cot(at, v, n):
        for m, w in enumerate(shifted(v.reshape(n, 2, H, COUT))):
            cots[pl.ds(at, n), :, pl.ds(256 * m, COUT)] = w

    def place_edge(n):
        for d in range(4):
            arrived(ge_all.at[n, lax.rem(rank + 4 - d, 4)], er.at[1, n, d])
        cols = []
        for h in (0, 64):
            block = [ge_all[n, r][:, h:h + OWN_OUT].astype(F32) for r in range(4)]
            cols.append(jnp.concatenate(block, 1))
        place_cot(130 * n, jnp.concatenate(cols, 0), 2)

    def place_piece(k):
        arrived(g_block(sib, k), gr.at[1, k])
        arrived(g_block(diag, k), gr.at[2, k])
        for b in range(4 * k, 4 * k + 4):
            place_cot(2 + 8 * b, g_all[:, pl.ds(128 * b, 128)].astype(F32).T, 8)

    def adjoint(n):
        g = [cots[pl.ds(n * 26 + 2 - kx, 26)].reshape(416, 768) for kx in range(3)]
        acc = nn(jnp.concatenate(g, 1), conv_t[...])
        ts = pl.ds(n * 13, 13)
        d = (acc.reshape(13, 2, 2, H, COUT) * fs[ts]).astype(BF16).astype(F32)
        for cp in range(2):
            even, odd = d[:, cp, 0], d[:, cp, 1]
            for ky, v in enumerate((down(odd), even, odd, up(even))):
                df[cp, ky, ts] = v

    place_edge(0)
    place_piece(0)
    place_piece(1)
    pl.loop(0, 2)(adjoint)
    place_edge(1)
    place_piece(2)
    place_piece(3)
    pl.loop(2, 5)(adjoint)

    def window(ky, kx):
        return df[kx % 2, ky, pl.ds(kx // 2, 64)].reshape(POS, COUT).astype(BF16)

    for which in (2, 0, 1, 3):
        ky = (xa, xb, xo, x)[which]
        for pair in range(2):
            a, b = [nn(coarse[...], window(ky, kx)) for kx in (2 * pair, 2 * pair + 1)]
            slabs = (a[:, :128], jnp.concatenate([a[:, 128:], b[:, :64]], 1), b[:, 64:])
            for n, slab in enumerate(slabs):
                p = 3 * pair + n
                part[ky, p] = slab.astype(BF16)
                if which < 3:
                    along_x(p, which)

    def picked(count, size):
        row = lax.broadcasted_iota(jnp.int32, (count, size), 0)
        col = lax.broadcasted_iota(jnp.int32, (count, size), 1)
        return (row == col + size * rank).astype(F32).astype(BF16)

    pick = picked(CIN, OWN_IN)
    for t in range(16):
        own_up[t] = nn(up_w[t // 4, t % 4], pick).astype(BF16)

    total = None
    for t in range(16):
        term = nn(window(t // 4, t % 4), own_up[t])
        total = term if total is None else total + term
    c_pos[...] = total

    pick = picked(COUT, OWN_OUT)
    for t in range(9):
        mine[t] = nn(conv_w[t // 3, t % 3], pick).astype(BF16)

    @pl.loop(0, 22)
    def _(n):
        v = hid[1, pl.ds(n * 6, 6)].astype(F32).reshape(6, 2, H, COUT)
        above, _, below = shifted(v)
        hid[0, pl.ds(n * 6, 6)] = above
        hid[2, pl.ds(n * 6, 6)] = below

    def refine(n):
        acc = None
        for t in range(9):
            term = nn(hid[t // 3, pl.ds(16 * n + t % 3, 16)].reshape(256, COUT), mine[t])
            acc = term if acc is None else acc + term
        r_pos[pl.ds(256 * n, 256), :] = acc + own_bias


    for d in far_first:
        zz = lax.rem(z + d, nz)
        acc = part[x, zz].astype(F32)
        for which in range(3):
            arrived(rx1.at[zz, which], x1r.at[zz, which])
            acc = acc + rx1[zz, which].astype(F32)
        if d > 0:
            sb2[d] = acc.astype(BF16)
            send(sb2.at[d], rz.at[d], zs_s.at[d], zs_r.at[d], zdev[d])
        else:
            kept[...] = acc
    for n in range(8):
        refine(n)
    acc = kept[...]
    for d in near_first[1:]:
        arrived(rz.at[d], zs_r.at[d])
        acc = acc + rz[d].astype(F32)
    ys[...] = acc
    send(ys, yr, y_sem.at[0], y_sem.at[1], ydev)
    arrived(yr, y_sem.at[1])
    res[x, z] = (acc + yr[...]).astype(BF16)
    here = res.at[x, z]
    for d in near_first[1:]:
        send(here, here, azs.at[d], azr.at[d], zdev[d])

    def direct(d):
        return min(d, nz - d) >= 3

    def spread_x(d):
        zz = lax.rem(z + nz - d, nz)
        got = res.at[x, zz]
        if d > 0:
            arrived(got, azr.at[d])
        if direct(d):
            send(got, got, axs.at[2, d], axr.at[2, d], dev(xo, z, y))
        send(got, got, axs.at[0, d], axr.at[0, d], dev(second(zz), z, y))
        send(got, got, axs.at[1, d], axr.at[1, d], dev(first(zz), z, y))

    def forward_x(d):
        zz = lax.rem(z + nz - d, nz)
        got = res.at[second(zz), zz]
        arrived(got, axr.at[0, d])
        if not direct(d):
            send(got, got, axs.at[2, d], axr.at[2, d], dev(first(zz), z, y))

    lag = 4
    for n in range(nz + lag):
        if n < nz:
            spread_x(near_first[n])
        if n == 0:
            for r in range(2):
                for i in range(H):
                    g32[pl.ds(2 * i + r, OWN_OUT, stride=16), :] = r_pos[pl.ds(8 * r + i, 128, stride=16), :].T
            refined[...] = g32[...].reshape(OWN_OUT, 16, 128).astype(BF16)
            for i in range(H):
                c_grad[i] = c_pos[pl.ds(i, WC, stride=H), :].astype(BF16)
        if n >= lag:
            forward_x(near_first[n - lag])
    for d in near_first:
        zz = lax.rem(z + nz - d, nz)
        arrived(res.at[first(zz), zz], axr.at[1, d])
        arrived(res.at[xo, zz], axr.at[2, d])
    for copy in started:
        copy.wait_send()


def strip(dims, *args):
    nx, nz, ny = dims
    dma = pltpu.SemaphoreType.DMA
    vm = pltpu.VMEM
    any_ = pl.BlockSpec(memory_space=pl.ANY)
    return pl.pallas_call(
        functools.partial(kernel, dims),
        out_shape=(
            jax.ShapeDtypeStruct((OWN_OUT, 2 * H, 2 * WC), BF16),
            jax.ShapeDtypeStruct((H, WC, OWN_IN), BF16),
            jax.ShapeDtypeStruct((nx, nz, PIECE, 128), BF16),
        ),
        in_specs=[any_] * 6,
        out_specs=[VM] * 3,
        scratch_shapes=[
            vm((1, COUT), F32),
            vm((1, COUT), F32),
            vm((H, WC, OWN_IN), BF16),
            vm((OWN_OUT, 2 * H, 2 * WC), BF16),
            vm((OWN_IN, POS), BF16),
            vm((OWN_OUT, FINE), BF16),
            vm((3 * OWN_OUT, FINE), BF16),
            vm((2, 16, OWN_IN), BF16),
            vm((2, 16, 128), BF16),
            vm((OWN_OUT * 2 * H, 2 * WC), F32),
            vm((CIN, POS), BF16),
            vm((COUT, FINE), BF16),
            vm((2, 4, 16, OWN_IN), BF16),
            vm((2, 4, 16, 128), BF16),
            vm((4, 4, COUT, CIN), BF16),
            vm((3, 3, COUT, COUT), BF16),
            vm((9 * 256, COUT), BF16),
            vm((9, COUT, OWN_OUT), BF16),
            vm((16, COUT, OWN_IN), BF16),
            vm((68, H, CIN), F32),
            vm((528, 6 * CIN), BF16),
            vm((66, 2, 2, H, COUT), F32),
            vm((66, 2, 2, H, COUT), F32),
            vm((3, 132, 16, COUT), BF16),
            vm((132, 16, 3 * 256), BF16),
            vm((2, 4, 66, H, COUT), F32),
            vm((nx, nz, PIECE, 128), BF16),
            vm((FINE, OWN_OUT), F32),
            vm((POS, OWN_IN), F32),
            vm((nz, 3, PIECE, 128), BF16),
            vm((PIECE, 128), F32),
            vm((nz, PIECE, 128), BF16),
            vm((nz, PIECE, 128), BF16),
            vm((PIECE, 128), F32),
            vm((PIECE, 128), F32),
            dma((6,)), dma((3, 2)), dma((3, 2)), dma((3, PIECES)), dma((3, PIECES)), dma((2, 2, 4)), dma((2, 2, 4)),
            dma((nz, 3)), dma((nz, 3)), dma((nz,)), dma((nz,)), dma((2,)),
            dma((nz,)), dma((nz,)), dma((3, nz)), dma((3, nz)),
        ],
        compiler_params=pltpu.CompilerParams(
            collective_id=0, has_side_effects=True, vmem_limit_bytes=LIMIT
        ),
        name="strip",
    )(*args)


def unpack_kernel(refined, c_grad, sums, refined_out, c_out, up_grad, conv_grad, ref, cg, src, up, conv, sems, out_sems):
    nx = sums.shape[0]
    loads = [pltpu.make_async_copy(sums.at[k], src.at[k], sems.at[k]) for k in range(nx)]
    loads += [
        pltpu.make_async_copy(refined, ref, sems.at[nx]),
        pltpu.make_async_copy(c_grad, cg, sems.at[nx + 1]),
    ]
    for copy in loads:
        copy.start()
    passes = [
        pltpu.make_async_copy(ref, refined_out, out_sems.at[nx]),
        pltpu.make_async_copy(cg, c_out, out_sems.at[nx + 1]),
    ]
    for ky in range(4):
        loads[ky].wait()
        for pair in range(2):
            a, m, b = [src[ky, 3 * pair + n].astype(F32) for n in range(3)]
            up[ky, 2 * pair] = jnp.concatenate([a, m[:, :64]], 1)
            up[ky, 2 * pair + 1] = jnp.concatenate([m[:, 64:], b], 1)
        copy = pltpu.make_async_copy(up.at[ky], up_grad.at[ky], out_sems.at[ky])
        copy.start()
        passes.append(copy)

    for load, copy in zip(loads[nx:], passes):
        load.wait()
        copy.start()

    def block(b):
        return src[b // 4, 6 + b % 4 // 2, pl.ds(b % 2 * OWN_OUT, OWN_OUT), :].astype(F32)

    for t in range(9):
        tail = block(9 + t // 2)[:, 64 * (t % 2):64 * (t % 2) + 64]
        conv[t // 3, t % 3] = jnp.concatenate([block(t), tail], 1)
    copy = pltpu.make_async_copy(conv, conv_grad, out_sems.at[nx + 2])
    copy.start()
    for copy in passes + [copy]:
        copy.wait()


def unpack(refined, c_grad, sums):
    any_ = pl.BlockSpec(memory_space=pl.ANY)
    up = (4, 4, OWN_IN, COUT)
    conv = (3, 3, OWN_OUT, COUT)
    return pl.pallas_call(
        unpack_kernel,
        out_shape=(
            jax.ShapeDtypeStruct(refined.shape, BF16),
            jax.ShapeDtypeStruct(c_grad.shape, BF16),
            jax.ShapeDtypeStruct(up, F32),
            jax.ShapeDtypeStruct(conv, F32),
        ),
        in_specs=[any_] * 3,
        out_specs=[any_] * 4,
        scratch_shapes=[
            pltpu.VMEM(refined.shape, BF16),
            pltpu.VMEM(c_grad.shape, BF16),
            pltpu.VMEM(sums.shape, BF16),
            pltpu.VMEM(up, F32),
            pltpu.VMEM(conv, F32),
            pltpu.SemaphoreType.DMA((6,)),
            pltpu.SemaphoreType.DMA((7,)),
        ],
        compiler_params=pltpu.CompilerParams(vmem_limit_bytes=LIMIT),
        name="unpack",
    )(refined, c_grad, sums)


def local(dims, coarse, up_weight, up_bias, conv_weight, conv_bias, cotangent):
    refined, c_grad, sums = strip(
        dims, coarse.transpose(1, 2, 0), cotangent, up_weight.transpose(0, 1, 3, 2), conv_weight,
        up_bias.reshape(1, COUT), conv_bias.reshape(1, COUT),
    )
    refined, c_grad, up_grad, conv_grad = unpack(refined, c_grad, sums)
    return refined, c_grad.transpose(2, 0, 1), up_grad, conv_grad.transpose(0, 1, 3, 2)


def solution(mesh):
    dims = (4, 8, 2)
    placed = (P("chan", None, "lon"), P(), P(), P(), P(), P("chan", None, "lon"))
    return jax.shard_map(
        functools.partial(local, dims),
        mesh=mesh,
        in_specs=placed,
        out_specs=(
            P("chan", None, "lon"),
            P("chan", None, "lon"),
            P(None, None, "chan", None),
            P(None, None, None, "chan"),
        ),
        check_vma=False,
    )
```

```python
import functools

import jax
import jax.numpy as jnp
from jax import lax
from jax.experimental import pallas as pl
from jax.experimental.pallas import tpu as pltpu
from jax.sharding import PartitionSpec as P

MESH = pl.DeviceIdType.MESH
F32, BF16 = jnp.float32, jnp.bfloat16
VM = pl.BlockSpec(memory_space=pltpu.VMEM)
CIN, COUT, H, WC = 384, 192, 8, 64
OWN_IN, OWN_OUT = CIN // 4, COUT // 4
POS, FINE = H * WC, 4 * H * WC
PIECE = 96
LIMIT = 60 << 20


def nn(a, b):
    return jnp.dot(a, b, preferred_element_type=F32)


def nt(a, b):
    return lax.dot_general(a, b, (((1,), (1,)), ((), ())), preferred_element_type=F32)


def down(v):
    row = lax.broadcasted_iota(jnp.int32, v.shape, v.ndim - 2)
    return jnp.where(row == 0, 0.0, pltpu.roll(v, 1, v.ndim - 2))


def up(v):
    row = lax.broadcasted_iota(jnp.int32, v.shape, v.ndim - 2)
    return jnp.where(row == H - 1, 0.0, pltpu.roll(v, H - 1, v.ndim - 2))


PIECES = 4


def shifted(v):
    even, odd = v[:, 0], v[:, 1]
    pairs = ((down(odd), even), (even, odd), (odd, up(even)))
    return [jnp.concatenate(pair, 1).astype(BF16) for pair in pairs]


def kernel(dims, coarse_hbm, cot_hbm, up_hbm, conv_hbm, up_b_hbm, conv_b_hbm,
           refined, c_grad, res,
           up_b, conv_b, coarse_in, cot_in, coarse, cot, cot3, c_end, g_end, g32, c_all, g_all, ce_all, ge_all, up_w, conv_w, conv_t, mine, own_up,
           xf, xl, pre, fs, hid, cots, df, part, r_pos, c_pos,
           rx1, kept, sb2, rz, ys, yr,
           w_sem, cs, cr, gs, gr, es, er, x1s, x1r, zs_s, zs_r, y_sem,
           azs, azr, axs, axr):
    nx, nz, ny = dims
    lon, rank = lax.axis_index("lon"), lax.axis_index("chan")
    n_lon = nx * nz * ny
    x, z, y = lon // (nz * ny), lax.rem(lon // ny, nz), lax.rem(lon, ny)
    far, core = rank // 2, lax.rem(rank, 2)
    sib, cross = far * 2 + 1 - core, (1 - far) * 2 + core
    diag = (1 - far) * 2 + 1 - core
    sides = (lax.rem(lon + 1, n_lon), lax.rem(lon + n_lon - 1, n_lon))
    xa, xb = x + 1 - 2 * lax.rem(x, 2), 3 - x
    xo = lax.rem(x + 2, 4)

    def dev(px, pz, py):
        return ((px * nz + pz) * ny + py, rank)

    def first(zz):
        return xa + lax.rem(zz, 2) * (xb - xa)

    def second(zz):
        return xb + lax.rem(zz, 2) * (xa - xb)

    near_first = sorted(range(nz), key=lambda d: min(d, nz - d))
    far_first = near_first[::-1]
    zdev = [dev(x, lax.rem(z + d, nz), y) for d in range(nz)]
    ydev = dev(x, z, 1 - y)

    loads = [
        pltpu.make_async_copy(coarse_hbm, coarse_in, w_sem.at[0]),
        pltpu.make_async_copy(cot_hbm, cot_in, w_sem.at[1]),
        pltpu.make_async_copy(up_hbm, up_w, w_sem.at[2]),
        pltpu.make_async_copy(conv_hbm, conv_w, w_sem.at[3]),
        pltpu.make_async_copy(up_b_hbm, up_b, w_sem.at[4]),
        pltpu.make_async_copy(conv_b_hbm, conv_b, w_sem.at[5]),
    ]
    for load in loads:
        load.start()

    barrier = pltpu.get_barrier_semaphore()
    greet = [zdev[d] for d in far_first[:-1]]
    greet += [(side, lax.rem(rank + d, 4)) for side in sides for d in range(4)]
    greet += [dev(xo, z, y), dev(xa, z, y), dev(xb, z, y)]
    greet += [(lon, lax.rem(rank + d, 4)) for d in range(1, 4)]
    for peer in greet:
        pl.semaphore_signal(barrier, inc=1, device_id=peer, device_id_type=MESH)

    loads[0].wait()
    for i in range(H):
        c_pos[pl.ds(i, WC, stride=H), :] = coarse_in[i].astype(F32)
    for n in range(4):
        coarse[:, pl.ds(128 * n, 128)] = c_pos[pl.ds(128 * n, 128), :].T.astype(BF16)
    c_end[0] = c_pos[pl.ds(POS - 16, 16), :].astype(BF16)
    c_end[1] = c_pos[pl.ds(0, 16), :].astype(BF16)
    loads[1].wait()
    g32[...] = cot_in[...].astype(F32).reshape(OWN_OUT * 16, 128)
    for r in range(2):
        for i in range(H):
            r_pos[pl.ds(8 * r + i, 128, stride=16), :] = g32[pl.ds(2 * i + r, OWN_OUT, stride=16), :].T
    for n in range(16):
        cot[:, pl.ds(128 * n, 128)] = r_pos[pl.ds(128 * n, 128), :].T.astype(BF16)
    gap = jnp.zeros((16, 64 - OWN_OUT), F32)
    for n, at in enumerate((FINE - 32, 0)):
        two = [r_pos[pl.ds(at, 16), :], gap, r_pos[pl.ds(at + 16, 16), :], gap]
        g_end[n] = jnp.concatenate(two, 1).astype(BF16)
    pl.semaphore_wait(barrier, len(greet))

    started = []

    def copy_of(a, b, s, r, to):
        return pltpu.make_async_remote_copy(
            src_ref=a, dst_ref=b, send_sem=s, recv_sem=r, device_id=to, device_id_type=MESH
        )

    def send(a, b, s, r, to):
        copy = copy_of(a, b, s, r, to)
        copy.start()
        started.append(copy)

    def arrived(b, r):
        copy_of(b, b, r, r, (lon, sib)).wait_recv()

    c_width = POS // 2

    def c_block(r, k):
        rows = pl.ds(pl.multiple_of(r * OWN_IN, 16), OWN_IN)
        return c_all.at[rows, pl.ds(k * c_width, c_width)]

    width = FINE // PIECES

    def g_block(r, k):
        return g_all.at[pl.ds(pl.multiple_of(r * OWN_OUT, 16), OWN_OUT), pl.ds(k * width, width)]

    c_own = [coarse.at[:, pl.ds(k * c_width, c_width)] for k in range(2)]
    for k in range(2):
        send(c_own[k], c_block(rank, k), cs.at[0, k], cr.at[0, k], (lon, cross))
    for n, side in enumerate(sides):
        for d in range(4):
            to = (side, lax.rem(rank + d, 4))
            send(c_end.at[n], ce_all.at[n, rank], es.at[0, n, d], er.at[0, n, d], to)
    for k in range(2):
        send(c_own[k], c_block(rank, k), cs.at[1, k], cr.at[1, k], (lon, sib))
    for n, side in enumerate(sides):
        for d in range(4):
            to = (side, lax.rem(rank + d, 4))
            send(g_end.at[n], ge_all.at[n, rank], es.at[1, n, d], er.at[1, n, d], to)
    for k in range(PIECES):
        own_part = cot.at[:, pl.ds(k * width, width)]
        send(own_part, g_block(rank, k), gs.at[0, k], gr.at[0, k], (lon, cross))
        send(own_part, g_block(rank, k), gs.at[1, k], gr.at[1, k], (lon, sib))
    c_all[pl.ds(pl.multiple_of(rank * OWN_IN, 16), OWN_IN), :] = coarse[...]
    g_all[pl.ds(pl.multiple_of(rank * OWN_OUT, 16), OWN_OUT), :] = cot[...]

    def pass_on(k):
        arrived(g_block(cross, k), gr.at[0, k])
        send(g_block(cross, k), g_block(cross, k), gs.at[2, k], gr.at[2, k], (lon, sib))

    pad = jnp.zeros((132, 16, 64), BF16)
    for m in range(3):
        cots[:, :, pl.ds(256 * m + COUT, 64)] = pad
    conv_t[...] = jnp.zeros(conv_t.shape, BF16)
    cot3[pl.ds(OWN_OUT, OWN_OUT), :] = cot[...]
    for m in (0, 2):
        for r in range(2):
            for i in range(H):
                p = 2 * i + r + m - 1
                rows = pl.ds(8 * r + i, 128, stride=16)
                if 0 <= p < 16:
                    r_pos[rows, :] = g32[pl.ds(p, OWN_OUT, stride=16), :].T
                else:
                    r_pos[rows, :] = jnp.zeros((128, OWN_OUT), F32)
        for n in range(16):
            cot3[pl.ds(OWN_OUT * m, OWN_OUT), pl.ds(128 * n, 128)] = r_pos[pl.ds(128 * n, 128), :].T.astype(BF16)

    for load in loads[2:]:
        load.wait()
    own_bias = jnp.zeros((1, OWN_OUT), F32)
    for r in range(4):
        own_bias += jnp.where(rank == r, conv_b[:, pl.ds(OWN_OUT * r, OWN_OUT)], 0.0)
    for t in range(9):
        w = conv_w[t // 3, t % 3]
        conv_t[pl.ds(768 * (t % 3) + 256 * (2 - t // 3), COUT), :] = w.astype(F32).T.astype(BF16)

    for k in range(2):
        arrived(c_block(cross, k), cr.at[0, k])
        send(c_block(cross, k), c_block(cross, k), cs.at[2, k], cr.at[2, k], (lon, sib))
    for k in range(2):
        arrived(c_block(sib, k), cr.at[1, k])
        arrived(c_block(diag, k), cr.at[2, k])
        for b in (2 * k, 2 * k + 1):
            xf[pl.ds(1 + 16 * b, 16)] = c_all[:, pl.ds(128 * b, 128)].astype(F32).T.reshape(16, H, CIN)
    for n in range(2):
        for d in range(4):
            arrived(ce_all.at[n, lax.rem(rank + 4 - d, 4)], er.at[0, n, d])
    left, right = [
        jnp.concatenate([ce_all[n, r].astype(F32) for r in range(4)], 1) for n in range(2)
    ]
    xf[0] = left[8:]
    xf[65] = right[:8]
    xf[66:68] = jnp.zeros((2, H, CIN), F32)

    @pl.loop(0, 3)
    def _(n):
        t0 = n * 22
        rows = pl.ds(pl.multiple_of(t0 * H, 16), 22 * H)
        for d in range(2):
            v = xf[pl.ds(t0 + 1 - d, 22)]
            for s, w in enumerate((down(v), v, up(v))):
                xl[rows, pl.ds((2 * s + d) * CIN, CIN)] = w.reshape(22 * H, CIN).astype(BF16)

    pass_on(0)
    for rp in range(2):
        for cp in range(2):
            taps = ((3, 1), (2, 0))[rp]
            w = jnp.concatenate([up_w[ky, cp + 2 * d] for ky in taps for d in range(2)], 1)
            val = nt(xl[:, pl.ds(rp * 2 * CIN, 4 * CIN)], w)
            pre[:, cp, rp] = val.reshape(66, H, COUT)
        pass_on(1 + rp)

    bias = up_b[...].reshape(1, 1, 1, 1, COUT)

    def activate(n):
        ts = pl.ds(n * 3, 3)
        v = pre[ts] + bias
        s = jax.nn.sigmoid(v)
        fs[ts] = s * (1.0 + v * (1.0 - s))
        h = (v * s).astype(BF16).astype(F32).reshape(6, 2, H, COUT)
        hid[1, pl.ds(n * 6, 6)] = h.reshape(6, 16, COUT).astype(BF16)

    pass_on(3)
    pl.loop(0, 22)(activate)

    peers = (xa, xb, xo)

    def along_x(p, which):
        send(part.at[peers[which], p], rx1.at[p, which], x1s.at[p, which], x1r.at[p, which],
             dev(peers[which], z, y))

    def spot(b):
        return b // 4, 6 + b % 4 // 2, pl.ds(b % 2 * OWN_OUT, OWN_OUT)

    def put(b, v):
        c, p, rows = spot(b)
        part[c, p, rows, :] = v.astype(BF16)

    tails = []
    taps = [nn(cot3[...], hid[1, pl.ds(kx, 128)].reshape(FINE, COUT)) for kx in range(3)]
    for t in range(9):
        g = taps[t % 3][OWN_OUT * (2 - t // 3):OWN_OUT * (3 - t // 3)]
        put(t, g[:, :128])
        tails.append(g[:, 128:])
    tails.append(jnp.zeros((OWN_OUT, 64), F32))
    for u in range(5):
        put(9 + u, jnp.concatenate(tails[2 * u:2 * u + 2], 1))
    for b in (14, 15):
        put(b, jnp.zeros((OWN_OUT, 128), F32))
    for p in (6, 7):
        for which in (2, 0, 1):
            along_x(p, which)

    def place_cot(at, v, n):
        for m, w in enumerate(shifted(v.reshape(n, 2, H, COUT))):
            cots[pl.ds(at, n), :, pl.ds(256 * m, COUT)] = w

    def place_edge(n):
        for d in range(4):
            arrived(ge_all.at[n, lax.rem(rank + 4 - d, 4)], er.at[1, n, d])
        cols = []
        for h in (0, 64):
            block = [ge_all[n, r][:, h:h + OWN_OUT].astype(F32) for r in range(4)]
            cols.append(jnp.concatenate(block, 1))
        place_cot(130 * n, jnp.concatenate(cols, 0), 2)

    def place_piece(k):
        arrived(g_block(sib, k), gr.at[1, k])
        arrived(g_block(diag, k), gr.at[2, k])
        for b in range(4 * k, 4 * k + 4):
            place_cot(2 + 8 * b, g_all[:, pl.ds(128 * b, 128)].astype(F32).T, 8)

    def adjoint(n):
        g = [cots[pl.ds(n * 26 + 2 - kx, 26)].reshape(416, 768) for kx in range(3)]
        acc = nn(jnp.concatenate(g, 1), conv_t[...])
        ts = pl.ds(n * 13, 13)
        d = (acc.reshape(13, 2, 2, H, COUT) * fs[ts]).astype(BF16).astype(F32)
        for cp in range(2):
            even, odd = d[:, cp, 0], d[:, cp, 1]
            for ky, v in enumerate((down(odd), even, odd, up(even))):
                df[cp, ky, ts] = v

    place_edge(0)
    place_piece(0)
    place_piece(1)
    pl.loop(0, 2)(adjoint)
    place_edge(1)
    place_piece(2)
    place_piece(3)
    pl.loop(2, 5)(adjoint)

    def window(ky, kx):
        return df[kx % 2, ky, pl.ds(kx // 2, 64)].reshape(POS, COUT).astype(BF16)

    for which in (2, 0, 1, 3):
        ky = (xa, xb, xo, x)[which]
        for pair in range(2):
            a, b = [nn(coarse[...], window(ky, kx)) for kx in (2 * pair, 2 * pair + 1)]
            slabs = (a[:, :128], jnp.concatenate([a[:, 128:], b[:, :64]], 1), b[:, 64:])
            for n, slab in enumerate(slabs):
                p = 3 * pair + n
                part[ky, p] = slab.astype(BF16)
                if which < 3:
                    along_x(p, which)

    def picked(count, size):
        row = lax.broadcasted_iota(jnp.int32, (count, size), 0)
        col = lax.broadcasted_iota(jnp.int32, (count, size), 1)
        return (row == col + size * rank).astype(F32).astype(BF16)

    pick = picked(CIN, OWN_IN)
    for t in range(16):
        own_up[t] = nn(up_w[t // 4, t % 4], pick).astype(BF16)

    total = None
    for t in range(16):
        term = nn(window(t // 4, t % 4), own_up[t])
        total = term if total is None else total + term
    c_pos[...] = total

    pick = picked(COUT, OWN_OUT)
    for t in range(9):
        mine[t] = nn(conv_w[t // 3, t % 3], pick).astype(BF16)

    @pl.loop(0, 22)
    def _(n):
        v = hid[1, pl.ds(n * 6, 6)].astype(F32).reshape(6, 2, H, COUT)
        above, _, below = shifted(v)
        hid[0, pl.ds(n * 6, 6)] = above
        hid[2, pl.ds(n * 6, 6)] = below

    def refine(n):
        acc = None
        for t in range(9):
            term = nn(hid[t // 3, pl.ds(16 * n + t % 3, 16)].reshape(256, COUT), mine[t])
            acc = term if acc is None else acc + term
        r_pos[pl.ds(256 * n, 256), :] = acc + own_bias


    for d in far_first:
        zz = lax.rem(z + d, nz)
        acc = part[x, zz].astype(F32)
        for which in range(3):
            arrived(rx1.at[zz, which], x1r.at[zz, which])
            acc = acc + rx1[zz, which].astype(F32)
        if d > 0:
            sb2[d] = acc.astype(BF16)
            send(sb2.at[d], rz.at[d], zs_s.at[d], zs_r.at[d], zdev[d])
        else:
            kept[...] = acc
    for n in range(8):
        refine(n)
    acc = kept[...]
    for d in near_first[1:]:
        arrived(rz.at[d], zs_r.at[d])
        acc = acc + rz[d].astype(F32)
    ys[...] = acc
    send(ys, yr, y_sem.at[0], y_sem.at[1], ydev)
    arrived(yr, y_sem.at[1])
    res[x, z] = (acc + yr[...]).astype(BF16)
    here = res.at[x, z]
    for d in near_first[1:]:
        send(here, here, azs.at[d], azr.at[d], zdev[d])

    def direct(d):
        return min(d, nz - d) >= 2

    def spread_x(d):
        zz = lax.rem(z + nz - d, nz)
        got = res.at[x, zz]
        if d > 0:
            arrived(got, azr.at[d])
        if direct(d):
            send(got, got, axs.at[2, d], axr.at[2, d], dev(xo, z, y))
        send(got, got, axs.at[0, d], axr.at[0, d], dev(second(zz), z, y))
        send(got, got, axs.at[1, d], axr.at[1, d], dev(first(zz), z, y))

    def forward_x(d):
        zz = lax.rem(z + nz - d, nz)
        got = res.at[second(zz), zz]
        arrived(got, axr.at[0, d])
        if not direct(d):
            send(got, got, axs.at[2, d], axr.at[2, d], dev(first(zz), z, y))

    lag = 4
    for n in range(nz + lag):
        if n < nz:
            spread_x(near_first[n])
        if n == 0:
            for r in range(2):
                for i in range(H):
                    g32[pl.ds(2 * i + r, OWN_OUT, stride=16), :] = r_pos[pl.ds(8 * r + i, 128, stride=16), :].T
            refined[...] = g32[...].reshape(OWN_OUT, 16, 128).astype(BF16)
            for i in range(H):
                c_grad[i] = c_pos[pl.ds(i, WC, stride=H), :].astype(BF16)
        if n >= lag:
            forward_x(near_first[n - lag])
    for d in near_first:
        zz = lax.rem(z + nz - d, nz)
        arrived(res.at[first(zz), zz], axr.at[1, d])
        arrived(res.at[xo, zz], axr.at[2, d])
    for copy in started:
        copy.wait_send()


def strip(dims, *args):
    nx, nz, ny = dims
    dma = pltpu.SemaphoreType.DMA
    vm = pltpu.VMEM
    any_ = pl.BlockSpec(memory_space=pl.ANY)
    return pl.pallas_call(
        functools.partial(kernel, dims),
        out_shape=(
            jax.ShapeDtypeStruct((OWN_OUT, 2 * H, 2 * WC), BF16),
            jax.ShapeDtypeStruct((H, WC, OWN_IN), BF16),
            jax.ShapeDtypeStruct((nx, nz, PIECE, 128), BF16),
        ),
        in_specs=[any_] * 6,
        out_specs=[VM] * 3,
        scratch_shapes=[
            vm((1, COUT), F32),
            vm((1, COUT), F32),
            vm((H, WC, OWN_IN), BF16),
            vm((OWN_OUT, 2 * H, 2 * WC), BF16),
            vm((OWN_IN, POS), BF16),
            vm((OWN_OUT, FINE), BF16),
            vm((3 * OWN_OUT, FINE), BF16),
            vm((2, 16, OWN_IN), BF16),
            vm((2, 16, 128), BF16),
            vm((OWN_OUT * 2 * H, 2 * WC), F32),
            vm((CIN, POS), BF16),
            vm((COUT, FINE), BF16),
            vm((2, 4, 16, OWN_IN), BF16),
            vm((2, 4, 16, 128), BF16),
            vm((4, 4, COUT, CIN), BF16),
            vm((3, 3, COUT, COUT), BF16),
            vm((9 * 256, COUT), BF16),
            vm((9, COUT, OWN_OUT), BF16),
            vm((16, COUT, OWN_IN), BF16),
            vm((68, H, CIN), F32),
            vm((528, 6 * CIN), BF16),
            vm((66, 2, 2, H, COUT), F32),
            vm((66, 2, 2, H, COUT), F32),
            vm((3, 132, 16, COUT), BF16),
            vm((132, 16, 3 * 256), BF16),
            vm((2, 4, 66, H, COUT), F32),
            vm((nx, nz, PIECE, 128), BF16),
            vm((FINE, OWN_OUT), F32),
            vm((POS, OWN_IN), F32),
            vm((nz, 3, PIECE, 128), BF16),
            vm((PIECE, 128), F32),
            vm((nz, PIECE, 128), BF16),
            vm((nz, PIECE, 128), BF16),
            vm((PIECE, 128), F32),
            vm((PIECE, 128), F32),
            dma((6,)), dma((3, 2)), dma((3, 2)), dma((3, PIECES)), dma((3, PIECES)), dma((2, 2, 4)), dma((2, 2, 4)),
            dma((nz, 3)), dma((nz, 3)), dma((nz,)), dma((nz,)), dma((2,)),
            dma((nz,)), dma((nz,)), dma((3, nz)), dma((3, nz)),
        ],
        compiler_params=pltpu.CompilerParams(
            collective_id=0, has_side_effects=True, vmem_limit_bytes=LIMIT
        ),
        name="strip",
    )(*args)


def unpack_kernel(refined, c_grad, sums, refined_out, c_out, up_grad, conv_grad, ref, cg, src, up, conv, sems, out_sems):
    nx = sums.shape[0]
    loads = [pltpu.make_async_copy(sums.at[k], src.at[k], sems.at[k]) for k in range(nx)]
    loads += [
        pltpu.make_async_copy(refined, ref, sems.at[nx]),
        pltpu.make_async_copy(c_grad, cg, sems.at[nx + 1]),
    ]
    for copy in loads:
        copy.start()
    passes = [
        pltpu.make_async_copy(ref, refined_out, out_sems.at[nx]),
        pltpu.make_async_copy(cg, c_out, out_sems.at[nx + 1]),
    ]
    for ky in range(4):
        loads[ky].wait()
        for pair in range(2):
            a, m, b = [src[ky, 3 * pair + n].astype(F32) for n in range(3)]
            up[ky, 2 * pair] = jnp.concatenate([a, m[:, :64]], 1)
            up[ky, 2 * pair + 1] = jnp.concatenate([m[:, 64:], b], 1)
        copy = pltpu.make_async_copy(up.at[ky], up_grad.at[ky], out_sems.at[ky])
        copy.start()
        passes.append(copy)

    for load, copy in zip(loads[nx:], passes):
        load.wait()
        copy.start()

    def block(b):
        return src[b // 4, 6 + b % 4 // 2, pl.ds(b % 2 * OWN_OUT, OWN_OUT), :].astype(F32)

    for t in range(9):
        tail = block(9 + t // 2)[:, 64 * (t % 2):64 * (t % 2) + 64]
        conv[t // 3, t % 3] = jnp.concatenate([block(t), tail], 1)
    copy = pltpu.make_async_copy(conv, conv_grad, out_sems.at[nx + 2])
    copy.start()
    for copy in passes + [copy]:
        copy.wait()


def unpack(refined, c_grad, sums):
    any_ = pl.BlockSpec(memory_space=pl.ANY)
    up = (4, 4, OWN_IN, COUT)
    conv = (3, 3, OWN_OUT, COUT)
    return pl.pallas_call(
        unpack_kernel,
        out_shape=(
            jax.ShapeDtypeStruct(refined.shape, BF16),
            jax.ShapeDtypeStruct(c_grad.shape, BF16),
            jax.ShapeDtypeStruct(up, F32),
            jax.ShapeDtypeStruct(conv, F32),
        ),
        in_specs=[any_] * 3,
        out_specs=[any_] * 4,
        scratch_shapes=[
            pltpu.VMEM(refined.shape, BF16),
            pltpu.VMEM(c_grad.shape, BF16),
            pltpu.VMEM(sums.shape, BF16),
            pltpu.VMEM(up, F32),
            pltpu.VMEM(conv, F32),
            pltpu.SemaphoreType.DMA((6,)),
            pltpu.SemaphoreType.DMA((7,)),
        ],
        compiler_params=pltpu.CompilerParams(vmem_limit_bytes=LIMIT),
        name="unpack",
    )(refined, c_grad, sums)


def local(dims, coarse, up_weight, up_bias, conv_weight, conv_bias, cotangent):
    refined, c_grad, sums = strip(
        dims, coarse.transpose(1, 2, 0), cotangent, up_weight.transpose(0, 1, 3, 2), conv_weight,
        up_bias.reshape(1, COUT), conv_bias.reshape(1, COUT),
    )
    refined, c_grad, up_grad, conv_grad = unpack(refined, c_grad, sums)
    return refined, c_grad.transpose(2, 0, 1), up_grad, conv_grad.transpose(0, 1, 3, 2)


def solution(mesh):
    dims = (4, 8, 2)
    placed = (P("chan", None, "lon"), P(), P(), P(), P(), P("chan", None, "lon"))
    return jax.shard_map(
        functools.partial(local, dims),
        mesh=mesh,
        in_specs=placed,
        out_specs=(
            P("chan", None, "lon"),
            P("chan", None, "lon"),
            P(None, None, "chan", None),
            P(None, None, None, "chan"),
        ),
        check_vma=False,
    )
```
